32 devices in a mesh: dp: 8 (over z, y), tensor: 4 (over x, core).
Axes of the slice: x: 2, y: 2, z: 4, core: 2. Of those that a mesh axis runs over, the one named last changes fastest.
Arguments:
- tokens: bfloat16 [8192, 1152], P('dp'), may hold values from -6 to 6
- condition: bfloat16 [16, 1152], replicated, may hold values from -6 to 6
- latent_lengths: int32 [16], replicated, may hold values from 1 to 1024, as said below
- in_weight: bfloat16 [1152, 3, 1152], P(None, None, 'tensor'), may hold values from -0.1875 to 0.1875
- in_bias: bfloat16 [2, 1152], P(None, 'tensor'), may hold values from -3 to 3
- out_weight: bfloat16 [1152, 1152], P(None, 'tensor'), may hold values from -1.5 to 1.5
- out_bias: bfloat16 [1152], replicated, may hold values from -3 to 3
- up_weight: bfloat16 [1152, 4608], P(None, 'tensor'), may hold values from -0.1875 to 0.1875
- up_bias: bfloat16 [4608], P('tensor'), may hold values from -3 to 3
- down_weight: bfloat16 [1152, 4608], P(None, 'tensor'), may hold values from -0.09375 to 0.09375
- down_bias: bfloat16 [1152], replicated, may hold values from -3 to 3
- mod_weight: bfloat16 [1152, 6912], P(None, 'tensor'), may hold values from -0.1875 to 0.1875
- mod_bias: bfloat16 [6912], P('tensor'), may hold values from -3 to 3
- out_grad: bfloat16 [8192, 1152], P('dp'), may hold values from -6 to 6
Outputs:
- output: bfloat16 [8192, 1152], P(('dp', 'tensor'))
- grad_tokens: float32 [8192, 1152], P('dp', 'tensor')
- grad_condition: float32 [16, 1152], P('dp', 'tensor')
- grad_in_weight: float32 [1152, 3, 1152], P('dp', None, 'tensor')
- grad_in_bias: float32 [2, 1152], P(None, 'tensor')
- grad_out_weight: float32 [1152, 1152], P('dp', 'tensor')
- grad_out_bias: float32 [1152], replicated
- grad_up_weight: float32 [1152, 4608], P('dp', 'tensor')
- grad_up_bias: float32 [4608], P('tensor')
- grad_down_weight: float32 [1152, 4608], P('dp', 'tensor')
- grad_down_bias: float32 [1152], replicated
- grad_mod_weight: float32 [1152, 6912], P('dp', 'tensor')
- grad_mod_bias: float32 [6912], P('tensor')
The draws below stay inside these ranges and needn't reach their ends.
Inputs may be any that keep to these rules, and one draw needn't show every extreme that they name: `latent_lengths`: lengths of the 16 latents in stream order; they sum to 8192.
All inputs are finite; a program needn't handle non-finite values.
Results may differ from the reference program's by a relative error of at most 0.017.
Values may be sent and summed in bfloat16 or wider, within the bound.
No kernel may reach another device: no remote copies, remote signals or barrier semaphores. Data moves between devices by JAX's collectives and lax.ppermute only.
A program may use at most 256 MiB of HBM per device.

```python
import jax
import jax.numpy as jnp
from jax import lax

D = 1152
HEADS = 16
HD = 72
FF = 4608
TOK_DEV = 1024
MOST = 1024
LATENTS = 16
TOKENS = 8192


def draw_latent_lengths(key, part):
    half = LATENTS // 2
    others = LATENTS - half
    first_most = max(1, (min(TOK_DEV, MOST) - 1) // half)
    first_key, second_key = jax.random.split(jax.random.fold_in(key, 11))
    first = jax.random.randint(first_key, (half,), 1, first_most + 1).astype(jnp.int32)
    first = first.at[0].set(1)
    used = jnp.sum(first).astype(jnp.int32)
    deficit = (others * MOST - (TOKENS - used)).astype(jnp.int32)
    weights = jax.random.randint(second_key, (others - 1,), 1, 101).astype(jnp.int32)
    running = jnp.cumsum(weights).astype(jnp.int32)
    marks = (deficit * running // running[-1]).astype(jnp.int32)
    pieces = jnp.diff(jnp.concatenate([jnp.zeros((1,), jnp.int32), marks])).astype(jnp.int32)
    second = (MOST - jnp.concatenate([pieces, jnp.zeros((1,), jnp.int32)])).astype(jnp.int32)
    return jnp.concatenate([first, second]).astype(jnp.int32)


def spiked(entries, own_key, source, target, blocks, factor):
    def block_of(axis_at):
        return (jnp.arange(entries.shape[axis_at]) // (entries.shape[axis_at] // blocks)).reshape((-1,) + (1,) * (entries.ndim - 1 - axis_at))

    first = jax.random.permutation(own_key, blocks)[block_of(target)]
    other_side = (block_of(target) + blocks // 2) % blocks
    return jnp.where((block_of(source) == first) | (block_of(source) == other_side), factor * entries, entries)


def block_scale(own_key, shape, cuts, smallest, top_value):
    loudness = 1.0
    for position, shards_of in cuts:
        heights = jax.random.uniform(jax.random.fold_in(jax.random.fold_in(own_key, 6), position), (shards_of,), jnp.float32, smallest / len(cuts), top_value / len(cuts))
        loudness = loudness * jnp.repeat(jnp.exp(heights), shape[position] // shards_of).reshape((-1,) + (1,) * (len(shape) - 1 - position))
    return loudness


def centred(rng, shape, scale, limit, cuts=(), held_as=jnp.bfloat16):
    drawn = scale * jax.random.normal(rng, shape, jnp.float32)
    if cuts:
        drawn = drawn * block_scale(rng, shape, cuts, -0.22, 0.18)
    return jnp.clip(drawn, -limit, limit).astype(held_as)


def gaussian_with(key, dims, scale, reach, cuts, heavy, kind=jnp.bfloat16):
    array = scale * jax.random.normal(key, dims, jnp.float32)
    if cuts:
        array = array * block_scale(key, dims, cuts, -0.22, 0.18)
    return jnp.clip(spiked(array, jax.random.fold_in(key, 3), *heavy), -reach, reach).astype(kind)


def setup_inputs(seed: int = 0) -> dict:
    arg_keys = jax.random.split(jax.random.key(seed), 15)
    tokens = centred(arg_keys[0], (TOKENS, D), 1.0, 6.0, ((0, 8),))
    condition = centred(arg_keys[1], (LATENTS, D), 1.0, 6.0)
    latent_lengths = draw_latent_lengths(jax.random.fold_in(arg_keys[14], 71), 0)
    in_weight = centred(arg_keys[3], (D, 3, D), D ** -0.5, 0.1875, ((2, 4),))
    in_bias = centred(arg_keys[4], (2, D), 0.5, 3.0, ((1, 4),))
    out_weight = centred(arg_keys[5], (D, D), (D // 64) ** -0.5, 1.5, ((1, 4),))
    out_bias = centred(arg_keys[6], (D,), 0.5, 3.0)
    up_weight = centred(arg_keys[7], (D, FF), D ** -0.5, 0.1875, ((1, 4),))
    up_bias = centred(arg_keys[8], (FF,), 0.5, 3.0, ((0, 4),))
    down_weight = centred(arg_keys[9], (D, FF), FF ** -0.5, 0.09375, ((1, 4),))
    down_bias = centred(arg_keys[10], (D,), 0.5, 3.0)
    mod_weight = centred(arg_keys[11], (D, 6 * D), D ** -0.5, 0.1875, ((1, 4),))
    mod_bias = centred(arg_keys[12], (6 * D,), 0.5, 3.0, ((0, 4),))
    out_grad = gaussian_with(arg_keys[13], (TOKENS, D), 1.0, 6.0, ((0, 8),), (0, 1, 8, 2.0))
    return {"tokens": tokens, "condition": condition, "latent_lengths": latent_lengths, "in_weight": in_weight, "in_bias": in_bias, "out_weight": out_weight, "out_bias": out_bias, "up_weight": up_weight, "up_bias": up_bias, "down_weight": down_weight, "down_bias": down_bias, "mod_weight": mod_weight, "mod_bias": mod_bias, "out_grad": out_grad}


@jax.custom_vjp
def low(v):
    return lax.optimization_barrier(v.astype(jnp.bfloat16)).astype(jnp.float32)

@jax.custom_vjp
def low_back(v):
    return v

def low_keep(v):
    return (low(v), None)

def low_pass(kept, grad):
    return (grad,)

def back_keep(v):
    return (v, None)

def back_low(kept, grad):
    return (low(grad),)
low.defvjp(low_keep, low_pass)
low_back.defvjp(back_keep, back_low)
highest = lax.Precision.HIGHEST

def rounded_both(value):
    return low_back(low(value))

def layer_norm(value):
    center = value - lax.optimization_barrier(jnp.mean(value, axis=-1, keepdims=True))
    spread = lax.optimization_barrier(jnp.mean(center * center, axis=-1, keepdims=True))
    return center * lax.rsqrt(spread + 1e-06)

def gelu_tanh(value):
    return jax.nn.gelu(value, approximate=True)

def token_latents(latent_lengths):
    lengths = latent_lengths.astype(jnp.int32)
    starts = (jnp.cumsum(lengths) - lengths).astype(jnp.int32)
    places = jnp.arange(TOKENS, dtype=jnp.int32)
    return (lax.optimization_barrier(jnp.sum((places[:, None] >= starts[None, :]).astype(jnp.int32), axis=1)) - 1).astype(jnp.int32)

def attend(query, keys, values, latent_ids):
    block = min(512, TOKENS)
    span = block + 2 * MOST
    padding = jnp.zeros((MOST, D), jnp.float32)
    keys_pad = jnp.concatenate([padding, keys, padding], axis=0)
    values_pad = jnp.concatenate([padding, values, padding], axis=0)
    edge = jnp.full((MOST,), -1, jnp.int32)
    ids_pad = jnp.concatenate([edge, latent_ids, edge], axis=0)
    starts = (jnp.arange(TOKENS // block, dtype=jnp.int32) * block).astype(jnp.int32)

    def one_block(start):
        query_blk = lax.dynamic_slice_in_dim(query, start, block, 0).reshape(block, HEADS, HD)
        keys_blk = lax.dynamic_slice_in_dim(keys_pad, start, span, 0).reshape(span, HEADS, HD)
        values_blk = lax.dynamic_slice_in_dim(values_pad, start, span, 0).reshape(span, HEADS, HD)
        query_ids = lax.dynamic_slice_in_dim(latent_ids, start, block, 0)
        key_ids = lax.dynamic_slice_in_dim(ids_pad, start, span, 0)
        scores = low_back(jnp.einsum('qhc,khc->hqk', query_blk, keys_blk, precision=highest) * HD ** (-0.5))
        allowed = query_ids[:, None] == key_ids[None, :]
        scores = jnp.where(allowed[None], scores, -1e+30)
        probs = low(jax.nn.softmax(scores, axis=-1))
        mixed = jnp.einsum('hqk,khc->qhc', probs, values_blk, precision=highest)
        return rounded_both(mixed.reshape(block, D))
    return lax.map(jax.checkpoint(one_block), starts).reshape(TOKENS, D)

def layer(tokens, condition, in_weight, in_bias, out_weight, out_bias, up_weight, up_bias, down_weight, down_bias, mod_weight, mod_bias, latent_ids):
    silu_cond = low(jax.nn.silu(condition))
    modulation = rounded_both(jnp.dot(silu_cond, mod_weight, precision=highest) + mod_bias)
    select = (latent_ids[:, None] == jnp.arange(LATENTS, dtype=jnp.int32)[None, :]).astype(jnp.float32)
    per_token = jnp.dot(select, modulation, precision=highest).reshape(TOKENS, 6, D)
    shift_a = per_token[:, 0]
    scale_a = per_token[:, 1]
    gate_a = per_token[:, 2]
    shift_m = per_token[:, 3]
    scale_m = per_token[:, 4]
    gate_m = per_token[:, 5]
    entry = low(layer_norm(tokens) * (1.0 + scale_a) + shift_a)
    projected = jnp.einsum('td,dcf->ctf', entry, in_weight, precision=highest)
    query = rounded_both(projected[0] + in_bias[0])
    keys = rounded_both(projected[1])
    values = rounded_both(projected[2] + in_bias[1])
    attended = attend(query, keys, values, latent_ids)
    branch = low_back(jnp.einsum('tf,df->td', attended, out_weight, precision=highest) + out_bias)
    middle = tokens + gate_a * branch
    entry_m = low(layer_norm(middle) * (1.0 + scale_m) + shift_m)
    hidden_pre = low_back(jnp.dot(entry_m, up_weight, precision=highest) + up_bias)
    hidden = low(gelu_tanh(hidden_pre))
    branch_m = low_back(jnp.einsum('tf,df->td', hidden, down_weight, precision=highest) + down_bias)
    return middle + gate_m * branch_m

def reference(tokens, condition, latent_lengths, in_weight, in_bias, out_weight, out_bias, up_weight, up_bias, down_weight, down_bias, mod_weight, mod_bias, out_grad):
    latent_ids = token_latents(latent_lengths)
    floats = tuple((item.astype(jnp.float32) for item in (tokens, condition, in_weight, in_bias, out_weight, out_bias, up_weight, up_bias, down_weight, down_bias, mod_weight, mod_bias)))

    def forward(*arrays):
        return layer(*arrays, latent_ids)
    result, pullback = jax.vjp(forward, *floats)
    grads = pullback(out_grad.astype(jnp.float32))
    return (result.astype(jnp.bfloat16), grads[0], grads[1], grads[2], grads[3], grads[4], grads[5], grads[6], grads[7], grads[8], grads[9], grads[10], grads[11])
```

```python
import functools
import math

import jax
import jax.numpy as jnp
from jax import lax
from jax.experimental import pallas as pl
from jax.experimental.pallas import tpu as pltpu
from jax.sharding import PartitionSpec as P

HD = 72
FACTOR = HD ** (-0.5)
LOG2E = math.log2(math.e)
NEG = -1e30
BQ = 256
BK = 256
F32 = jnp.float32
BF16 = jnp.bfloat16


def contract(a, b, dims):
    return lax.dot_general(a, b, (dims, ((), ())), preferred_element_type=F32)


def forward_kernel(bases, heads, bounds, span, query, *refs):
    segments = len(bases)
    keys = refs[:segments]
    values = refs[segments : 2 * segments]
    out, logsum, mixed = refs[2 * segments :]
    rows = query.shape[2]
    scale = FACTOR * LOG2E

    def query_block(i, _):
        at = pl.multiple_of(i * BQ, BQ)
        own = pl.ds(at, BQ)
        begin = span[0:1, own]
        end = span[1:2, own]
        q = [query[h, :, own] for h in range(heads)]
        mixed[...] = jnp.zeros_like(mixed)
        state = tuple(jnp.full((1, BQ), NEG, F32) for _ in range(heads)) + tuple(
            jnp.zeros((1, BQ), F32) for _ in range(heads)
        )
        for s, base in enumerate(bases):

            def key_block(j, state, s=s, base=base):
                k_at = pl.multiple_of(j * BK, BK)
                block = pl.ds(k_at, BK)
                place = lax.broadcasted_iota(jnp.int32, (BK, BQ), 0) + (k_at + base)
                allowed = (place >= begin) & (place < end)
                tops, totals = [], []
                for h in range(heads):
                    raw = contract(keys[s][h, :, block], q[h], ((0,), (0,)))
                    raw = jnp.where(allowed, raw * scale, NEG)
                    top = jnp.maximum(state[h], jnp.max(raw, axis=0, keepdims=True))
                    probs = jnp.exp2(raw - top)
                    shrink = jnp.exp2(state[h] - top)
                    tops.append(top)
                    totals.append(state[heads + h] * shrink + jnp.sum(probs, axis=0, keepdims=True))
                    mixed[h] = mixed[h] * shrink + contract(
                        values[s][h, :, block], probs.astype(BF16), ((1,), (0,))
                    )
                return tuple(tops) + tuple(totals)

            state = lax.fori_loop(bounds[s, 0, i], bounds[s, 1, i], key_block, state)
        for h in range(heads):
            total = state[heads + h]
            out[h, :, own] = (mixed[h] / total).astype(BF16)
            logsum[h, :, own] = state[h] + jnp.log2(total)
        return 0

    lax.fori_loop(0, rows // BQ, query_block, 0)


def attend(bounds, span, query, keys, values, bases):
    heads, hd, rows = query.shape
    vmem = pl.BlockSpec(memory_space=pltpu.VMEM)
    return pl.pallas_call(
        functools.partial(forward_kernel, bases, heads),
        out_shape=(
            jax.ShapeDtypeStruct((heads, hd, rows), BF16),
            jax.ShapeDtypeStruct((heads, 1, rows), F32),
        ),
        in_specs=[pl.BlockSpec(memory_space=pltpu.SMEM)] + [vmem] * (2 + 2 * len(bases)),
        out_specs=(vmem, vmem),
        scratch_shapes=[pltpu.VMEM((heads, hd, BQ), F32)],
        compiler_params=pltpu.CompilerParams(vmem_limit_bytes=40 << 20),
        cost_estimate=pl.CostEstimate(
            flops=24 * heads * rows * rows * HD,
            bytes_accessed=12 << 20,
            transcendentals=heads * rows * rows,
        ),
    )(bounds, span, query, *keys, *values)


def backward_kernel(bases, heads, bounds, span, query, grad, attended, logsum, *refs):
    segments = len(bases)
    keys = refs[:segments]
    values = refs[segments : 2 * segments]
    grad_query = refs[2 * segments]
    grad_keys = refs[2 * segments + 1 : 3 * segments + 1]
    grad_values = refs[3 * segments + 1 : 4 * segments + 1]
    delta, sum_query, sum_keys, sum_values = refs[4 * segments + 1 :]
    scale = FACTOR * LOG2E
    rows = query.shape[2]
    for h in range(heads):
        delta[h] = jnp.sum(
            grad[h].astype(F32) * attended[h].astype(F32), axis=0, keepdims=True
        )
    sum_query[...] = jnp.zeros_like(sum_query)
    for s, base in enumerate(bases):

        def key_block(j, _, s=s, base=base):
            k_at = pl.multiple_of(j * BK, BK)
            block = pl.ds(k_at, BK)
            place = lax.broadcasted_iota(jnp.int32, (BK, BQ), 0) + (k_at + base)
            sum_keys[...] = jnp.zeros_like(sum_keys)
            sum_values[...] = jnp.zeros_like(sum_values)

            def query_block(i, _):
                own = pl.ds(pl.multiple_of(i * BQ, BQ), BQ)
                allowed = (place >= span[0:1, own]) & (place < span[1:2, own])
                for h in range(heads):
                    k = keys[s][h, :, block]
                    q = query[h, :, own]
                    g = grad[h, :, own]
                    raw = contract(k, q, ((0,), (0,)))
                    raw = jnp.where(allowed, raw * scale - logsum[h, :, own], NEG)
                    probs = jnp.exp2(raw)
                    grad_probs = contract(values[s][h, :, block], g, ((0,), (0,)))
                    grad_raw = (probs * (grad_probs - delta[h, :, own])).astype(BF16)
                    sum_values[h] += contract(g, probs.astype(BF16), ((1,), (1,)))
                    sum_keys[h] += contract(q, grad_raw, ((1,), (1,)))
                    sum_query[h, :, own] += contract(k, grad_raw, ((1,), (0,)))
                return 0

            lax.fori_loop(bounds[s, 0, j], bounds[s, 1, j], query_block, 0)
            for h in range(heads):
                grad_keys[s][h, :, block] = (sum_keys[h] * FACTOR).astype(BF16)
                grad_values[s][h, :, block] = sum_values[h].astype(BF16)
            return 0

        lax.fori_loop(0, keys[s].shape[2] // BK, key_block, 0)
    grad_query[...] = (sum_query[...] * FACTOR).astype(BF16)


def attend_back(bounds, span, query, grad, attended, logsum, keys, values, bases):
    heads, hd, rows = query.shape
    segments = len(bases)
    vmem = pl.BlockSpec(memory_space=pltpu.VMEM)
    shape = jax.ShapeDtypeStruct((heads, hd, rows), BF16)
    found = pl.pallas_call(
        functools.partial(backward_kernel, bases, heads),
        out_shape=(shape,) * (1 + 2 * segments),
        in_specs=[pl.BlockSpec(memory_space=pltpu.SMEM)] + [vmem] * (5 + 2 * segments),
        out_specs=(vmem,) * (1 + 2 * segments),
        scratch_shapes=[
            pltpu.VMEM((heads, 1, rows), F32),
            pltpu.VMEM((heads, hd, rows), F32),
            pltpu.VMEM((heads, hd, BK), F32),
            pltpu.VMEM((heads, hd, BK), F32),
        ],
        compiler_params=pltpu.CompilerParams(vmem_limit_bytes=44 << 20),
        cost_estimate=pl.CostEstimate(
            flops=60 * heads * rows * rows * HD,
            bytes_accessed=24 << 20,
            transcendentals=heads * rows * rows,
        ),
    )(bounds, span, query, grad, attended, logsum, *keys, *values)
    return found[0], found[1 : 1 + segments], found[1 + segments :]


def swap(value, axis, bit):
    return lax.ppermute(value, axis, [(i, i ^ bit) for i in range(lax.axis_size(axis))])


def shift(value, axis, distance):
    devices = range(lax.axis_size(axis))
    return lax.ppermute(value, axis, [(i, i + distance) for i in devices if i + distance in devices])


def bits_of(axis):
    size = lax.axis_size(axis)
    return [1 << b for b in range(size.bit_length() - 1)]


def bit_set(axis, bit):
    return (lax.axis_index(axis) & bit) != 0


def sum_all(value, axis):
    for bit in bits_of(axis):
        value = value + swap(value, axis, bit)
    return value


def in_order(mine, other, upper, dim=0):
    return jnp.where(
        upper, jnp.stack([other, mine], axis=dim), jnp.stack([mine, other], axis=dim)
    )


def gather_tensor(value):
    pair = in_order(value, swap(value, "tensor", 2), bit_set("tensor", 2))
    quad = in_order(pair, swap(pair, "tensor", 1), bit_set("tensor", 1), dim=1)
    return quad.reshape((4 * value.shape[0],) + value.shape[1:])


def scatter_tensor(partial):
    n = partial.shape[0] // 4
    core = lax.axis_index("tensor") % 2
    across = lax.axis_index("tensor") // 2
    parts = partial.astype(BF16).reshape((2, 2, n) + partial.shape[1:])
    kept = lax.dynamic_index_in_dim(parts, core, 1, keepdims=False)
    sent = lax.dynamic_index_in_dim(parts, 1 - core, 1, keepdims=False)
    half = kept.astype(F32) + swap(sent, "tensor", 1).astype(F32)
    half_low = half.astype(BF16)
    stay = lax.dynamic_index_in_dim(half, across, 0, keepdims=False)
    leave = lax.dynamic_index_in_dim(half_low, 1 - across, 0, keepdims=False)
    return stay + swap(leave, "tensor", 2).astype(F32)


def scatter_data(partial):
    size = lax.axis_size("dp")
    if size != 8:
        return lax.psum_scatter(
            partial.astype(BF16), "dp", scatter_dimension=0, tiled=True
        ).astype(F32)
    index = lax.axis_index("dp")
    near, far = index % 2, index // 2
    rows = partial.shape[0] // 8
    parts = partial.astype(BF16).reshape((4, 2, rows) + partial.shape[1:])
    kept = lax.dynamic_index_in_dim(parts, near, 1, keepdims=False)
    sent = lax.dynamic_index_in_dim(parts, 1 - near, 1, keepdims=False)
    half = kept.astype(F32) + swap(sent, "dp", 1).astype(F32)
    half_low = half.astype(BF16)
    total = lax.dynamic_index_in_dim(half, far, 0, keepdims=False)
    for step in (1, -1, 2, -2, 3, -3):
        part = lax.dynamic_index_in_dim(half_low, jnp.clip(far + step, 0, 3), 0, keepdims=False)
        total = total + shift(part, "dp", 2 * step).astype(F32)
    return total


def layer_norm(value):
    center = value - jnp.mean(value, axis=-1, keepdims=True)
    spread = jnp.mean(center * center, axis=-1, keepdims=True)
    return center * lax.rsqrt(spread + 1e-06)


def gelu_tanh(value):
    return jax.nn.gelu(value, approximate=True)


def onehot_sum(select, values):
    upper = values.astype(BF16)
    lower = (values - upper.astype(F32)).astype(BF16)
    first = jnp.einsum("tl,tm->lm", select, upper, preferred_element_type=F32)
    return first + jnp.einsum("tl,tm->lm", select, lower, preferred_element_type=F32)


def on_device(
    tokens,
    condition,
    latent_lengths,
    in_weight,
    in_bias,
    out_weight,
    out_bias,
    up_weight,
    up_bias,
    down_weight,
    down_bias,
    mod_weight,
    mod_bias,
    out_grad,
):
    rows, width = tokens.shape
    latents = condition.shape[0]
    local_width = in_weight.shape[2]
    heads = local_width // HD
    data_size = lax.axis_size("dp")
    data_index = lax.axis_index("dp")
    tensor_index = lax.axis_index("tensor")
    quarter = rows // 4
    row_start = tensor_index * quarter

    def mine(value):
        return lax.dynamic_slice_in_dim(value, row_start, quarter, 0)

    places = jnp.arange(latents, dtype=jnp.int32)
    earlier = places[None, :] < places[:, None]
    starts = jnp.sum(jnp.where(earlier, latent_lengths[None, :], 0), axis=1)
    ends = starts + latent_lengths
    first_row = data_index * rows
    own_places = first_row + jnp.arange(rows, dtype=jnp.int32)

    def span_of(at):
        inside = (at[:, None] >= starts[None, :]) & (at[:, None] < ends[None, :])
        begin = jnp.sum(jnp.where(inside, starts[None, :] - first_row, 0), axis=1)
        end = jnp.sum(jnp.where(inside, ends[None, :] - first_row, 0), axis=1)
        return begin, end, inside

    begin, end, matches = span_of(own_places)
    select = matches.astype(BF16)
    select_mine = mine(select)
    span = jnp.stack([begin, end])
    bases = (-rows, 0, rows)
    forward_bounds = []
    backward_bounds = []
    for base in bases:
        low = jnp.clip(begin[::BQ] - base, 0, rows) // BK
        high = (jnp.clip(end[BQ - 1 :: BQ] - base, 0, rows) + BK - 1) // BK
        forward_bounds.append(jnp.stack([low, high]))
        key_at = first_row + base + jnp.arange(rows // BK, dtype=jnp.int32) * BK
        low = jnp.clip(span_of(key_at)[0], 0, rows) // BQ
        high = (jnp.clip(span_of(key_at + BK - 1)[1], 0, rows) + BQ - 1) // BQ
        valid = (key_at >= 0) & (key_at < rows * data_size)
        backward_bounds.append(jnp.where(valid[None, :], jnp.stack([low, high]), 0))
    forward_bounds = jnp.stack(forward_bounds)
    backward_bounds = jnp.stack(backward_bounds)

    cond_full = condition.astype(F32)
    silu_cond = jax.nn.silu(cond_full).astype(BF16)
    mod_local = (
        jnp.dot(silu_cond, mod_weight, preferred_element_type=F32) + mod_bias.astype(F32)
    ).astype(BF16)
    modulation = gather_tensor(mod_local[None])
    modulation = modulation.transpose(1, 0, 2).reshape(latents, 6 * width)

    def spread(chosen, first, count):
        return jnp.dot(
            chosen,
            modulation[:, first * width : (first + count) * width],
            preferred_element_type=BF16,
        )

    shift_scale = spread(select, 0, 2)
    shift_a = shift_scale[:, :width].astype(F32)
    scale_a = shift_scale[:, width:].astype(F32)
    others = spread(select_mine, 2, 4).astype(F32)
    gate_a, shift_m, scale_m, gate_m = (others[:, i * width : (i + 1) * width] for i in range(4))
    gate_m_all = spread(select, 5, 1).astype(F32)

    tokens_full = tokens.astype(F32)
    normed, norm_back = jax.vjp(layer_norm, tokens_full)
    entry = (normed * (1.0 + scale_a) + shift_a).astype(BF16)
    bias_full = in_bias.astype(F32)

    def project(which, bias):
        found = lax.dot_general(
            in_weight[:, which], entry, (((0,), (1,)), ((), ())), preferred_element_type=F32
        )
        if bias is not None:
            found = found + bias[:, None]
        return found.astype(BF16)

    keys = project(1, None)
    values = project(2, bias_full[1])
    pair = jnp.stack([keys, values])
    behind = shift(pair, "dp", 1)
    ahead = shift(pair, "dp", -1)
    query = project(0, bias_full[0]).reshape(heads, HD, rows)
    all_pairs = [p.reshape(2, heads, HD, rows) for p in (behind, pair, ahead)]
    all_keys = [p[0] for p in all_pairs]
    all_values = [p[1] for p in all_pairs]
    attended, logsum = attend(forward_bounds, span, query, all_keys, all_values, bases)
    attended_flat = attended.reshape(local_width, rows)
    attn_part = lax.dot_general(
        attended_flat, out_weight, (((0,), (1,)), ((), ())), preferred_element_type=F32
    )
    branch = scatter_tensor(attn_part) + out_bias.astype(F32)

    middle = mine(tokens).astype(F32) + gate_a * branch
    normed_m, norm_back_m = jax.vjp(layer_norm, middle)
    entry_m = gather_tensor((normed_m * (1.0 + scale_m) + shift_m).astype(BF16))
    hidden_pre = jnp.dot(entry_m, up_weight, preferred_element_type=F32) + up_bias.astype(F32)
    hidden_full, gelu_back = jax.vjp(gelu_tanh, hidden_pre)
    hidden = hidden_full.astype(BF16)
    grad_out = out_grad.astype(F32)
    grad_branch_m = (gate_m_all * grad_out).astype(BF16)
    grad_hidden = jnp.einsum("td,df->tf", grad_branch_m, down_weight, preferred_element_type=F32)
    grad_pre = gelu_back(grad_hidden)[0].astype(BF16)
    entry_part = jnp.einsum("tf,df->td", grad_pre, up_weight, preferred_element_type=F32)
    grad_entry_m = scatter_tensor(entry_part)
    mlp_part = jnp.einsum("tf,df->td", hidden, down_weight, preferred_element_type=F32)
    branch_m = scatter_tensor(mlp_part) + down_bias.astype(F32)
    output = (middle + gate_m * branch_m).astype(BF16)
    grad_out_mine = mine(out_grad).astype(F32)
    grad_gate_m = grad_out_mine * branch_m
    grad_down_b = jnp.sum(grad_branch_m.astype(F32), axis=0)
    grad_down_w = jnp.einsum("td,tf->df", grad_branch_m, hidden, preferred_element_type=F32)
    grad_up_b = jnp.sum(grad_pre.astype(F32), axis=0)
    grad_up_w = jnp.einsum("td,tf->df", entry_m, grad_pre, preferred_element_type=F32)
    grad_middle = grad_out_mine + norm_back_m(grad_entry_m * (1.0 + scale_m))[0]
    grad_gate_a = grad_middle * branch
    grad_branch_mine = (gate_a * grad_middle).astype(BF16)
    grad_out_b = jnp.sum(grad_branch_mine.astype(F32), axis=0)
    grad_branch = gather_tensor(grad_branch_mine)
    grad_attended = lax.dot_general(
        out_weight, grad_branch, (((0,), (1,)), ((), ())), preferred_element_type=F32
    ).astype(BF16)

    grad_query, grad_keys, grad_values = attend_back(
        backward_bounds,
        span,
        query,
        grad_attended.reshape(heads, HD, rows),
        attended,
        logsum,
        all_keys,
        all_values,
        bases,
    )
    to_behind = shift(jnp.stack([grad_keys[0], grad_values[0]]), "dp", -1)
    to_ahead = shift(jnp.stack([grad_keys[2], grad_values[2]]), "dp", 1)
    grad_out_w = lax.dot_general(
        grad_branch, attended_flat, (((0,), (1,)), ((), ())), preferred_element_type=F32
    )
    grad_kv = [
        (
            own[1].astype(F32) + to_behind[c].astype(F32) + to_ahead[c].astype(F32)
        ).astype(BF16).reshape(local_width, rows)
        for c, own in enumerate((grad_keys, grad_values))
    ]
    grad_proj = jnp.stack([grad_query.reshape(local_width, rows), *grad_kv])
    grad_in_w = jnp.einsum("td,cft->dcf", entry, grad_proj, preferred_element_type=F32)
    grad_in_b = jnp.stack(
        [jnp.sum(grad_proj[c].astype(F32), axis=1) for c in (0, 2)]
    )
    grad_entry = jnp.einsum("cft,dcf->td", grad_proj, in_weight, preferred_element_type=F32)
    input_part = norm_back(grad_entry * (1.0 + scale_a))[0]

    split_terms = jnp.concatenate([grad_entry, grad_entry * normed], axis=1)
    kept_terms = jnp.concatenate(
        [grad_gate_a, grad_entry_m, grad_entry_m * normed_m, grad_gate_m], axis=1
    )
    per_latent = jnp.concatenate(
        [onehot_sum(select, split_terms), onehot_sum(select_mine, kept_terms)], axis=1
    )
    columns_here = mod_weight.shape[1]
    arranged = per_latent.reshape(latents, 4, columns_here).transpose(1, 0, 2)
    grad_mod = lax.dynamic_index_in_dim(arranged, tensor_index, 0, keepdims=False)
    for bit in (1, 2, 3):
        grad_mod = grad_mod + swap(
            lax.dynamic_index_in_dim(arranged, tensor_index ^ bit, 0, keepdims=False), "tensor", bit
        )
    grad_mod = sum_all(grad_mod, "dp").astype(BF16)
    own_width = width // data_size
    own_silu = lax.dynamic_slice_in_dim(silu_cond, data_index * own_width, own_width, 1)
    grad_mod_w = jnp.einsum("ld,lm->dm", own_silu, grad_mod, preferred_element_type=F32)
    grad_mod_b = jnp.sum(grad_mod.astype(F32), axis=0)
    own_count = latents // data_size
    own_grad_mod = lax.dynamic_slice_in_dim(grad_mod, data_index * own_count, own_count, 0)
    own_cond = lax.dynamic_slice_in_dim(cond_full, data_index * own_count, own_count, 0)
    silu_grad = jnp.einsum("lm,dm->ld", own_grad_mod, mod_weight, preferred_element_type=F32)
    cond_part = jax.vjp(jax.nn.silu, own_cond)[1](silu_grad)[0]
    cond_parts = cond_part.reshape(own_count, 4, width // 4).transpose(1, 0, 2)
    grad_cond = lax.dynamic_index_in_dim(cond_parts, tensor_index, 0, keepdims=False)
    for bit in (1, 2, 3):
        grad_cond = grad_cond + swap(
            lax.dynamic_index_in_dim(cond_parts, tensor_index ^ bit, 0, keepdims=False),
            "tensor",
            bit,
        )

    placed = lax.dynamic_update_slice_in_dim(
        jnp.zeros((rows, width), F32), grad_middle, row_start, 0
    )
    grad_tokens = scatter_tensor((input_part + placed).T).T
    all_out_b = sum_all(grad_out_b, "tensor")
    small = jnp.concatenate([grad_in_b.reshape(-1), all_out_b, grad_up_b, grad_down_b])
    small = sum_all(small, "dp")
    cuts = [2 * local_width, 2 * local_width + width, 2 * local_width + width + grad_up_b.shape[0]]
    sum_in_b, sum_out_b, sum_up_b, sum_down_b = jnp.split(small, cuts)
    return (
        output,
        grad_tokens,
        grad_cond,
        scatter_data(grad_in_w),
        sum_in_b.reshape(2, local_width),
        scatter_data(grad_out_w),
        sum_out_b,
        scatter_data(grad_up_w),
        sum_up_b,
        scatter_data(grad_down_w),
        sum_down_b,
        grad_mod_w,
        grad_mod_b,
    )


def solution(mesh):
    placed = (
        P("dp", None),
        P(),
        P(),
        P(None, None, "tensor"),
        P(None, "tensor"),
        P(None, "tensor"),
        P(),
        P(None, "tensor"),
        P("tensor"),
        P(None, "tensor"),
        P(),
        P(None, "tensor"),
        P("tensor"),
        P("dp", None),
    )
    return jax.shard_map(
        on_device,
        mesh=mesh,
        in_specs=placed,
        out_specs=(
            P(("dp", "tensor"), None),
            P("dp", "tensor"),
            P("dp", "tensor"),
            P("dp", None, "tensor"),
            P(None, "tensor"),
            P("dp", "tensor"),
            P(),
            P("dp", "tensor"),
            P("tensor"),
            P("dp", "tensor"),
            P(),
            P("dp", "tensor"),
            P("tensor"),
        ),
        check_vma=False,
    )
```

```python
import functools
import math

import jax
import jax.numpy as jnp
from jax import lax
from jax.experimental import pallas as pl
from jax.experimental.pallas import tpu as pltpu
from jax.sharding import PartitionSpec as P

HD = 72
FACTOR = HD ** (-0.5)
LOG2E = math.log2(math.e)
NEG = -1e30
BQ = 256
BK = 256
F32 = jnp.float32
BF16 = jnp.bfloat16


def contract(a, b, dims):
    return lax.dot_general(a, b, (dims, ((), ())), preferred_element_type=F32)


def forward_kernel(bases, heads, last, bounds, span, query, mixed_in, top_in, total_in, *refs):
    segments = len(bases)
    keys = refs[:segments]
    values = refs[segments : 2 * segments]
    mixed_out, top_out, total_out, mixed = refs[2 * segments :]
    rows = query.shape[2]
    scale = FACTOR * LOG2E

    def query_block(i, _):
        own = pl.ds(pl.multiple_of(i * BQ, BQ), BQ)
        begin = span[0:1, own]
        end = span[1:2, own]
        for h in range(heads):
            mixed[h] = mixed_in[h, :, own]
        state = tuple(top_in[h, :, own] for h in range(heads)) + tuple(
            total_in[h, :, own] for h in range(heads)
        )
        for s, base in enumerate(bases):

            def key_block(j, state, s=s, base=base):
                k_at = pl.multiple_of(j * BK, BK)
                block = pl.ds(k_at, BK)
                place = lax.broadcasted_iota(jnp.int32, (BK, BQ), 0) + (k_at + base)
                allowed = (place >= begin) & (place < end)
                raws = [
                    contract(keys[s][h, :, block], query[h, :, own], ((0,), (0,)))
                    for h in range(heads)
                ]
                tops, totals, shrinks, lows = [], [], [], []
                for h in range(heads):
                    raw = jnp.where(allowed, raws[h] * scale, NEG)
                    top = jnp.maximum(state[h], jnp.max(raw, axis=0, keepdims=True))
                    probs = jnp.exp2(raw - top)
                    shrink = jnp.exp2(state[h] - top)
                    tops.append(top)
                    totals.append(state[heads + h] * shrink + jnp.sum(probs, axis=0, keepdims=True))
                    shrinks.append(shrink)
                    lows.append(probs.astype(BF16))
                for h in range(heads):
                    mixed[h] = mixed[h] * shrinks[h] + contract(
                        values[s][h, :, block], lows[h], ((1,), (0,))
                    )
                return tuple(tops) + tuple(totals)

            state = lax.fori_loop(bounds[s, 0, i], bounds[s, 1, i], key_block, state)
        for h in range(heads):
            top, total = state[h], state[heads + h]
            if last:
                mixed_out[h, :, own] = (mixed[h] / total).astype(BF16)
                top_out[h, :, own] = top + jnp.log2(total)
            else:
                mixed_out[h, :, own] = mixed[h]
                top_out[h, :, own] = top
            total_out[h, :, own] = total
        return 0

    lax.fori_loop(0, rows // BQ, query_block, 0)


def attend(bounds, span, query, carried, keys, values, bases, last):
    heads, hd, rows = query.shape
    vmem = pl.BlockSpec(memory_space=pltpu.VMEM)
    line = jax.ShapeDtypeStruct((heads, 1, rows), F32)
    return pl.pallas_call(
        functools.partial(forward_kernel, bases, heads, last),
        out_shape=(
            jax.ShapeDtypeStruct((heads, hd, rows), BF16 if last else F32),
            line,
            line,
        ),
        in_specs=[pl.BlockSpec(memory_space=pltpu.SMEM)] + [vmem] * (5 + 2 * len(bases)),
        out_specs=(vmem,) * 3,
        scratch_shapes=[pltpu.VMEM((heads, hd, BQ), F32)],
        compiler_params=pltpu.CompilerParams(vmem_limit_bytes=40 << 20),
        cost_estimate=pl.CostEstimate(
            flops=24 * heads * rows * rows * HD,
            bytes_accessed=24 << 20,
            transcendentals=heads * rows * rows,
        ),
    )(bounds, span, query, *carried, *keys, *values)


def tile_back(heads, allowed, keys, values, query, grad, logsum, delta):
    scale = FACTOR * LOG2E
    raws = [contract(keys[h], query[h], ((0,), (0,))) for h in range(heads)]
    grads = [contract(values[h], grad[h], ((0,), (0,))) for h in range(heads)]
    found = []
    for h in range(heads):
        raw = jnp.where(allowed, raws[h] * scale - logsum[h], NEG)
        probs = jnp.exp2(raw)
        found.append((probs.astype(BF16), (probs * (grads[h] - delta[h])).astype(BF16)))
    return found


def backward_kernel(bases, heads, bounds, span, query, grad, logsum, delta, *refs):
    segments = len(bases)
    keys = refs[:segments]
    values = refs[segments : 2 * segments]
    grad_query, grad_keys, grad_values, sum_query, sum_keys, sum_values = refs[2 * segments :]
    sum_query[...] = jnp.zeros_like(sum_query)
    for s, base in enumerate(bases):

        def key_block(j, _, s=s, base=base):
            k_at = pl.multiple_of(j * BK, BK)
            block = pl.ds(k_at, BK)
            place = lax.broadcasted_iota(jnp.int32, (BK, BQ), 0) + (k_at + base)
            if base == 0:
                sum_keys[...] = jnp.zeros_like(sum_keys)
                sum_values[...] = jnp.zeros_like(sum_values)

            def query_block(i, _):
                own = pl.ds(pl.multiple_of(i * BQ, BQ), BQ)
                allowed = (place >= span[0:1, own]) & (place < span[1:2, own])
                q = [query[h, :, own] for h in range(heads)]
                g = [grad[h, :, own] for h in range(heads)]
                k = [keys[s][h, :, block] for h in range(heads)]
                found = tile_back(
                    heads,
                    allowed,
                    k,
                    [values[s][h, :, block] for h in range(heads)],
                    q,
                    g,
                    [logsum[h, :, own] for h in range(heads)],
                    [delta[h, :, own] for h in range(heads)],
                )
                for h in range(heads):
                    probs, grad_raw = found[h]
                    if base == 0:
                        sum_values[h] += contract(g[h], probs, ((1,), (1,)))
                        sum_keys[h] += contract(q[h], grad_raw, ((1,), (1,)))
                    sum_query[h, :, own] += contract(k[h], grad_raw, ((1,), (0,)))
                return 0

            lax.fori_loop(bounds[s, 0, j], bounds[s, 1, j], query_block, 0)
            if base == 0:
                for h in range(heads):
                    grad_keys[h, :, block] = sum_keys[h]
                    grad_values[h, :, block] = sum_values[h]
            return 0

        lax.fori_loop(0, keys[s].shape[2] // BK, key_block, 0)
    grad_query[...] = (sum_query[...] * FACTOR).astype(BF16)


def attend_back(bounds, span, query, grad, logsum, delta, keys, values, bases):
    heads, hd, rows = query.shape
    vmem = pl.BlockSpec(memory_space=pltpu.VMEM)
    full = jax.ShapeDtypeStruct((heads, hd, rows), F32)
    return pl.pallas_call(
        functools.partial(backward_kernel, bases, heads),
        out_shape=(jax.ShapeDtypeStruct((heads, hd, rows), BF16), full, full),
        in_specs=[pl.BlockSpec(memory_space=pltpu.SMEM)] + [vmem] * (5 + 2 * len(bases)),
        out_specs=(vmem,) * 3,
        scratch_shapes=[
            pltpu.VMEM((heads, hd, rows), F32),
            pltpu.VMEM((heads, hd, BK), F32),
            pltpu.VMEM((heads, hd, BK), F32),
        ],
        compiler_params=pltpu.CompilerParams(vmem_limit_bytes=44 << 20),
        cost_estimate=pl.CostEstimate(
            flops=60 * heads * rows * rows * HD,
            bytes_accessed=30 << 20,
            transcendentals=heads * rows * rows,
        ),
    )(bounds, span, query, grad, logsum, delta, *keys, *values)


def others_kernel(segments, heads, bounds, keys, values, keys_in, values_in, *refs):
    spans, query, grad, logsum, delta = (refs[n * segments : (n + 1) * segments] for n in range(5))
    grad_keys, grad_values, sum_keys, sum_values = refs[5 * segments :]

    def key_block(j, _):
        k_at = pl.multiple_of(j * BK, BK)
        block = pl.ds(k_at, BK)
        place = lax.broadcasted_iota(jnp.int32, (BK, BQ), 0) + k_at
        for h in range(heads):
            sum_keys[h] = keys_in[h, :, block]
            sum_values[h] = values_in[h, :, block]
        for s in range(segments):

            def query_block(i, _, s=s):
                own = pl.ds(pl.multiple_of(i * BQ, BQ), BQ)
                allowed = (place >= spans[s][0:1, own]) & (place < spans[s][1:2, own])
                q = [query[s][h, :, own] for h in range(heads)]
                g = [grad[s][h, :, own] for h in range(heads)]
                found = tile_back(
                    heads,
                    allowed,
                    [keys[h, :, block] for h in range(heads)],
                    [values[h, :, block] for h in range(heads)],
                    q,
                    g,
                    [logsum[s][h, :, own] for h in range(heads)],
                    [delta[s][h, :, own] for h in range(heads)],
                )
                for h in range(heads):
                    probs, grad_raw = found[h]
                    sum_values[h] += contract(g[h], probs, ((1,), (1,)))
                    sum_keys[h] += contract(q[h], grad_raw, ((1,), (1,)))
                return 0

            lax.fori_loop(bounds[s, 0, j], bounds[s, 1, j], query_block, 0)
        for h in range(heads):
            grad_keys[h, :, block] = (sum_keys[h] * FACTOR).astype(BF16)
            grad_values[h, :, block] = sum_values[h].astype(BF16)
        return 0

    lax.fori_loop(0, keys.shape[2] // BK, key_block, 0)


def others_back(bounds, keys, values, keys_in, values_in, spans, query, grad, logsum, delta):
    heads, hd, rows = keys.shape
    segments = len(query)
    vmem = pl.BlockSpec(memory_space=pltpu.VMEM)
    shape = jax.ShapeDtypeStruct((heads, hd, rows), BF16)
    return pl.pallas_call(
        functools.partial(others_kernel, segments, heads),
        out_shape=(shape, shape),
        in_specs=[pl.BlockSpec(memory_space=pltpu.SMEM)] + [vmem] * (4 + 5 * segments),
        out_specs=(vmem, vmem),
        scratch_shapes=[pltpu.VMEM((heads, hd, BK), F32), pltpu.VMEM((heads, hd, BK), F32)],
        compiler_params=pltpu.CompilerParams(vmem_limit_bytes=40 << 20),
        cost_estimate=pl.CostEstimate(
            flops=30 * heads * rows * rows * HD,
            bytes_accessed=30 << 20,
            transcendentals=heads * rows * rows // 2,
        ),
    )(bounds, keys, values, keys_in, values_in, *spans, *query, *grad, *logsum, *delta)


def swap(value, axis, bit):
    return lax.ppermute(value, axis, [(i, i ^ bit) for i in range(lax.axis_size(axis))])


def shift(value, axis, distance):
    devices = range(lax.axis_size(axis))
    return lax.ppermute(value, axis, [(i, i + distance) for i in devices if i + distance in devices])


def bits_of(axis):
    size = lax.axis_size(axis)
    return [1 << b for b in range(size.bit_length() - 1)]


def bit_set(axis, bit):
    return (lax.axis_index(axis) & bit) != 0


def sum_all(value, axis):
    for bit in bits_of(axis):
        value = value + swap(value, axis, bit)
    return value


def after(anchor, *values):
    held = values if anchor is None else lax.optimization_barrier((anchor, *values))[1:]
    return held[0] if len(values) == 1 else held


def in_order(mine, other, upper, dim=0):
    return jnp.where(
        upper, jnp.stack([other, mine], axis=dim), jnp.stack([mine, other], axis=dim)
    )


def gather_tensor(value):
    pair = in_order(value, swap(value, "tensor", 2), bit_set("tensor", 2))
    quad = in_order(pair, swap(pair, "tensor", 1), bit_set("tensor", 1), dim=1)
    return quad.reshape((4 * value.shape[0],) + value.shape[1:])


def scatter_tensor(partial):
    n = partial.shape[0] // 4
    core = lax.axis_index("tensor") % 2
    across = lax.axis_index("tensor") // 2
    parts = partial.astype(BF16).reshape((2, 2, n) + partial.shape[1:])
    kept = lax.dynamic_index_in_dim(parts, core, 1, keepdims=False)
    sent = lax.dynamic_index_in_dim(parts, 1 - core, 1, keepdims=False)
    come = swap(sent, "tensor", 1)
    come = after((yield sent), come)
    half = kept.astype(F32) + come.astype(F32)
    half_low = half.astype(BF16)
    stay = lax.dynamic_index_in_dim(half, across, 0, keepdims=False)
    leave = lax.dynamic_index_in_dim(half_low, 1 - across, 0, keepdims=False)
    come = swap(leave, "tensor", 2)
    come = after((yield leave), come)
    return stay + come.astype(F32)


def scatter_data(partial):
    size = lax.axis_size("dp")
    index = lax.axis_index("dp")
    bits = bits_of("dp")
    count = len(bits)
    rest = (partial.shape[0] // size,) + partial.shape[1:]
    held = partial.astype(BF16).reshape((2,) * count + rest)
    left = list(reversed(bits))
    for bit in [1] + bits[:0:-1]:
        axis = left.index(bit)
        mine = (index // bit) % 2
        kept = lax.dynamic_index_in_dim(held, mine, axis, keepdims=False)
        sent = lax.dynamic_index_in_dim(held, 1 - mine, axis, keepdims=False).astype(BF16)
        come = swap(sent, "dp", bit)
        come = after((yield sent), come)
        held = kept.astype(F32) + come.astype(F32)
        left.remove(bit)
    return held


def finish(steps, anchor=None):
    try:
        while True:
            steps.send(anchor)
    except StopIteration as end:
        return end.value


def layer_norm(value):
    center = value - jnp.mean(value, axis=-1, keepdims=True)
    spread = jnp.mean(center * center, axis=-1, keepdims=True)
    return center * lax.rsqrt(spread + 1e-06)


def gelu_tanh(value):
    return jax.nn.gelu(value, approximate=True)


def onehot_sum(select, values, form):
    upper = values.astype(BF16)
    lower = (values - upper.astype(F32)).astype(BF16)
    first = jnp.einsum(form, select, upper, preferred_element_type=F32)
    return first + jnp.einsum(form, select, lower, preferred_element_type=F32)


def on_device(
    tokens,
    condition,
    latent_lengths,
    in_weight,
    in_bias,
    out_weight,
    out_bias,
    up_weight,
    up_bias,
    down_weight,
    down_bias,
    mod_weight,
    mod_bias,
    out_grad,
):
    rows, width = tokens.shape
    latents = condition.shape[0]
    local_width = in_weight.shape[2]
    heads = local_width // HD
    data_size = lax.axis_size("dp")
    data_index = lax.axis_index("dp")
    tensor_index = lax.axis_index("tensor")
    quarter = rows // 4
    row_start = tensor_index * quarter

    def mine(value):
        return lax.dynamic_slice_in_dim(value, row_start, quarter, 0)

    places = jnp.arange(latents, dtype=jnp.int32)
    earlier = places[None, :] < places[:, None]
    starts = jnp.sum(jnp.where(earlier, latent_lengths[None, :], 0), axis=1)
    ends = starts + latent_lengths
    first_row = data_index * rows
    own_places = first_row + jnp.arange(rows, dtype=jnp.int32)

    def span_of(at):
        inside = (at[:, None] >= starts[None, :]) & (at[:, None] < ends[None, :])
        begin = jnp.sum(jnp.where(inside, starts[None, :] - first_row, 0), axis=1)
        end = jnp.sum(jnp.where(inside, ends[None, :] - first_row, 0), axis=1)
        return begin, end, inside

    bases = (-rows, 0, rows)
    windows = [span_of(own_places + base) for base in bases]
    spans = [jnp.stack(window[:2]) for window in windows]
    selects = [window[2].astype(BF16) for window in windows]
    begin, end = windows[1][:2]
    span, select = spans[1], selects[1]
    select_mine = mine(select)
    forward_bounds, backward_bounds, other_bounds = [], [], []
    for base in bases:
        low = jnp.clip(begin[::BQ] - base, 0, rows) // BK
        high = (jnp.clip(end[BQ - 1 :: BQ] - base, 0, rows) + BK - 1) // BK
        forward_bounds.append(jnp.stack([low, high]))
        key_at = first_row + base + jnp.arange(rows // BK, dtype=jnp.int32) * BK
        low = jnp.clip(span_of(key_at)[0], 0, rows) // BQ
        high = (jnp.clip(span_of(key_at + BK - 1)[1], 0, rows) + BQ - 1) // BQ
        valid = (key_at >= 0) & (key_at < rows * data_size)
        backward_bounds.append(jnp.where(valid[None, :], jnp.stack([low, high]), 0))
        low = jnp.clip(begin[::BK] - base, 0, rows) // BQ
        high = (jnp.clip(end[BK - 1 :: BK] - base, 0, rows) + BQ - 1) // BQ
        other_bounds.append(jnp.stack([low, high]))
    backward_bounds = jnp.stack(backward_bounds)
    other_bounds = jnp.stack([other_bounds[0], other_bounds[2]])

    tokens_mine = mine(tokens)
    behind_tokens = gather_tensor(shift(tokens_mine, "dp", 1))
    ahead_tokens = gather_tensor(shift(tokens_mine, "dp", -1))

    cond_full = condition.astype(F32)
    silu_cond = jax.nn.silu(cond_full).astype(BF16)
    mod_local = (
        jnp.dot(silu_cond, mod_weight, preferred_element_type=F32) + mod_bias.astype(F32)
    ).astype(BF16)
    modulation = gather_tensor(mod_local[None])
    modulation = modulation.transpose(1, 0, 2).reshape(latents, 6 * width)

    def spread(chosen, first, count):
        return jnp.dot(
            chosen,
            modulation[:, first * width : (first + count) * width],
            preferred_element_type=BF16,
        )

    others = spread(select_mine, 2, 4).astype(F32)
    gate_a, shift_m, scale_m, gate_m = (others[:, i * width : (i + 1) * width] for i in range(4))
    gate_m_all = spread(select, 5, 1).astype(F32)

    bias_full = in_bias.astype(F32)
    proj_bias = jnp.stack([bias_full[0], jnp.zeros_like(bias_full[0]), bias_full[1]])

    def entry_of(rows_of, chosen):
        shift_scale = spread(chosen, 0, 2)
        scale = shift_scale[:, width:].astype(F32)
        value = rows_of.astype(F32)
        center = value - jnp.mean(value, axis=-1, keepdims=True)
        inverse = lax.rsqrt(jnp.mean(center * center, axis=-1, keepdims=True) + 1e-06)
        normed = center * inverse
        entry = (normed * (1.0 + scale) + shift_scale[:, :width].astype(F32)).astype(BF16)
        return entry, normed, inverse

    def project(entry):
        found = jnp.einsum("dcf,td->cft", in_weight, entry, preferred_element_type=F32)
        found = (found + proj_bias[:, :, None]).astype(BF16)
        return found.reshape(3, heads, HD, rows)

    entry, normed, inverse = entry_of(tokens, select)
    normed_turned, inverse = normed.T, inverse.T
    own = project(entry)
    sides = [
        project(entry_of(behind_tokens, selects[0])[0]),
        project(entry_of(ahead_tokens, selects[2])[0]),
    ]
    query = own[0]
    line = jnp.zeros((heads, 1, rows), F32)
    carried = attend(
        jnp.stack([forward_bounds[1]]),
        span,
        query,
        (jnp.zeros((heads, HD, rows), F32), line + NEG, line),
        [own[1]],
        [own[2]],
        (0,),
        False,
    )
    attended, logsum, _ = attend(
        jnp.stack([forward_bounds[0], forward_bounds[2]]),
        span,
        query,
        carried,
        [side[1] for side in sides],
        [side[2] for side in sides],
        (-rows, rows),
        True,
    )
    attended_flat = attended.reshape(local_width, rows)
    attn_part = lax.dot_general(
        attended_flat, out_weight, (((0,), (1,)), ((), ())), preferred_element_type=F32
    )
    attn_steps = scatter_tensor(attn_part)
    next(attn_steps)
    branch = finish(attn_steps) + out_bias.astype(F32)

    middle = tokens_mine.astype(F32) + gate_a * branch
    normed_m, norm_back_m = jax.vjp(layer_norm, middle)
    entry_m = gather_tensor((normed_m * (1.0 + scale_m) + shift_m).astype(BF16))
    hidden_pre = jnp.dot(entry_m, up_weight, preferred_element_type=F32) + up_bias.astype(F32)
    hidden_full, gelu_back = jax.vjp(gelu_tanh, hidden_pre)
    hidden = hidden_full.astype(BF16)
    grad_out = out_grad.astype(F32)
    grad_branch_m = (gate_m_all * grad_out).astype(BF16)
    grad_hidden = jnp.einsum("td,df->tf", grad_branch_m, down_weight, preferred_element_type=F32)
    grad_pre = gelu_back(grad_hidden)[0].astype(BF16)
    grad_down_w = jnp.einsum("td,tf->df", grad_branch_m, hidden, preferred_element_type=F32)
    down_steps = scatter_data(grad_down_w)
    down_sent = next(down_steps)
    grad_pre = after(down_sent, grad_pre)
    entry_part = jnp.einsum("tf,df->td", grad_pre, up_weight, preferred_element_type=F32)
    entry_steps = scatter_tensor(entry_part)
    grad_pre = after(next(entry_steps), grad_pre)
    grad_out_mine = mine(out_grad).astype(F32)
    grad_up_w = jnp.einsum("td,tf->df", entry_m, grad_pre, preferred_element_type=F32)
    up_steps = scatter_data(grad_up_w)
    up_sent = next(up_steps)
    grad_entry_m = finish(entry_steps, up_sent)
    grad_down_b = jnp.sum(grad_branch_m.astype(F32), axis=0)
    grad_up_b = jnp.sum(grad_pre.astype(F32), axis=0)
    grad_middle = grad_out_mine + norm_back_m(grad_entry_m * (1.0 + scale_m))[0]
    grad_gate_a = grad_middle * branch
    grad_branch_mine = (gate_a * grad_middle).astype(BF16)
    grad_out_b = jnp.sum(grad_branch_mine.astype(F32), axis=0)
    grad_branch = gather_tensor(grad_branch_mine)
    grad_attended = lax.dot_general(
        out_weight, grad_branch, (((0,), (1,)), ((), ())), preferred_element_type=F32
    ).astype(BF16)

    mlp_part = jnp.einsum(
        "tf,df->td",
        after(grad_branch_mine, hidden),
        down_weight,
        preferred_element_type=F32,
    )
    mlp_steps = scatter_tensor(mlp_part)
    next(mlp_steps)

    grad_heads = grad_attended.reshape(heads, HD, rows)
    delta = jnp.sum(grad_heads.astype(F32) * attended.astype(F32), axis=1, keepdims=True)
    stats = jnp.stack([logsum, delta])
    side_grads = [shift(grad_heads, "dp", 1), shift(grad_heads, "dp", -1)]
    side_stats = [shift(stats, "dp", 1), shift(stats, "dp", -1)]
    grad_query, part_keys, part_values = attend_back(
        backward_bounds,
        span,
        query,
        grad_heads,
        logsum,
        delta,
        [sides[0][1], own[1], sides[1][1]],
        [sides[0][2], own[2], sides[1][2]],
        bases,
    )
    mlp_steps.send(grad_heads)
    down_steps.send(grad_heads)
    up_steps.send(grad_query)
    branch_m = finish(mlp_steps, grad_query) + down_bias.astype(F32)
    output = (middle + gate_m * branch_m).astype(BF16)
    grad_gate_m = grad_out_mine * branch_m
    grad_out_w = lax.dot_general(
        grad_branch, attended_flat, (((0,), (1,)), ((), ())), preferred_element_type=F32
    )
    grad_keys, grad_values = others_back(
        other_bounds,
        own[1],
        own[2],
        part_keys,
        part_values,
        [spans[0], spans[2]],
        [side[0] for side in sides],
        side_grads,
        [side[0] for side in side_stats],
        [side[1] for side in side_stats],
    )
    grad_proj = [x.reshape(local_width, rows) for x in (grad_query, grad_keys, grad_values)]
    grad_q_w, grad_k_w, grad_v_w = (
        lax.dot_general(entry, x, (((0,), (1,)), ((), ())), preferred_element_type=F32)
        for x in grad_proj
    )
    early_steps = scatter_data(jnp.concatenate([grad_out_w, grad_q_w], axis=1))
    next(early_steps)
    late_steps = scatter_data(jnp.concatenate([grad_k_w, grad_v_w], axis=1))
    late_sent = next(late_steps)
    early_steps.send(late_sent)
    grad_proj = after(late_sent, *grad_proj)
    grad_in_b = jnp.stack([jnp.sum(grad_proj[c].astype(F32), axis=1) for c in (0, 2)])
    grad_entry = lax.dot_general(
        in_weight.reshape(width, 3 * local_width),
        jnp.concatenate(grad_proj, axis=0),
        (((1,), (0,)), ((), ())),
        preferred_element_type=F32,
    )
    scale_turned = lax.dot_general(
        modulation[:, width : 2 * width],
        select,
        (((0,), (1,)), ((), ())),
        preferred_element_type=BF16,
    ).astype(F32)
    scaled = grad_entry * (1.0 + scale_turned)
    input_part = (
        scaled
        - jnp.mean(scaled, axis=0, keepdims=True)
        - normed_turned * jnp.mean(scaled * normed_turned, axis=0, keepdims=True)
    ) * inverse

    split_terms = jnp.concatenate([grad_entry, grad_entry * normed_turned], axis=0)
    kept_terms = jnp.concatenate(
        [grad_gate_a, grad_entry_m, grad_entry_m * normed_m, grad_gate_m], axis=1
    )
    per_latent = jnp.concatenate(
        [onehot_sum(select, split_terms, "tl,mt->lm"), onehot_sum(select_mine, kept_terms, "tl,tm->lm")],
        axis=1,
    )
    columns_here = mod_weight.shape[1]
    arranged = per_latent.reshape(latents, 4, columns_here).transpose(1, 0, 2)
    arranged = arranged.reshape(4, latents * columns_here)

    def for_device(flip):
        chosen = lax.dynamic_index_in_dim(arranged, tensor_index ^ flip, 0, keepdims=False)
        return jnp.concatenate([chosen, grad_out_b])

    given = [for_device(flip) for flip in range(4)]
    come = [swap(given[flip], "tensor", flip) for flip in (1, 2, 3)]
    placed = lax.dynamic_update_slice_in_dim(
        jnp.zeros((width, rows), F32), grad_middle.T, row_start, 1
    )
    tokens_steps = scatter_tensor(input_part + placed)
    tokens_sent = next(tokens_steps)
    come = after(tokens_sent, *come)
    small = (given[0] + come[0]) + (come[1] + come[2])
    small = jnp.concatenate([small, grad_in_b.reshape(-1), grad_up_b, grad_down_b])
    tokens_sent = tokens_steps.send(small)
    for place, bit in enumerate(bits_of("dp")):
        come = swap(small, "dp", bit)
        if place == 0:
            come = after(tokens_sent, come)
        small = small + come
        if place == 0:
            up_steps.send(small)
        if place == 1:
            late_sent = late_steps.send(small)
            small = after(late_sent, small)
    cuts, at = [], 0
    for size in (latents * columns_here, width, 2 * local_width, grad_up_b.shape[0]):
        at += size
        cuts.append(at)
    grad_mod, sum_out_b, sum_in_b, sum_up_b, sum_down_b = jnp.split(small, cuts)
    grad_mod = grad_mod.reshape(latents, columns_here).astype(BF16)
    own_width = width // data_size
    own_silu = lax.dynamic_slice_in_dim(silu_cond, data_index * own_width, own_width, 1)
    grad_mod_w = jnp.einsum("ld,lm->dm", own_silu, grad_mod, preferred_element_type=F32)
    grad_mod_b = jnp.sum(grad_mod.astype(F32), axis=0)
    own_count = latents // data_size
    own_grad_mod = lax.dynamic_slice_in_dim(grad_mod, data_index * own_count, own_count, 0)
    own_cond = lax.dynamic_slice_in_dim(cond_full, data_index * own_count, own_count, 0)
    silu_grad = jnp.einsum("lm,dm->ld", own_grad_mod, mod_weight, preferred_element_type=F32)
    cond_part = jax.vjp(jax.nn.silu, own_cond)[1](silu_grad)[0]
    cond_parts = cond_part.reshape(own_count, 4, width // 4).transpose(1, 0, 2)
    grad_cond = lax.dynamic_index_in_dim(cond_parts, tensor_index, 0, keepdims=False)
    for bit in (1, 2, 3):
        grad_cond = grad_cond + swap(
            lax.dynamic_index_in_dim(cond_parts, tensor_index ^ bit, 0, keepdims=False),
            "tensor",
            bit,
        )

    grad_tokens = finish(tokens_steps, grad_mod_w).T
    sum_down_w = finish(down_steps, grad_keys)
    sum_up_w = finish(up_steps, grad_mod_w)
    early = finish(early_steps, grad_mod_w)
    late = finish(late_steps)
    sum_out_w = early[:, :local_width]
    sum_in_w = jnp.stack(
        [early[:, local_width:], late[:, :local_width], late[:, local_width:]], axis=1
    )
    return (
        output,
        grad_tokens,
        grad_cond,
        sum_in_w,
        sum_in_b.reshape(2, local_width),
        sum_out_w,
        sum_out_b,
        sum_up_w,
        sum_up_b,
        sum_down_w,
        sum_down_b,
        grad_mod_w,
        grad_mod_b,
    )


def solution(mesh):
    placed = (
        P("dp", None),
        P(),
        P(),
        P(None, None, "tensor"),
        P(None, "tensor"),
        P(None, "tensor"),
        P(),
        P(None, "tensor"),
        P("tensor"),
        P(None, "tensor"),
        P(),
        P(None, "tensor"),
        P("tensor"),
        P("dp", None),
    )
    return jax.shard_map(
        on_device,
        mesh=mesh,
        in_specs=placed,
        out_specs=(
            P(("dp", "tensor"), None),
            P("dp", "tensor"),
            P("dp", "tensor"),
            P("dp", None, "tensor"),
            P(None, "tensor"),
            P("dp", "tensor"),
            P(),
            P("dp", "tensor"),
            P("tensor"),
            P("dp", "tensor"),
            P(),
            P("dp", "tensor"),
            P("tensor"),
        ),
        check_vma=False,
    )
```

```python
import functools
import math

import jax
import jax.numpy as jnp
from jax import lax
from jax.experimental import pallas as pl
from jax.experimental.layout import Layout, with_layout_constraint
from jax.experimental.pallas import tpu as pltpu
from jax.sharding import PartitionSpec as P

HD = 72
FACTOR = HD ** (-0.5)
LOG2E = math.log2(math.e)
NEG = -1e30
BQ = 256
BK = 256
F32 = jnp.float32
BF16 = jnp.bfloat16


def contract(a, b, dims):
    return lax.dot_general(a, b, (dims, ((), ())), preferred_element_type=F32)


def forward_kernel(bases, heads, last, bounds, span, query, mixed_in, top_in, total_in, *refs):
    segments = len(bases)
    keys = refs[:segments]
    values = refs[segments : 2 * segments]
    mixed_out, top_out, total_out, mixed = refs[2 * segments :]
    rows = query.shape[2]
    scale = FACTOR * LOG2E

    def query_block(i, _):
        own = pl.ds(pl.multiple_of(i * BQ, BQ), BQ)
        begin = span[0:1, own]
        end = span[1:2, own]
        for h in range(heads):
            mixed[h] = mixed_in[h, :, own]
        state = tuple(top_in[h, :, own] for h in range(heads)) + tuple(
            total_in[h, :, own] for h in range(heads)
        )
        for s, base in enumerate(bases):

            def key_block(j, state, s=s, base=base):
                k_at = pl.multiple_of(j * BK, BK)
                block = pl.ds(k_at, BK)
                place = lax.broadcasted_iota(jnp.int32, (BK, BQ), 0) + (k_at + base)
                allowed = (place >= begin) & (place < end)
                raws = [
                    contract(keys[s][h, :, block], query[h, :, own], ((0,), (0,)))
                    for h in range(heads)
                ]
                tops, totals, shrinks, lows = [], [], [], []
                for h in range(heads):
                    raw = jnp.where(allowed, raws[h] * scale, NEG)
                    top = jnp.maximum(state[h], jnp.max(raw, axis=0, keepdims=True))
                    probs = jnp.exp2(raw - top)
                    shrink = jnp.exp2(state[h] - top)
                    tops.append(top)
                    totals.append(state[heads + h] * shrink + jnp.sum(probs, axis=0, keepdims=True))
                    shrinks.append(shrink)
                    lows.append(probs.astype(BF16))
                for h in range(heads):
                    mixed[h] = mixed[h] * shrinks[h] + contract(
                        values[s][h, :, block], lows[h], ((1,), (0,))
                    )
                return tuple(tops) + tuple(totals)

            state = lax.fori_loop(bounds[s, 0, i], bounds[s, 1, i], key_block, state)
        for h in range(heads):
            top, total = state[h], state[heads + h]
            if last:
                mixed_out[h, :, own] = (mixed[h] / total).astype(BF16)
                top_out[h, :, own] = top + jnp.log2(total)
            else:
                mixed_out[h, :, own] = mixed[h]
                top_out[h, :, own] = top
            total_out[h, :, own] = total
        return 0

    lax.fori_loop(0, rows // BQ, query_block, 0)


def attend(bounds, span, query, carried, keys, values, bases, last):
    heads, hd, rows = query.shape
    vmem = pl.BlockSpec(memory_space=pltpu.VMEM)
    line = jax.ShapeDtypeStruct((heads, 1, rows), F32)
    return pl.pallas_call(
        functools.partial(forward_kernel, bases, heads, last),
        out_shape=(
            jax.ShapeDtypeStruct((heads, hd, rows), BF16 if last else F32),
            line,
            line,
        ),
        in_specs=[pl.BlockSpec(memory_space=pltpu.SMEM)] + [vmem] * (5 + 2 * len(bases)),
        out_specs=(vmem,) * 3,
        scratch_shapes=[pltpu.VMEM((heads, hd, BQ), F32)],
        compiler_params=pltpu.CompilerParams(vmem_limit_bytes=40 << 20),
        cost_estimate=pl.CostEstimate(flops=1 << 20, bytes_accessed=1 << 20, transcendentals=0),
    )(bounds, span, query, *carried, *keys, *values)


def tile_back(heads, allowed, keys, values, query, grad, logsum, delta):
    scale = FACTOR * LOG2E
    raws = [contract(keys[h], query[h], ((0,), (0,))) for h in range(heads)]
    grads = [contract(values[h], grad[h], ((0,), (0,))) for h in range(heads)]
    found = []
    for h in range(heads):
        raw = jnp.where(allowed, raws[h] * scale - logsum[h], NEG)
        probs = jnp.exp2(raw)
        found.append((probs.astype(BF16), (probs * (grads[h] - delta[h])).astype(BF16)))
    return found


def backward_kernel(bases, heads, bounds, span, query, grad, logsum, delta, *refs):
    segments = len(bases)
    keys = refs[:segments]
    values = refs[segments : 2 * segments]
    grad_query, grad_keys, grad_values, sum_query, sum_keys, sum_values = refs[2 * segments :]
    sum_query[...] = jnp.zeros_like(sum_query)
    for s, base in enumerate(bases):

        def key_block(j, _, s=s, base=base):
            k_at = pl.multiple_of(j * BK, BK)
            block = pl.ds(k_at, BK)
            place = lax.broadcasted_iota(jnp.int32, (BK, BQ), 0) + (k_at + base)
            if base == 0:
                sum_keys[...] = jnp.zeros_like(sum_keys)
                sum_values[...] = jnp.zeros_like(sum_values)

            def query_block(i, _):
                own = pl.ds(pl.multiple_of(i * BQ, BQ), BQ)
                allowed = (place >= span[0:1, own]) & (place < span[1:2, own])
                q = [query[h, :, own] for h in range(heads)]
                g = [grad[h, :, own] for h in range(heads)]
                k = [keys[s][h, :, block] for h in range(heads)]
                found = tile_back(
                    heads,
                    allowed,
                    k,
                    [values[s][h, :, block] for h in range(heads)],
                    q,
                    g,
                    [logsum[h, :, own] for h in range(heads)],
                    [delta[h, :, own] for h in range(heads)],
                )
                for h in range(heads):
                    probs, grad_raw = found[h]
                    if base == 0:
                        sum_values[h] += contract(g[h], probs, ((1,), (1,)))
                        sum_keys[h] += contract(q[h], grad_raw, ((1,), (1,)))
                    sum_query[h, :, own] += contract(k[h], grad_raw, ((1,), (0,)))
                return 0

            lax.fori_loop(bounds[s, 0, j], bounds[s, 1, j], query_block, 0)
            if base == 0:
                for h in range(heads):
                    grad_keys[h, :, block] = sum_keys[h]
                    grad_values[h, :, block] = sum_values[h]
            return 0

        lax.fori_loop(0, keys[s].shape[2] // BK, key_block, 0)
    grad_query[...] = (sum_query[...] * FACTOR).astype(BF16)


def attend_back(bounds, span, query, grad, logsum, delta, keys, values, bases):
    heads, hd, rows = query.shape
    vmem = pl.BlockSpec(memory_space=pltpu.VMEM)
    full = jax.ShapeDtypeStruct((heads, hd, rows), F32)
    return pl.pallas_call(
        functools.partial(backward_kernel, bases, heads),
        out_shape=(jax.ShapeDtypeStruct((heads, hd, rows), BF16), full, full),
        in_specs=[pl.BlockSpec(memory_space=pltpu.SMEM)] + [vmem] * (5 + 2 * len(bases)),
        out_specs=(vmem,) * 3,
        scratch_shapes=[
            pltpu.VMEM((heads, hd, rows), F32),
            pltpu.VMEM((heads, hd, BK), F32),
            pltpu.VMEM((heads, hd, BK), F32),
        ],
        compiler_params=pltpu.CompilerParams(vmem_limit_bytes=44 << 20),
        cost_estimate=pl.CostEstimate(flops=1 << 20, bytes_accessed=1 << 20, transcendentals=0),
    )(bounds, span, query, grad, logsum, delta, *keys, *values)


def others_kernel(segments, heads, bounds, keys, values, keys_in, values_in, *refs):
    spans, query, grad, logsum, delta = (refs[n * segments : (n + 1) * segments] for n in range(5))
    grad_keys, grad_values, sum_keys, sum_values = refs[5 * segments :]

    def key_block(j, _):
        k_at = pl.multiple_of(j * BK, BK)
        block = pl.ds(k_at, BK)
        place = lax.broadcasted_iota(jnp.int32, (BK, BQ), 0) + k_at
        for h in range(heads):
            sum_keys[h] = keys_in[h, :, block]
            sum_values[h] = values_in[h, :, block]
        for s in range(segments):

            def query_block(i, _, s=s):
                own = pl.ds(pl.multiple_of(i * BQ, BQ), BQ)
                allowed = (place >= spans[s][0:1, own]) & (place < spans[s][1:2, own])
                q = [query[s][h, :, own] for h in range(heads)]
                g = [grad[s][h, :, own] for h in range(heads)]
                found = tile_back(
                    heads,
                    allowed,
                    [keys[h, :, block] for h in range(heads)],
                    [values[h, :, block] for h in range(heads)],
                    q,
                    g,
                    [logsum[s][h, :, own] for h in range(heads)],
                    [delta[s][h, :, own] for h in range(heads)],
                )
                for h in range(heads):
                    probs, grad_raw = found[h]
                    sum_values[h] += contract(g[h], probs, ((1,), (1,)))
                    sum_keys[h] += contract(q[h], grad_raw, ((1,), (1,)))
                return 0

            lax.fori_loop(bounds[s, 0, j], bounds[s, 1, j], query_block, 0)
        for h in range(heads):
            grad_keys[h, :, block] = (sum_keys[h] * FACTOR).astype(BF16)
            grad_values[h, :, block] = sum_values[h].astype(BF16)
        return 0

    lax.fori_loop(0, keys.shape[2] // BK, key_block, 0)


def others_back(bounds, keys, values, keys_in, values_in, spans, query, grad, logsum, delta):
    heads, hd, rows = keys.shape
    segments = len(query)
    vmem = pl.BlockSpec(memory_space=pltpu.VMEM)
    shape = jax.ShapeDtypeStruct((heads, hd, rows), BF16)
    return pl.pallas_call(
        functools.partial(others_kernel, segments, heads),
        out_shape=(shape, shape),
        in_specs=[pl.BlockSpec(memory_space=pltpu.SMEM)] + [vmem] * (4 + 5 * segments),
        out_specs=(vmem, vmem),
        scratch_shapes=[pltpu.VMEM((heads, hd, BK), F32), pltpu.VMEM((heads, hd, BK), F32)],
        compiler_params=pltpu.CompilerParams(vmem_limit_bytes=40 << 20),
        cost_estimate=pl.CostEstimate(flops=1 << 20, bytes_accessed=1 << 20, transcendentals=0),
    )(bounds, keys, values, keys_in, values_in, *spans, *query, *grad, *logsum, *delta)


def swap(value, axis, bit):
    return lax.ppermute(value, axis, [(i, i ^ bit) for i in range(lax.axis_size(axis))])


def shift(value, axis, distance):
    devices = range(lax.axis_size(axis))
    return lax.ppermute(value, axis, [(i, i + distance) for i in devices if i + distance in devices])


def bits_of(axis):
    size = lax.axis_size(axis)
    return [1 << b for b in range(size.bit_length() - 1)]


def bit_set(axis, bit):
    return (lax.axis_index(axis) & bit) != 0


def sum_all(value, axis):
    for bit in bits_of(axis):
        value = value + swap(value, axis, bit)
    return value


def after(anchor, *values):
    held = values if anchor is None else lax.optimization_barrier((anchor, *values))[1:]
    return held[0] if len(values) == 1 else held


def in_order(mine, other, upper, dim=0):
    return jnp.where(
        upper, jnp.stack([other, mine], axis=dim), jnp.stack([mine, other], axis=dim)
    )


def gather_tensor(value):
    pair = in_order(value, swap(value, "tensor", 2), bit_set("tensor", 2))
    quad = in_order(pair, swap(pair, "tensor", 1), bit_set("tensor", 1), dim=1)
    return quad.reshape((4 * value.shape[0],) + value.shape[1:])


def scatter_tensor(partial):
    n = partial.shape[0] // 4
    core = lax.axis_index("tensor") % 2
    across = lax.axis_index("tensor") // 2
    parts = partial.astype(BF16).reshape((2, 2, n) + partial.shape[1:])
    kept = lax.dynamic_index_in_dim(parts, core, 1, keepdims=False)
    sent = lax.dynamic_index_in_dim(parts, 1 - core, 1, keepdims=False)
    come = swap(sent, "tensor", 1)
    come = after((yield sent), come)
    half = kept.astype(F32) + come.astype(F32)
    half_low = half.astype(BF16)
    stay = lax.dynamic_index_in_dim(half, across, 0, keepdims=False)
    leave = lax.dynamic_index_in_dim(half_low, 1 - across, 0, keepdims=False)
    come = swap(leave, "tensor", 2)
    come = after((yield leave), come)
    return stay + come.astype(F32)


def scatter_data(partial):
    size = lax.axis_size("dp")
    index = lax.axis_index("dp")
    bits = bits_of("dp")
    count = len(bits)
    rest = (partial.shape[0] // size,) + partial.shape[1:]
    held = partial.astype(BF16).reshape((2,) * count + rest)
    left = list(reversed(bits))
    for bit in [1] + bits[:0:-1]:
        axis = left.index(bit)
        mine = (index // bit) % 2
        kept = lax.dynamic_index_in_dim(held, mine, axis, keepdims=False)
        sent = lax.dynamic_index_in_dim(held, 1 - mine, axis, keepdims=False).astype(BF16)
        come = swap(sent, "dp", bit)
        come = after((yield sent), come)
        held = kept.astype(F32) + come.astype(F32)
        left.remove(bit)
    return held


def by_rows(value):
    return with_layout_constraint(value, Layout(major_to_minor=(0, 1)))


def finish(steps, anchor=None):
    try:
        while True:
            steps.send(anchor)
    except StopIteration as end:
        return end.value


def layer_norm(value):
    center = value - jnp.mean(value, axis=-1, keepdims=True)
    spread = jnp.mean(center * center, axis=-1, keepdims=True)
    return center * lax.rsqrt(spread + 1e-06)


def gelu_tanh(value):
    return jax.nn.gelu(value, approximate=True)


def onehot_sum(select, values, form):
    upper = values.astype(BF16)
    lower = (values - upper.astype(F32)).astype(BF16)
    first = jnp.einsum(form, select, upper, preferred_element_type=F32)
    return first + jnp.einsum(form, select, lower, preferred_element_type=F32)


def on_device(
    tokens,
    condition,
    latent_lengths,
    in_weight,
    in_bias,
    out_weight,
    out_bias,
    up_weight,
    up_bias,
    down_weight,
    down_bias,
    mod_weight,
    mod_bias,
    out_grad,
):
    rows, width = tokens.shape
    latents = condition.shape[0]
    local_width = in_weight.shape[2]
    heads = local_width // HD
    data_size = lax.axis_size("dp")
    data_index = lax.axis_index("dp")
    tensor_index = lax.axis_index("tensor")
    quarter = rows // 4
    row_start = tensor_index * quarter

    def mine(value):
        return lax.dynamic_slice_in_dim(value, row_start, quarter, 0)

    places = jnp.arange(latents, dtype=jnp.int32)
    earlier = places[None, :] < places[:, None]
    starts = jnp.sum(jnp.where(earlier, latent_lengths[None, :], 0), axis=1)
    ends = starts + latent_lengths
    first_row = data_index * rows
    own_places = first_row + jnp.arange(rows, dtype=jnp.int32)

    def span_of(at):
        inside = (at[:, None] >= starts[None, :]) & (at[:, None] < ends[None, :])
        begin = jnp.sum(jnp.where(inside, starts[None, :] - first_row, 0), axis=1)
        end = jnp.sum(jnp.where(inside, ends[None, :] - first_row, 0), axis=1)
        return begin, end, inside

    bases = (-rows, 0, rows)
    windows = [span_of(own_places + base) for base in bases]
    spans = [jnp.stack(window[:2]) for window in windows]
    selects = [window[2].astype(BF16) for window in windows]
    begin, end = windows[1][:2]
    span, select = spans[1], selects[1]
    select_mine = mine(select)
    forward_bounds, backward_bounds, other_bounds = [], [], []
    for base in bases:
        low = jnp.clip(begin[::BQ] - base, 0, rows) // BK
        high = (jnp.clip(end[BQ - 1 :: BQ] - base, 0, rows) + BK - 1) // BK
        forward_bounds.append(jnp.stack([low, high]))
        key_at = first_row + base + jnp.arange(rows // BK, dtype=jnp.int32) * BK
        low = jnp.clip(span_of(key_at)[0], 0, rows) // BQ
        high = (jnp.clip(span_of(key_at + BK - 1)[1], 0, rows) + BQ - 1) // BQ
        valid = (key_at >= 0) & (key_at < rows * data_size)
        backward_bounds.append(jnp.where(valid[None, :], jnp.stack([low, high]), 0))
        low = jnp.clip(begin[::BK] - base, 0, rows) // BQ
        high = (jnp.clip(end[BK - 1 :: BK] - base, 0, rows) + BQ - 1) // BQ
        other_bounds.append(jnp.stack([low, high]))
    backward_bounds = jnp.stack(backward_bounds)
    other_bounds = jnp.stack([other_bounds[0], other_bounds[2]])

    tokens_mine = mine(tokens)
    behind_tokens = gather_tensor(shift(tokens_mine, "dp", 1))
    ahead_tokens = gather_tensor(shift(tokens_mine, "dp", -1))

    cond_full = condition.astype(F32)
    silu_cond = jax.nn.silu(cond_full).astype(BF16)
    mod_local = (
        jnp.dot(silu_cond, mod_weight, preferred_element_type=F32) + mod_bias.astype(F32)
    ).astype(BF16)
    modulation = gather_tensor(mod_local[None])
    modulation = modulation.transpose(1, 0, 2).reshape(latents, 6 * width)

    def spread(chosen, first, count):
        return jnp.dot(
            chosen,
            modulation[:, first * width : (first + count) * width],
            preferred_element_type=BF16,
        )

    others = spread(select_mine, 2, 4).astype(F32)
    gate_a, shift_m, scale_m, gate_m = (others[:, i * width : (i + 1) * width] for i in range(4))
    gate_m_all = spread(select, 5, 1).astype(F32)

    bias_full = in_bias.astype(F32)
    proj_bias = jnp.stack([bias_full[0], jnp.zeros_like(bias_full[0]), bias_full[1]])

    def entry_of(rows_of, chosen):
        shift_scale = spread(chosen, 0, 2)
        scale = shift_scale[:, width:].astype(F32)
        value = rows_of.astype(F32)
        center = value - jnp.mean(value, axis=-1, keepdims=True)
        inverse = lax.rsqrt(jnp.mean(center * center, axis=-1, keepdims=True) + 1e-06)
        normed = center * inverse
        entry = (normed * (1.0 + scale) + shift_scale[:, :width].astype(F32)).astype(BF16)
        return entry, normed, inverse

    def project(entry):
        found = jnp.einsum("dcf,td->cft", in_weight, entry, preferred_element_type=F32)
        found = (found + proj_bias[:, :, None]).astype(BF16)
        return found.reshape(3, heads, HD, rows)

    entry, normed, inverse = entry_of(tokens, select)
    normed_turned, inverse = by_rows(normed.T), inverse.T
    own = project(entry)
    sides = [
        project(entry_of(behind_tokens, selects[0])[0]),
        project(entry_of(ahead_tokens, selects[2])[0]),
    ]
    query = own[0]
    line = jnp.zeros((heads, 1, rows), F32)
    carried = attend(
        jnp.stack([forward_bounds[1]]),
        span,
        query,
        (jnp.zeros((heads, HD, rows), F32), line + NEG, line),
        [own[1]],
        [own[2]],
        (0,),
        False,
    )
    attended, logsum, _ = attend(
        jnp.stack([forward_bounds[0], forward_bounds[2]]),
        span,
        query,
        carried,
        [side[1] for side in sides],
        [side[2] for side in sides],
        (-rows, rows),
        True,
    )
    side_attended = [shift(attended, "dp", 1), shift(attended, "dp", -1)]
    side_logsum = [shift(logsum, "dp", 1), shift(logsum, "dp", -1)]
    attended_flat = attended.reshape(local_width, rows)
    attn_part = lax.dot_general(
        attended_flat, out_weight, (((0,), (1,)), ((), ())), preferred_element_type=F32
    )
    attn_steps = scatter_tensor(attn_part)
    next(attn_steps)
    branch = finish(attn_steps) + out_bias.astype(F32)

    middle = tokens_mine.astype(F32) + gate_a * branch
    normed_m, norm_back_m = jax.vjp(layer_norm, middle)
    entry_m = gather_tensor((normed_m * (1.0 + scale_m) + shift_m).astype(BF16))
    entry_m, *side_attended = after(side_logsum[1], entry_m, *side_attended)
    hidden_pre = jnp.dot(entry_m, up_weight, preferred_element_type=F32) + up_bias.astype(F32)
    hidden_full, gelu_back = jax.vjp(gelu_tanh, hidden_pre)
    hidden = hidden_full.astype(BF16)
    grad_out = out_grad.astype(F32)
    grad_branch_m = (gate_m_all * grad_out).astype(BF16)
    grad_hidden = jnp.einsum("td,df->tf", grad_branch_m, down_weight, preferred_element_type=F32)
    grad_pre = gelu_back(grad_hidden)[0].astype(BF16)
    grad_down_w = jnp.einsum("td,tf->df", grad_branch_m, hidden, preferred_element_type=F32)
    down_steps = scatter_data(grad_down_w)
    down_sent = next(down_steps)
    grad_pre = after(down_sent, grad_pre)
    entry_part = jnp.einsum("tf,df->td", grad_pre, up_weight, preferred_element_type=F32)
    entry_steps = scatter_tensor(entry_part)
    grad_pre = after(next(entry_steps), grad_pre)
    grad_out_mine = mine(out_grad).astype(F32)
    grad_up_w = jnp.einsum("td,tf->df", entry_m, grad_pre, preferred_element_type=F32)
    up_steps = scatter_data(grad_up_w)
    up_sent = next(up_steps)
    grad_entry_m = finish(entry_steps, up_sent)
    grad_down_b = jnp.sum(grad_branch_m.astype(F32), axis=0)
    grad_up_b = jnp.sum(grad_pre.astype(F32), axis=0)
    grad_middle = grad_out_mine + norm_back_m(grad_entry_m * (1.0 + scale_m))[0]
    grad_gate_a = grad_middle * branch
    grad_branch_mine = (gate_a * grad_middle).astype(BF16)
    grad_out_b = jnp.sum(grad_branch_mine.astype(F32), axis=0)
    grad_branch = gather_tensor(grad_branch_mine)
    grad_attended = lax.dot_general(
        out_weight, grad_branch, (((0,), (1,)), ((), ())), preferred_element_type=F32
    ).astype(BF16)

    down_steps.send(grad_branch_mine)
    mlp_part = jnp.einsum(
        "tf,df->td",
        after(grad_branch_mine, hidden),
        down_weight,
        preferred_element_type=F32,
    )
    mlp_steps = scatter_tensor(mlp_part)
    next(mlp_steps)

    grad_heads = grad_attended.reshape(heads, HD, rows)

    def delta_of(grad, mixed):
        return jnp.sum(grad.astype(F32) * mixed.astype(F32), axis=1, keepdims=True)

    delta = delta_of(grad_heads, attended)
    side_grads = [shift(grad_heads, "dp", 1), shift(grad_heads, "dp", -1)]
    grad_query, part_keys, part_values = attend_back(
        backward_bounds,
        span,
        query,
        grad_heads,
        logsum,
        delta,
        [sides[0][1], own[1], sides[1][1]],
        [sides[0][2], own[2], sides[1][2]],
        bases,
    )
    mlp_steps.send(grad_heads)
    down_steps.send(grad_query)
    up_steps.send(grad_query)
    branch_m = finish(mlp_steps, grad_query) + down_bias.astype(F32)
    output = (middle + gate_m * branch_m).astype(BF16)
    grad_gate_m = grad_out_mine * branch_m
    grad_out_w = lax.dot_general(
        grad_branch, attended_flat, (((0,), (1,)), ((), ())), preferred_element_type=F32
    )
    grad_keys, grad_values = others_back(
        other_bounds,
        own[1],
        own[2],
        part_keys,
        part_values,
        [spans[0], spans[2]],
        [side[0] for side in sides],
        side_grads,
        side_logsum,
        [delta_of(g, mixed) for g, mixed in zip(side_grads, side_attended)],
    )
    grad_proj = [x.reshape(local_width, rows) for x in (grad_query, grad_keys, grad_values)]
    grad_q_w, grad_k_w, grad_v_w = (
        lax.dot_general(entry, x, (((0,), (1,)), ((), ())), preferred_element_type=F32)
        for x in grad_proj
    )
    early_steps = scatter_data(jnp.concatenate([grad_out_w, grad_q_w], axis=1))
    next(early_steps)
    early_steps.send(grad_keys)
    late_steps = scatter_data(jnp.concatenate([grad_k_w, grad_v_w], axis=1))
    late_sent = next(late_steps)
    grad_proj = after(late_sent, *grad_proj)
    grad_in_b = jnp.stack([jnp.sum(grad_proj[c].astype(F32), axis=1) for c in (0, 2)])
    grad_entry = lax.dot_general(
        in_weight.reshape(width, 3 * local_width),
        jnp.concatenate(grad_proj, axis=0),
        (((1,), (0,)), ((), ())),
        preferred_element_type=F32,
    )
    grad_entry = by_rows(grad_entry)
    scale_turned = lax.dot_general(
        modulation[:, width : 2 * width],
        select,
        (((0,), (1,)), ((), ())),
        preferred_element_type=BF16,
    ).astype(F32)
    scaled = grad_entry * (1.0 + scale_turned)
    input_part = (
        scaled
        - jnp.mean(scaled, axis=0, keepdims=True)
        - normed_turned * jnp.mean(scaled * normed_turned, axis=0, keepdims=True)
    ) * inverse

    split_terms = jnp.concatenate([grad_entry, grad_entry * normed_turned], axis=0)
    kept_terms = jnp.concatenate(
        [grad_gate_a, grad_entry_m, grad_entry_m * normed_m, grad_gate_m], axis=1
    )
    per_latent = jnp.concatenate(
        [onehot_sum(select, split_terms, "tl,mt->lm"), onehot_sum(select_mine, kept_terms, "tl,tm->lm")],
        axis=1,
    )
    columns_here = mod_weight.shape[1]
    arranged = per_latent.reshape(latents, 4, columns_here).transpose(1, 0, 2)

    out_b_row = jnp.pad(grad_out_b, (0, columns_here - width))[None]

    def for_device(flip):
        chosen = lax.dynamic_index_in_dim(arranged, tensor_index ^ flip, 0, keepdims=False)
        return jnp.concatenate([chosen, out_b_row])

    given = [for_device(flip) for flip in range(4)]
    come = [swap(given[flip], "tensor", flip) for flip in (1, 2, 3)]
    placed = lax.dynamic_update_slice_in_dim(
        jnp.zeros((width, rows), F32), grad_middle.T, row_start, 1
    )
    tokens_steps = scatter_tensor(input_part + placed)
    tokens_sent = next(tokens_steps)
    come = after(tokens_sent, *come)
    small = (given[0] + come[0]) + (come[1] + come[2])
    small = jnp.concatenate(
        [small]
        + [
            jnp.pad(value, (0, columns_here - value.shape[0]))[None]
            for value in (grad_in_b.reshape(-1), grad_up_b, grad_down_b)
        ]
    )
    late_sent = late_steps.send(input_part)
    tokens_sent = tokens_steps.send(late_sent)
    for place, bit in enumerate(bits_of("dp")):
        come = swap(small, "dp", bit)
        if place == 0:
            come = after(tokens_sent, come)
        small = small + come
        if place == 0:
            up_steps.send(small)
    grad_mod = small[:latents].astype(BF16)
    sum_out_b = small[latents, :width]
    sum_in_b = small[latents + 1, : 2 * local_width]
    sum_up_b = small[latents + 2, : grad_up_b.shape[0]]
    sum_down_b = small[latents + 3, :width]
    own_width = width // data_size
    own_silu = lax.dynamic_slice_in_dim(silu_cond, data_index * own_width, own_width, 1)
    grad_mod_w = jnp.einsum("ld,lm->dm", own_silu, grad_mod, preferred_element_type=F32)
    grad_mod_b = jnp.sum(grad_mod.astype(F32), axis=0)
    own_count = latents // data_size
    own_grad_mod = lax.dynamic_slice_in_dim(grad_mod, data_index * own_count, own_count, 0)
    own_cond = lax.dynamic_slice_in_dim(cond_full, data_index * own_count, own_count, 0)
    silu_grad = jnp.einsum("lm,dm->ld", own_grad_mod, mod_weight, preferred_element_type=F32)
    cond_part = jax.vjp(jax.nn.silu, own_cond)[1](silu_grad)[0]
    cond_parts = cond_part.reshape(own_count, 4, width // 4).transpose(1, 0, 2)
    grad_cond = lax.dynamic_index_in_dim(cond_parts, tensor_index, 0, keepdims=False)
    for bit in (1, 2, 3):
        grad_cond = grad_cond + swap(
            lax.dynamic_index_in_dim(cond_parts, tensor_index ^ bit, 0, keepdims=False),
            "tensor",
            bit,
        )

    grad_tokens = finish(tokens_steps, grad_mod_w).T
    sum_down_w = finish(down_steps, grad_keys)
    sum_up_w = finish(up_steps, grad_mod_w)
    early = finish(early_steps, grad_mod_w)
    late = finish(late_steps, grad_mod_w)
    sum_out_w = early[:, :local_width]
    sum_in_w = jnp.stack(
        [early[:, local_width:], late[:, :local_width], late[:, local_width:]], axis=1
    )
    return (
        output,
        grad_tokens,
        grad_cond,
        sum_in_w,
        sum_in_b.reshape(2, local_width),
        sum_out_w,
        sum_out_b,
        sum_up_w,
        sum_up_b,
        sum_down_w,
        sum_down_b,
        grad_mod_w,
        grad_mod_b,
    )


def solution(mesh):
    placed = (
        P("dp", None),
        P(),
        P(),
        P(None, None, "tensor"),
        P(None, "tensor"),
        P(None, "tensor"),
        P(),
        P(None, "tensor"),
        P("tensor"),
        P(None, "tensor"),
        P(),
        P(None, "tensor"),
        P("tensor"),
        P("dp", None),
    )
    return jax.shard_map(
        on_device,
        mesh=mesh,
        in_specs=placed,
        out_specs=(
            P(("dp", "tensor"), None),
            P("dp", "tensor"),
            P("dp", "tensor"),
            P("dp", None, "tensor"),
            P(None, "tensor"),
            P("dp", "tensor"),
            P(),
            P("dp", "tensor"),
            P("tensor"),
            P("dp", "tensor"),
            P(),
            P("dp", "tensor"),
            P("tensor"),
        ),
        check_vma=False,
    )
```

```python
import functools
import math

import jax
import jax.numpy as jnp
from jax import lax
from jax.experimental import pallas as pl
from jax.experimental.pallas import tpu as pltpu
from jax.sharding import PartitionSpec as P

HD = 72
FACTOR = HD ** (-0.5)
LOG2E = math.log2(math.e)
NEG = -1e30
BQ = 256
BK = 256
F32 = jnp.float32
BF16 = jnp.bfloat16


def contract(a, b, dims):
    return lax.dot_general(a, b, (dims, ((), ())), preferred_element_type=F32)


def forward_kernel(bases, heads, last, bounds, span, query, mixed_in, top_in, total_in, *refs):
    segments = len(bases)
    keys = refs[:segments]
    values = refs[segments : 2 * segments]
    mixed_out, top_out, total_out, mixed = refs[2 * segments :]
    rows = query.shape[2]
    scale = FACTOR * LOG2E

    def query_block(i, _):
        own = pl.ds(pl.multiple_of(i * BQ, BQ), BQ)
        begin = span[0:1, own]
        end = span[1:2, own]
        for h in range(heads):
            mixed[h] = mixed_in[h, :, own]
        state = tuple(top_in[h, :, own] for h in range(heads)) + tuple(
            total_in[h, :, own] for h in range(heads)
        )
        for s, base in enumerate(bases):

            def key_block(j, state, s=s, base=base):
                k_at = pl.multiple_of(j * BK, BK)
                block = pl.ds(k_at, BK)
                place = lax.broadcasted_iota(jnp.int32, (BK, BQ), 0) + (k_at + base)
                allowed = (place >= begin) & (place < end)
                raws = [
                    contract(keys[s][h, :, block], query[h, :, own], ((0,), (0,)))
                    for h in range(heads)
                ]
                tops, totals, shrinks, lows = [], [], [], []
                for h in range(heads):
                    raw = jnp.where(allowed, raws[h] * scale, NEG)
                    top = jnp.maximum(state[h], jnp.max(raw, axis=0, keepdims=True))
                    probs = jnp.exp2(raw - top)
                    shrink = jnp.exp2(state[h] - top)
                    tops.append(top)
                    totals.append(state[heads + h] * shrink + jnp.sum(probs, axis=0, keepdims=True))
                    shrinks.append(shrink)
                    lows.append(probs.astype(BF16))
                for h in range(heads):
                    mixed[h] = mixed[h] * shrinks[h] + contract(
                        values[s][h, :, block], lows[h], ((1,), (0,))
                    )
                return tuple(tops) + tuple(totals)

            state = lax.fori_loop(bounds[s, 0, i], bounds[s, 1, i], key_block, state)
        for h in range(heads):
            top, total = state[h], state[heads + h]
            if last:
                mixed_out[h, :, own] = (mixed[h] / total).astype(BF16)
                top_out[h, :, own] = top + jnp.log2(total)
            else:
                mixed_out[h, :, own] = mixed[h]
                top_out[h, :, own] = top
            total_out[h, :, own] = total
        return 0

    lax.fori_loop(0, rows // BQ, query_block, 0)


def attend(bounds, span, query, carried, keys, values, bases, last):
    heads, hd, rows = query.shape
    vmem = pl.BlockSpec(memory_space=pltpu.VMEM)
    line = jax.ShapeDtypeStruct((heads, 1, rows), F32)
    return pl.pallas_call(
        functools.partial(forward_kernel, bases, heads, last),
        out_shape=(
            jax.ShapeDtypeStruct((heads, hd, rows), BF16 if last else F32),
            line,
            line,
        ),
        in_specs=[pl.BlockSpec(memory_space=pltpu.SMEM)] + [vmem] * (5 + 2 * len(bases)),
        out_specs=(vmem,) * 3,
        scratch_shapes=[pltpu.VMEM((heads, hd, BQ), F32)],
        compiler_params=pltpu.CompilerParams(vmem_limit_bytes=40 << 20),
        cost_estimate=pl.CostEstimate(flops=1 << 20, bytes_accessed=1 << 20, transcendentals=0),
    )(bounds, span, query, *carried, *keys, *values)


def tile_back(heads, allowed, keys, values, query, grad, logsum, delta):
    scale = FACTOR * LOG2E
    raws = [contract(keys[h], query[h], ((0,), (0,))) for h in range(heads)]
    grads = [contract(values[h], grad[h], ((0,), (0,))) for h in range(heads)]
    found = []
    for h in range(heads):
        raw = jnp.where(allowed, raws[h] * scale - logsum[h], NEG)
        probs = jnp.exp2(raw)
        found.append((probs.astype(BF16), (probs * (grads[h] - delta[h])).astype(BF16)))
    return found


def backward_kernel(bases, heads, bounds, span, query, grad, logsum, delta, *refs):
    segments = len(bases)
    keys = refs[:segments]
    values = refs[segments : 2 * segments]
    grad_query, grad_keys, grad_values, sum_query, sum_keys, sum_values = refs[2 * segments :]
    sum_query[...] = jnp.zeros_like(sum_query)
    for s, base in enumerate(bases):

        def key_block(j, _, s=s, base=base):
            k_at = pl.multiple_of(j * BK, BK)
            block = pl.ds(k_at, BK)
            place = lax.broadcasted_iota(jnp.int32, (BK, BQ), 0) + (k_at + base)
            if base == 0:
                sum_keys[...] = jnp.zeros_like(sum_keys)
                sum_values[...] = jnp.zeros_like(sum_values)

            def query_block(i, _):
                own = pl.ds(pl.multiple_of(i * BQ, BQ), BQ)
                allowed = (place >= span[0:1, own]) & (place < span[1:2, own])
                q = [query[h, :, own] for h in range(heads)]
                g = [grad[h, :, own] for h in range(heads)]
                k = [keys[s][h, :, block] for h in range(heads)]
                found = tile_back(
                    heads,
                    allowed,
                    k,
                    [values[s][h, :, block] for h in range(heads)],
                    q,
                    g,
                    [logsum[h, :, own] for h in range(heads)],
                    [delta[h, :, own] for h in range(heads)],
                )
                for h in range(heads):
                    probs, grad_raw = found[h]
                    if base == 0:
                        sum_values[h] += contract(g[h], probs, ((1,), (1,)))
                        sum_keys[h] += contract(q[h], grad_raw, ((1,), (1,)))
                    sum_query[h, :, own] += contract(k[h], grad_raw, ((1,), (0,)))
                return 0

            lax.fori_loop(bounds[s, 0, j], bounds[s, 1, j], query_block, 0)
            if base == 0:
                for h in range(heads):
                    grad_keys[h, :, block] = sum_keys[h]
                    grad_values[h, :, block] = sum_values[h]
            return 0

        lax.fori_loop(0, keys[s].shape[2] // BK, key_block, 0)
    grad_query[...] = (sum_query[...] * FACTOR).astype(BF16)


def attend_back(bounds, span, query, grad, logsum, delta, keys, values, bases):
    heads, hd, rows = query.shape
    vmem = pl.BlockSpec(memory_space=pltpu.VMEM)
    full = jax.ShapeDtypeStruct((heads, hd, rows), F32)
    return pl.pallas_call(
        functools.partial(backward_kernel, bases, heads),
        out_shape=(jax.ShapeDtypeStruct((heads, hd, rows), BF16), full, full),
        in_specs=[pl.BlockSpec(memory_space=pltpu.SMEM)] + [vmem] * (5 + 2 * len(bases)),
        out_specs=(vmem,) * 3,
        scratch_shapes=[
            pltpu.VMEM((heads, hd, rows), F32),
            pltpu.VMEM((heads, hd, BK), F32),
            pltpu.VMEM((heads, hd, BK), F32),
        ],
        compiler_params=pltpu.CompilerParams(vmem_limit_bytes=44 << 20),
        cost_estimate=pl.CostEstimate(flops=1 << 20, bytes_accessed=1 << 20, transcendentals=0),
    )(bounds, span, query, grad, logsum, delta, *keys, *values)


def others_kernel(segments, heads, bounds, keys, values, keys_in, values_in, *refs):
    spans, query, grad, logsum, delta = (refs[n * segments : (n + 1) * segments] for n in range(5))
    grad_keys, grad_values, sum_keys, sum_values = refs[5 * segments :]

    def key_block(j, _):
        k_at = pl.multiple_of(j * BK, BK)
        block = pl.ds(k_at, BK)
        place = lax.broadcasted_iota(jnp.int32, (BK, BQ), 0) + k_at
        for h in range(heads):
            sum_keys[h] = keys_in[h, :, block]
            sum_values[h] = values_in[h, :, block]
        for s in range(segments):

            def query_block(i, _, s=s):
                own = pl.ds(pl.multiple_of(i * BQ, BQ), BQ)
                allowed = (place >= spans[s][0:1, own]) & (place < spans[s][1:2, own])
                q = [query[s][h, :, own] for h in range(heads)]
                g = [grad[s][h, :, own] for h in range(heads)]
                found = tile_back(
                    heads,
                    allowed,
                    [keys[h, :, block] for h in range(heads)],
                    [values[h, :, block] for h in range(heads)],
                    q,
                    g,
                    [logsum[s][h, :, own] for h in range(heads)],
                    [delta[s][h, :, own] for h in range(heads)],
                )
                for h in range(heads):
                    probs, grad_raw = found[h]
                    sum_values[h] += contract(g[h], probs, ((1,), (1,)))
                    sum_keys[h] += contract(q[h], grad_raw, ((1,), (1,)))
                return 0

            lax.fori_loop(bounds[s, 0, j], bounds[s, 1, j], query_block, 0)
        for h in range(heads):
            grad_keys[h, :, block] = (sum_keys[h] * FACTOR).astype(BF16)
            grad_values[h, :, block] = sum_values[h].astype(BF16)
        return 0

    lax.fori_loop(0, keys.shape[2] // BK, key_block, 0)


def others_back(bounds, keys, values, keys_in, values_in, spans, query, grad, logsum, delta):
    heads, hd, rows = keys.shape
    segments = len(query)
    vmem = pl.BlockSpec(memory_space=pltpu.VMEM)
    shape = jax.ShapeDtypeStruct((heads, hd, rows), BF16)
    return pl.pallas_call(
        functools.partial(others_kernel, segments, heads),
        out_shape=(shape, shape),
        in_specs=[pl.BlockSpec(memory_space=pltpu.SMEM)] + [vmem] * (4 + 5 * segments),
        out_specs=(vmem, vmem),
        scratch_shapes=[pltpu.VMEM((heads, hd, BK), F32), pltpu.VMEM((heads, hd, BK), F32)],
        compiler_params=pltpu.CompilerParams(vmem_limit_bytes=40 << 20),
        cost_estimate=pl.CostEstimate(flops=1 << 20, bytes_accessed=1 << 20, transcendentals=0),
    )(bounds, keys, values, keys_in, values_in, *spans, *query, *grad, *logsum, *delta)


def swap(value, axis, bit):
    return lax.ppermute(value, axis, [(i, i ^ bit) for i in range(lax.axis_size(axis))])


def shift(value, axis, distance):
    devices = range(lax.axis_size(axis))
    return lax.ppermute(value, axis, [(i, i + distance) for i in devices if i + distance in devices])


def bits_of(axis):
    size = lax.axis_size(axis)
    return [1 << b for b in range(size.bit_length() - 1)]


def bit_set(axis, bit):
    return (lax.axis_index(axis) & bit) != 0


def sum_all(value, axis):
    for bit in bits_of(axis):
        value = value + swap(value, axis, bit)
    return value


def after(anchor, *values):
    held = values if anchor is None else lax.optimization_barrier((anchor, *values))[1:]
    return held[0] if len(values) == 1 else held


def in_order(mine, other, upper, dim=0):
    return jnp.where(
        upper, jnp.stack([other, mine], axis=dim), jnp.stack([mine, other], axis=dim)
    )


def gather_tensor(value):
    pair = in_order(value, swap(value, "tensor", 2), bit_set("tensor", 2))
    quad = in_order(pair, swap(pair, "tensor", 1), bit_set("tensor", 1), dim=1)
    return quad.reshape((4 * value.shape[0],) + value.shape[1:])


def scatter_tensor(partial):
    n = partial.shape[0] // 4
    core = lax.axis_index("tensor") % 2
    across = lax.axis_index("tensor") // 2
    parts = partial.astype(BF16).reshape((2, 2, n) + partial.shape[1:])
    kept = lax.dynamic_index_in_dim(parts, core, 1, keepdims=False)
    sent = lax.dynamic_index_in_dim(parts, 1 - core, 1, keepdims=False)
    come = swap(sent, "tensor", 1)
    come = after((yield sent), come)
    half = kept.astype(F32) + come.astype(F32)
    half_low = half.astype(BF16)
    stay = lax.dynamic_index_in_dim(half, across, 0, keepdims=False)
    leave = lax.dynamic_index_in_dim(half_low, 1 - across, 0, keepdims=False)
    come = swap(leave, "tensor", 2)
    come = after((yield leave), come)
    return stay + come.astype(F32)


def scatter_data(partial):
    size = lax.axis_size("dp")
    index = lax.axis_index("dp")
    bits = bits_of("dp")
    count = len(bits)
    rest = (partial.shape[0] // size,) + partial.shape[1:]
    held = partial.astype(BF16).reshape((2,) * count + rest)
    left = list(reversed(bits))
    for bit in [1] + bits[:0:-1]:
        axis = left.index(bit)
        mine = (index // bit) % 2
        kept = lax.dynamic_index_in_dim(held, mine, axis, keepdims=False)
        sent = lax.dynamic_index_in_dim(held, 1 - mine, axis, keepdims=False).astype(BF16)
        come = swap(sent, "dp", bit)
        come = after((yield sent), come)
        held = kept.astype(F32) + come.astype(F32)
        left.remove(bit)
    return held


def finish(steps, anchor=None):
    try:
        while True:
            steps.send(anchor)
    except StopIteration as end:
        return end.value


def layer_norm(value):
    center = value - jnp.mean(value, axis=-1, keepdims=True)
    spread = jnp.mean(center * center, axis=-1, keepdims=True)
    return center * lax.rsqrt(spread + 1e-06)


def gelu_tanh(value):
    return jax.nn.gelu(value, approximate=True)


def onehot_sum(select, values, form):
    upper = values.astype(BF16)
    lower = (values - upper.astype(F32)).astype(BF16)
    first = jnp.einsum(form, select, upper, preferred_element_type=F32)
    return first + jnp.einsum(form, select, lower, preferred_element_type=F32)


def on_device(
    tokens,
    condition,
    latent_lengths,
    in_weight,
    in_bias,
    out_weight,
    out_bias,
    up_weight,
    up_bias,
    down_weight,
    down_bias,
    mod_weight,
    mod_bias,
    out_grad,
):
    rows, width = tokens.shape
    latents = condition.shape[0]
    local_width = in_weight.shape[2]
    heads = local_width // HD
    data_size = lax.axis_size("dp")
    data_index = lax.axis_index("dp")
    tensor_index = lax.axis_index("tensor")
    quarter = rows // 4
    row_start = tensor_index * quarter

    def mine(value):
        return lax.dynamic_slice_in_dim(value, row_start, quarter, 0)

    places = jnp.arange(latents, dtype=jnp.int32)
    earlier = places[None, :] < places[:, None]
    starts = jnp.sum(jnp.where(earlier, latent_lengths[None, :], 0), axis=1)
    ends = starts + latent_lengths
    first_row = data_index * rows
    own_places = first_row + jnp.arange(rows, dtype=jnp.int32)

    def span_of(at):
        inside = (at[:, None] >= starts[None, :]) & (at[:, None] < ends[None, :])
        begin = jnp.sum(jnp.where(inside, starts[None, :] - first_row, 0), axis=1)
        end = jnp.sum(jnp.where(inside, ends[None, :] - first_row, 0), axis=1)
        return begin, end, inside

    bases = (-rows, 0, rows)
    windows = [span_of(own_places + base) for base in bases]
    spans = [jnp.stack(window[:2]) for window in windows]
    selects = [window[2].astype(BF16) for window in windows]
    begin, end = windows[1][:2]
    span, select = spans[1], selects[1]
    select_mine = mine(select)
    forward_bounds, backward_bounds, other_bounds = [], [], []
    for base in bases:
        low = jnp.clip(begin[::BQ] - base, 0, rows) // BK
        high = (jnp.clip(end[BQ - 1 :: BQ] - base, 0, rows) + BK - 1) // BK
        forward_bounds.append(jnp.stack([low, high]))
        key_at = first_row + base + jnp.arange(rows // BK, dtype=jnp.int32) * BK
        low = jnp.clip(span_of(key_at)[0], 0, rows) // BQ
        high = (jnp.clip(span_of(key_at + BK - 1)[1], 0, rows) + BQ - 1) // BQ
        valid = (key_at >= 0) & (key_at < rows * data_size)
        backward_bounds.append(jnp.where(valid[None, :], jnp.stack([low, high]), 0))
        low = jnp.clip(begin[::BK] - base, 0, rows) // BQ
        high = (jnp.clip(end[BK - 1 :: BK] - base, 0, rows) + BQ - 1) // BQ
        other_bounds.append(jnp.stack([low, high]))
    backward_bounds = jnp.stack(backward_bounds)
    other_bounds = jnp.stack([other_bounds[0], other_bounds[2]])

    tokens_mine = mine(tokens)
    behind_tokens = gather_tensor(shift(tokens_mine, "dp", 1))
    ahead_tokens = gather_tensor(shift(tokens_mine, "dp", -1))

    cond_full = condition.astype(F32)
    silu_cond = jax.nn.silu(cond_full).astype(BF16)
    mod_local = (
        jnp.dot(silu_cond, mod_weight, preferred_element_type=F32) + mod_bias.astype(F32)
    ).astype(BF16)
    modulation = gather_tensor(mod_local[None])
    modulation = modulation.transpose(1, 0, 2).reshape(latents, 6 * width)

    def spread(chosen, first, count):
        return jnp.dot(
            chosen,
            modulation[:, first * width : (first + count) * width],
            preferred_element_type=BF16,
        )

    others = spread(select_mine, 2, 4).astype(F32)
    gate_a, shift_m, scale_m, gate_m = (others[:, i * width : (i + 1) * width] for i in range(4))
    gate_m_all = spread(select, 5, 1).astype(F32)

    bias_full = in_bias.astype(F32)
    proj_bias = jnp.stack([bias_full[0], jnp.zeros_like(bias_full[0]), bias_full[1]])

    def entry_of(rows_of, chosen):
        shift_scale = spread(chosen, 0, 2)
        scale = shift_scale[:, width:].astype(F32)
        value = rows_of.astype(F32)
        center = value - jnp.mean(value, axis=-1, keepdims=True)
        inverse = lax.rsqrt(jnp.mean(center * center, axis=-1, keepdims=True) + 1e-06)
        normed = center * inverse
        entry = (normed * (1.0 + scale) + shift_scale[:, :width].astype(F32)).astype(BF16)
        return entry, normed, inverse

    def project(entry):
        found = jnp.einsum("dcf,td->cft", in_weight, entry, preferred_element_type=F32)
        found = (found + proj_bias[:, :, None]).astype(BF16)
        return found.reshape(3, heads, HD, rows)

    entry, normed, inverse = entry_of(tokens, select)
    normed_turned, inverse = normed.T, inverse.T
    own = project(entry)
    sides = [
        project(entry_of(behind_tokens, selects[0])[0]),
        project(entry_of(ahead_tokens, selects[2])[0]),
    ]
    query = own[0]
    line = jnp.zeros((heads, 1, rows), F32)
    carried = attend(
        jnp.stack([forward_bounds[1]]),
        span,
        query,
        (jnp.zeros((heads, HD, rows), F32), line + NEG, line),
        [own[1]],
        [own[2]],
        (0,),
        False,
    )
    attended, logsum, _ = attend(
        jnp.stack([forward_bounds[0], forward_bounds[2]]),
        span,
        query,
        carried,
        [side[1] for side in sides],
        [side[2] for side in sides],
        (-rows, rows),
        True,
    )
    side_attended = [shift(attended, "dp", 1), shift(attended, "dp", -1)]
    side_logsum = [shift(logsum, "dp", 1), shift(logsum, "dp", -1)]
    attended_flat = attended.reshape(local_width, rows)
    attn_part = lax.dot_general(
        attended_flat, out_weight, (((0,), (1,)), ((), ())), preferred_element_type=F32
    )
    attn_steps = scatter_tensor(attn_part)
    next(attn_steps)
    branch = finish(attn_steps) + out_bias.astype(F32)

    middle = tokens_mine.astype(F32) + gate_a * branch
    normed_m, norm_back_m = jax.vjp(layer_norm, middle)
    entry_m = gather_tensor((normed_m * (1.0 + scale_m) + shift_m).astype(BF16))
    hidden_pre = jnp.dot(entry_m, up_weight, preferred_element_type=F32) + up_bias.astype(F32)
    hidden_full, gelu_back = jax.vjp(gelu_tanh, hidden_pre)
    hidden = hidden_full.astype(BF16)
    grad_out = out_grad.astype(F32)
    grad_branch_m = (gate_m_all * grad_out).astype(BF16)
    grad_hidden = jnp.einsum("td,df->tf", grad_branch_m, down_weight, preferred_element_type=F32)
    grad_pre = gelu_back(grad_hidden)[0].astype(BF16)
    grad_down_w = jnp.einsum("td,tf->df", grad_branch_m, hidden, preferred_element_type=F32)
    down_steps = scatter_data(grad_down_w)
    down_sent = next(down_steps)
    grad_pre = after(down_sent, grad_pre)
    entry_part = jnp.einsum("tf,df->td", grad_pre, up_weight, preferred_element_type=F32)
    entry_steps = scatter_tensor(entry_part)
    grad_pre = after(next(entry_steps), grad_pre)
    grad_out_mine = mine(out_grad).astype(F32)
    grad_up_w = jnp.einsum("td,tf->df", entry_m, grad_pre, preferred_element_type=F32)
    up_steps = scatter_data(grad_up_w)
    up_sent = next(up_steps)
    grad_entry_m = finish(entry_steps, up_sent)
    grad_entry_m, *side_attended = after(side_logsum[1], grad_entry_m, *side_attended)
    grad_down_b = jnp.sum(grad_branch_m.astype(F32), axis=0)
    grad_up_b = jnp.sum(grad_pre.astype(F32), axis=0)
    grad_middle = grad_out_mine + norm_back_m(grad_entry_m * (1.0 + scale_m))[0]
    grad_gate_a = grad_middle * branch
    grad_branch_mine = (gate_a * grad_middle).astype(BF16)
    grad_out_b = jnp.sum(grad_branch_mine.astype(F32), axis=0)
    grad_branch = gather_tensor(grad_branch_mine)
    grad_attended = lax.dot_general(
        out_weight, grad_branch, (((0,), (1,)), ((), ())), preferred_element_type=F32
    ).astype(BF16)

    down_steps.send(grad_branch_mine)
    mlp_part = jnp.einsum(
        "tf,df->td",
        after(grad_branch_mine, hidden),
        down_weight,
        preferred_element_type=F32,
    )
    mlp_steps = scatter_tensor(mlp_part)
    next(mlp_steps)

    grad_heads = grad_attended.reshape(heads, HD, rows)

    def delta_of(grad, mixed):
        return jnp.sum(grad.astype(F32) * mixed.astype(F32), axis=1, keepdims=True)

    delta = delta_of(grad_heads, attended)
    side_grads = [shift(grad_heads, "dp", 1), shift(grad_heads, "dp", -1)]
    grad_query, part_keys, part_values = attend_back(
        backward_bounds,
        span,
        query,
        grad_heads,
        logsum,
        delta,
        [sides[0][1], own[1], sides[1][1]],
        [sides[0][2], own[2], sides[1][2]],
        bases,
    )
    mlp_steps.send(grad_heads)
    down_steps.send(grad_query)
    up_steps.send(grad_query)
    branch_m = finish(mlp_steps, grad_query) + down_bias.astype(F32)
    output = (middle + gate_m * branch_m).astype(BF16)
    grad_gate_m = grad_out_mine * branch_m
    grad_out_w = lax.dot_general(
        grad_branch, attended_flat, (((0,), (1,)), ((), ())), preferred_element_type=F32
    )
    grad_keys, grad_values = others_back(
        other_bounds,
        own[1],
        own[2],
        part_keys,
        part_values,
        [spans[0], spans[2]],
        [side[0] for side in sides],
        side_grads,
        side_logsum,
        [delta_of(g, mixed) for g, mixed in zip(side_grads, side_attended)],
    )
    grad_proj = [x.reshape(local_width, rows) for x in (grad_query, grad_keys, grad_values)]
    grad_q_w, grad_k_w, grad_v_w = (
        lax.dot_general(entry, x, (((0,), (1,)), ((), ())), preferred_element_type=F32)
        for x in grad_proj
    )
    early_steps = scatter_data(jnp.concatenate([grad_out_w, grad_q_w], axis=1))
    next(early_steps)
    early_steps.send(grad_keys)
    late_steps = scatter_data(jnp.concatenate([grad_k_w, grad_v_w], axis=1))
    late_sent = next(late_steps)
    grad_proj = after(late_sent, *grad_proj)
    grad_in_b = jnp.stack([jnp.sum(grad_proj[c].astype(F32), axis=1) for c in (0, 2)])
    grad_entry = lax.dot_general(
        in_weight.reshape(width, 3 * local_width),
        jnp.concatenate(grad_proj, axis=0),
        (((1,), (0,)), ((), ())),
        preferred_element_type=F32,
    )

    scale_turned = lax.dot_general(
        modulation[:, width : 2 * width],
        select,
        (((0,), (1,)), ((), ())),
        preferred_element_type=BF16,
    ).astype(F32)
    scaled = grad_entry * (1.0 + scale_turned)
    input_part = (
        scaled
        - jnp.mean(scaled, axis=0, keepdims=True)
        - normed_turned * jnp.mean(scaled * normed_turned, axis=0, keepdims=True)
    ) * inverse

    split_terms = jnp.concatenate([grad_entry, grad_entry * normed_turned], axis=0)
    kept_terms = jnp.concatenate(
        [grad_gate_a, grad_entry_m, grad_entry_m * normed_m, grad_gate_m], axis=1
    )
    per_latent = jnp.concatenate(
        [onehot_sum(select, split_terms, "tl,mt->lm"), onehot_sum(select_mine, kept_terms, "tl,tm->lm")],
        axis=1,
    )
    columns_here = mod_weight.shape[1]
    arranged = per_latent.reshape(latents, 4, columns_here).transpose(1, 0, 2)

    out_b_row = jnp.pad(grad_out_b, (0, columns_here - width))[None]

    def for_device(flip):
        chosen = lax.dynamic_index_in_dim(arranged, tensor_index ^ flip, 0, keepdims=False)
        return jnp.concatenate([chosen, out_b_row])

    given = [for_device(flip) for flip in range(4)]
    come = [swap(given[flip], "tensor", flip) for flip in (1, 2, 3)]
    placed = lax.dynamic_update_slice_in_dim(
        jnp.zeros((width, rows), F32), grad_middle.T, row_start, 1
    )
    tokens_steps = scatter_tensor(input_part + placed)
    tokens_sent = next(tokens_steps)
    come = after(tokens_sent, *come)
    small = (given[0] + come[0]) + (come[1] + come[2])
    small = jnp.concatenate(
        [small]
        + [
            jnp.pad(value, (0, columns_here - value.shape[0]))[None]
            for value in (grad_in_b.reshape(-1), grad_up_b, grad_down_b)
        ]
    )
    late_sent = late_steps.send(input_part)
    tokens_sent = tokens_steps.send(late_sent)
    for place, bit in enumerate(bits_of("dp")):
        come = swap(small, "dp", bit)
        if place == 0:
            come = after(tokens_sent, come)
        small = small + come
        if place == 0:
            up_steps.send(small)
    grad_mod = small[:latents].astype(BF16)
    sum_out_b = small[latents, :width]
    sum_in_b = small[latents + 1, : 2 * local_width]
    sum_up_b = small[latents + 2, : grad_up_b.shape[0]]
    sum_down_b = small[latents + 3, :width]
    own_width = width // data_size
    own_silu = lax.dynamic_slice_in_dim(silu_cond, data_index * own_width, own_width, 1)
    grad_mod_w = jnp.einsum("ld,lm->dm", own_silu, grad_mod, preferred_element_type=F32)
    grad_mod_b = jnp.sum(grad_mod.astype(F32), axis=0)
    own_count = latents // data_size
    own_grad_mod = lax.dynamic_slice_in_dim(grad_mod, data_index * own_count, own_count, 0)
    own_cond = lax.dynamic_slice_in_dim(cond_full, data_index * own_count, own_count, 0)
    silu_grad = jnp.einsum("lm,dm->ld", own_grad_mod, mod_weight, preferred_element_type=F32)
    cond_part = jax.vjp(jax.nn.silu, own_cond)[1](silu_grad)[0]
    cond_parts = cond_part.reshape(own_count, 4, width // 4).transpose(1, 0, 2)
    grad_cond = lax.dynamic_index_in_dim(cond_parts, tensor_index, 0, keepdims=False)
    for bit in (1, 2, 3):
        grad_cond = grad_cond + swap(
            lax.dynamic_index_in_dim(cond_parts, tensor_index ^ bit, 0, keepdims=False),
            "tensor",
            bit,
        )

    grad_tokens = finish(tokens_steps, grad_mod_w).T
    sum_down_w = finish(down_steps, grad_keys)
    sum_up_w = finish(up_steps, grad_mod_w)
    early = finish(early_steps, grad_mod_w)
    late = finish(late_steps, grad_mod_w)
    sum_out_w = early[:, :local_width]
    sum_in_w = jnp.stack(
        [early[:, local_width:], late[:, :local_width], late[:, local_width:]], axis=1
    )
    return (
        output,
        grad_tokens,
        grad_cond,
        sum_in_w,
        sum_in_b.reshape(2, local_width),
        sum_out_w,
        sum_out_b,
        sum_up_w,
        sum_up_b,
        sum_down_w,
        sum_down_b,
        grad_mod_w,
        grad_mod_b,
    )


def solution(mesh):
    placed = (
        P("dp", None),
        P(),
        P(),
        P(None, None, "tensor"),
        P(None, "tensor"),
        P(None, "tensor"),
        P(),
        P(None, "tensor"),
        P("tensor"),
        P(None, "tensor"),
        P(),
        P(None, "tensor"),
        P("tensor"),
        P("dp", None),
    )
    return jax.shard_map(
        on_device,
        mesh=mesh,
        in_specs=placed,
        out_specs=(
            P(("dp", "tensor"), None),
            P("dp", "tensor"),
            P("dp", "tensor"),
            P("dp", None, "tensor"),
            P(None, "tensor"),
            P("dp", "tensor"),
            P(),
            P("dp", "tensor"),
            P("tensor"),
            P("dp", "tensor"),
            P(),
            P("dp", "tensor"),
            P("tensor"),
        ),
        check_vma=False,
    )
```

```python
import functools
import math

import jax
import jax.numpy as jnp
from jax import lax
from jax.experimental import pallas as pl
from jax.experimental.pallas import tpu as pltpu
from jax.sharding import PartitionSpec as P

HD = 72
FACTOR = HD ** (-0.5)
LOG2E = math.log2(math.e)
NEG = -1e30
BQ = 256
BK = 256
F32 = jnp.float32
BF16 = jnp.bfloat16


def contract(a, b, dims):
    return lax.dot_general(a, b, (dims, ((), ())), preferred_element_type=F32)


def forward_kernel(bases, heads, last, bounds, span, query, mixed_in, top_in, total_in, *refs):
    segments = len(bases)
    keys = refs[:segments]
    values = refs[segments : 2 * segments]
    mixed_out, top_out, total_out, mixed = refs[2 * segments :]
    rows = query.shape[2]
    scale = FACTOR * LOG2E

    def query_block(i, _):
        own = pl.ds(pl.multiple_of(i * BQ, BQ), BQ)
        begin = span[0:1, own]
        end = span[1:2, own]
        for h in range(heads):
            mixed[h] = mixed_in[h, :, own]
        state = tuple(top_in[h, :, own] for h in range(heads)) + tuple(
            total_in[h, :, own] for h in range(heads)
        )
        for s, base in enumerate(bases):

            def key_block(j, state, s=s, base=base):
                k_at = pl.multiple_of(j * BK, BK)
                block = pl.ds(k_at, BK)
                place = lax.broadcasted_iota(jnp.int32, (BK, BQ), 0) + (k_at + base)
                allowed = (place >= begin) & (place < end)
                raws = [
                    contract(keys[s][h, :, block], query[h, :, own], ((0,), (0,)))
                    for h in range(heads)
                ]
                tops, totals, shrinks, lows = [], [], [], []
                for h in range(heads):
                    raw = jnp.where(allowed, raws[h] * scale, NEG)
                    top = jnp.maximum(state[h], jnp.max(raw, axis=0, keepdims=True))
                    probs = jnp.exp2(raw - top)
                    shrink = jnp.exp2(state[h] - top)
                    tops.append(top)
                    totals.append(state[heads + h] * shrink + jnp.sum(probs, axis=0, keepdims=True))
                    shrinks.append(shrink)
                    lows.append(probs.astype(BF16))
                for h in range(heads):
                    mixed[h] = mixed[h] * shrinks[h] + contract(
                        values[s][h, :, block], lows[h], ((1,), (0,))
                    )
                return tuple(tops) + tuple(totals)

            state = lax.fori_loop(bounds[s, 0, i], bounds[s, 1, i], key_block, state)
        for h in range(heads):
            top, total = state[h], state[heads + h]
            if last:
                mixed_out[h, :, own] = (mixed[h] / total).astype(BF16)
                top_out[h, :, own] = top + jnp.log2(total)
            else:
                mixed_out[h, :, own] = mixed[h]
                top_out[h, :, own] = top
            total_out[h, :, own] = total
        return 0

    lax.fori_loop(0, rows // BQ, query_block, 0)


def attend(bounds, span, query, carried, keys, values, bases, last):
    heads, hd, rows = query.shape
    vmem = pl.BlockSpec(memory_space=pltpu.VMEM)
    line = jax.ShapeDtypeStruct((heads, 1, rows), F32)
    return pl.pallas_call(
        functools.partial(forward_kernel, bases, heads, last),
        out_shape=(
            jax.ShapeDtypeStruct((heads, hd, rows), BF16 if last else F32),
            line,
            line,
        ),
        in_specs=[pl.BlockSpec(memory_space=pltpu.SMEM)] + [vmem] * (5 + 2 * len(bases)),
        out_specs=(vmem,) * 3,
        scratch_shapes=[pltpu.VMEM((heads, hd, BQ), F32)],
        compiler_params=pltpu.CompilerParams(vmem_limit_bytes=40 << 20),
        cost_estimate=pl.CostEstimate(flops=1 << 20, bytes_accessed=1 << 20, transcendentals=0),
    )(bounds, span, query, *carried, *keys, *values)


def tile_back(heads, allowed, keys, values, query, grad, logsum, delta):
    scale = FACTOR * LOG2E
    raws = [contract(keys[h], query[h], ((0,), (0,))) for h in range(heads)]
    grads = [contract(values[h], grad[h], ((0,), (0,))) for h in range(heads)]
    found = []
    for h in range(heads):
        raw = jnp.where(allowed, raws[h] * scale - logsum[h], NEG)
        probs = jnp.exp2(raw)
        found.append((probs.astype(BF16), (probs * (grads[h] - delta[h])).astype(BF16)))
    return found


def backward_kernel(bases, heads, bounds, span, query, grad, logsum, delta, *refs):
    segments = len(bases)
    keys = refs[:segments]
    values = refs[segments : 2 * segments]
    grad_query, grad_keys, grad_values, sum_query, sum_keys, sum_values = refs[2 * segments :]
    sum_query[...] = jnp.zeros_like(sum_query)
    for s, base in enumerate(bases):

        def key_block(j, _, s=s, base=base):
            k_at = pl.multiple_of(j * BK, BK)
            block = pl.ds(k_at, BK)
            place = lax.broadcasted_iota(jnp.int32, (BK, BQ), 0) + (k_at + base)
            if base == 0:
                sum_keys[...] = jnp.zeros_like(sum_keys)
                sum_values[...] = jnp.zeros_like(sum_values)

            def query_block(i, _):
                own = pl.ds(pl.multiple_of(i * BQ, BQ), BQ)
                allowed = (place >= span[0:1, own]) & (place < span[1:2, own])
                q = [query[h, :, own] for h in range(heads)]
                g = [grad[h, :, own] for h in range(heads)]
                k = [keys[s][h, :, block] for h in range(heads)]
                found = tile_back(
                    heads,
                    allowed,
                    k,
                    [values[s][h, :, block] for h in range(heads)],
                    q,
                    g,
                    [logsum[h, :, own] for h in range(heads)],
                    [delta[h, :, own] for h in range(heads)],
                )
                for h in range(heads):
                    probs, grad_raw = found[h]
                    if base == 0:
                        sum_values[h] += contract(g[h], probs, ((1,), (1,)))
                        sum_keys[h] += contract(q[h], grad_raw, ((1,), (1,)))
                    sum_query[h, :, own] += contract(k[h], grad_raw, ((1,), (0,)))
                return 0

            lax.fori_loop(bounds[s, 0, j], bounds[s, 1, j], query_block, 0)
            if base == 0:
                for h in range(heads):
                    grad_keys[h, :, block] = sum_keys[h]
                    grad_values[h, :, block] = sum_values[h]
            return 0

        lax.fori_loop(0, keys[s].shape[2] // BK, key_block, 0)
    grad_query[...] = (sum_query[...] * FACTOR).astype(BF16)


def attend_back(bounds, span, query, grad, logsum, delta, keys, values, bases):
    heads, hd, rows = query.shape
    vmem = pl.BlockSpec(memory_space=pltpu.VMEM)
    full = jax.ShapeDtypeStruct((heads, hd, rows), F32)
    return pl.pallas_call(
        functools.partial(backward_kernel, bases, heads),
        out_shape=(jax.ShapeDtypeStruct((heads, hd, rows), BF16), full, full),
        in_specs=[pl.BlockSpec(memory_space=pltpu.SMEM)] + [vmem] * (5 + 2 * len(bases)),
        out_specs=(vmem,) * 3,
        scratch_shapes=[
            pltpu.VMEM((heads, hd, rows), F32),
            pltpu.VMEM((heads, hd, BK), F32),
            pltpu.VMEM((heads, hd, BK), F32),
        ],
        compiler_params=pltpu.CompilerParams(vmem_limit_bytes=44 << 20),
        cost_estimate=pl.CostEstimate(flops=1 << 20, bytes_accessed=1 << 20, transcendentals=0),
    )(bounds, span, query, grad, logsum, delta, *keys, *values)


def others_kernel(segments, heads, bounds, keys, values, keys_in, values_in, *refs):
    spans, query, grad, logsum, delta = (refs[n * segments : (n + 1) * segments] for n in range(5))
    grad_keys, grad_values, sum_keys, sum_values = refs[5 * segments :]

    def key_block(j, _):
        k_at = pl.multiple_of(j * BK, BK)
        block = pl.ds(k_at, BK)
        place = lax.broadcasted_iota(jnp.int32, (BK, BQ), 0) + k_at
        for h in range(heads):
            sum_keys[h] = keys_in[h, :, block]
            sum_values[h] = values_in[h, :, block]
        for s in range(segments):

            def query_block(i, _, s=s):
                own = pl.ds(pl.multiple_of(i * BQ, BQ), BQ)
                allowed = (place >= spans[s][0:1, own]) & (place < spans[s][1:2, own])
                q = [query[s][h, :, own] for h in range(heads)]
                g = [grad[s][h, :, own] for h in range(heads)]
                found = tile_back(
                    heads,
                    allowed,
                    [keys[h, :, block] for h in range(heads)],
                    [values[h, :, block] for h in range(heads)],
                    q,
                    g,
                    [logsum[s][h, :, own] for h in range(heads)],
                    [delta[s][h, :, own] for h in range(heads)],
                )
                for h in range(heads):
                    probs, grad_raw = found[h]
                    sum_values[h] += contract(g[h], probs, ((1,), (1,)))
                    sum_keys[h] += contract(q[h], grad_raw, ((1,), (1,)))
                return 0

            lax.fori_loop(bounds[s, 0, j], bounds[s, 1, j], query_block, 0)
        for h in range(heads):
            grad_keys[h, :, block] = (sum_keys[h] * FACTOR).astype(BF16)
            grad_values[h, :, block] = sum_values[h].astype(BF16)
        return 0

    lax.fori_loop(0, keys.shape[2] // BK, key_block, 0)


def others_back(bounds, keys, values, keys_in, values_in, spans, query, grad, logsum, delta):
    heads, hd, rows = keys.shape
    segments = len(query)
    vmem = pl.BlockSpec(memory_space=pltpu.VMEM)
    shape = jax.ShapeDtypeStruct((heads, hd, rows), BF16)
    return pl.pallas_call(
        functools.partial(others_kernel, segments, heads),
        out_shape=(shape, shape),
        in_specs=[pl.BlockSpec(memory_space=pltpu.SMEM)] + [vmem] * (4 + 5 * segments),
        out_specs=(vmem, vmem),
        scratch_shapes=[pltpu.VMEM((heads, hd, BK), F32), pltpu.VMEM((heads, hd, BK), F32)],
        compiler_params=pltpu.CompilerParams(vmem_limit_bytes=40 << 20),
        cost_estimate=pl.CostEstimate(flops=1 << 20, bytes_accessed=1 << 20, transcendentals=0),
    )(bounds, keys, values, keys_in, values_in, *spans, *query, *grad, *logsum, *delta)


def swap(value, axis, bit):
    return lax.ppermute(value, axis, [(i, i ^ bit) for i in range(lax.axis_size(axis))])


def shift(value, axis, distance):
    devices = range(lax.axis_size(axis))
    return lax.ppermute(value, axis, [(i, i + distance) for i in devices if i + distance in devices])


def bits_of(axis):
    size = lax.axis_size(axis)
    return [1 << b for b in range(size.bit_length() - 1)]


def bit_set(axis, bit):
    return (lax.axis_index(axis) & bit) != 0


def sum_all(value, axis):
    for bit in bits_of(axis):
        value = value + swap(value, axis, bit)
    return value


def after(anchor, *values):
    held = values if anchor is None else lax.optimization_barrier((anchor, *values))[1:]
    return held[0] if len(values) == 1 else held


def in_order(mine, other, upper, dim=0):
    return jnp.where(
        upper, jnp.stack([other, mine], axis=dim), jnp.stack([mine, other], axis=dim)
    )


def gather_tensor(value):
    pair = in_order(value, swap(value, "tensor", 2), bit_set("tensor", 2))
    quad = in_order(pair, swap(pair, "tensor", 1), bit_set("tensor", 1), dim=1)
    return quad.reshape((4 * value.shape[0],) + value.shape[1:])


def scatter_tensor(partial):
    n = partial.shape[0] // 4
    core = lax.axis_index("tensor") % 2
    across = lax.axis_index("tensor") // 2
    parts = partial.astype(BF16).reshape((2, 2, n) + partial.shape[1:])
    kept = lax.dynamic_index_in_dim(parts, core, 1, keepdims=False)
    sent = lax.dynamic_index_in_dim(parts, 1 - core, 1, keepdims=False)
    come = swap(sent, "tensor", 1)
    come = after((yield sent), come)
    half = kept.astype(F32) + come.astype(F32)
    half_low = half.astype(BF16)
    stay = lax.dynamic_index_in_dim(half, across, 0, keepdims=False)
    leave = lax.dynamic_index_in_dim(half_low, 1 - across, 0, keepdims=False)
    come = swap(leave, "tensor", 2)
    come = after((yield leave), come)
    return stay + come.astype(F32)


def scatter_data(partials):
    joined = jnp.concatenate([partial.astype(BF16) for partial in partials], axis=1)
    found = lax.psum_scatter(joined, "dp", scatter_dimension=0, tiled=True).astype(F32)
    cuts, at = [], 0
    for partial in partials[:-1]:
        at += partial.shape[1]
        cuts.append(at)
    return jnp.split(found, cuts, axis=1)


def finish(steps, anchor=None):
    try:
        while True:
            steps.send(anchor)
    except StopIteration as end:
        return end.value


def layer_norm(value):
    center = value - jnp.mean(value, axis=-1, keepdims=True)
    spread = jnp.mean(center * center, axis=-1, keepdims=True)
    return center * lax.rsqrt(spread + 1e-06)


def gelu_tanh(value):
    return jax.nn.gelu(value, approximate=True)


def onehot_sum(select, values, form):
    upper = values.astype(BF16)
    lower = (values - upper.astype(F32)).astype(BF16)
    first = jnp.einsum(form, select, upper, preferred_element_type=F32)
    return first + jnp.einsum(form, select, lower, preferred_element_type=F32)


def on_device(
    tokens,
    condition,
    latent_lengths,
    in_weight,
    in_bias,
    out_weight,
    out_bias,
    up_weight,
    up_bias,
    down_weight,
    down_bias,
    mod_weight,
    mod_bias,
    out_grad,
):
    rows, width = tokens.shape
    latents = condition.shape[0]
    local_width = in_weight.shape[2]
    heads = local_width // HD
    data_size = lax.axis_size("dp")
    data_index = lax.axis_index("dp")
    tensor_index = lax.axis_index("tensor")
    quarter = rows // 4
    row_start = tensor_index * quarter

    def mine(value):
        return lax.dynamic_slice_in_dim(value, row_start, quarter, 0)

    places = jnp.arange(latents, dtype=jnp.int32)
    earlier = places[None, :] < places[:, None]
    starts = jnp.sum(jnp.where(earlier, latent_lengths[None, :], 0), axis=1)
    ends = starts + latent_lengths
    first_row = data_index * rows
    own_places = first_row + jnp.arange(rows, dtype=jnp.int32)

    def span_of(at):
        inside = (at[:, None] >= starts[None, :]) & (at[:, None] < ends[None, :])
        begin = jnp.sum(jnp.where(inside, starts[None, :] - first_row, 0), axis=1)
        end = jnp.sum(jnp.where(inside, ends[None, :] - first_row, 0), axis=1)
        return begin, end, inside

    bases = (-rows, 0, rows)
    windows = [span_of(own_places + base) for base in bases]
    spans = [jnp.stack(window[:2]) for window in windows]
    selects = [window[2].astype(BF16) for window in windows]
    begin, end = windows[1][:2]
    span, select = spans[1], selects[1]
    select_mine = mine(select)
    forward_bounds, backward_bounds, other_bounds = [], [], []
    for base in bases:
        low = jnp.clip(begin[::BQ] - base, 0, rows) // BK
        high = (jnp.clip(end[BQ - 1 :: BQ] - base, 0, rows) + BK - 1) // BK
        forward_bounds.append(jnp.stack([low, high]))
        key_at = first_row + base + jnp.arange(rows // BK, dtype=jnp.int32) * BK
        low = jnp.clip(span_of(key_at)[0], 0, rows) // BQ
        high = (jnp.clip(span_of(key_at + BK - 1)[1], 0, rows) + BQ - 1) // BQ
        valid = (key_at >= 0) & (key_at < rows * data_size)
        backward_bounds.append(jnp.where(valid[None, :], jnp.stack([low, high]), 0))
        low = jnp.clip(begin[::BK] - base, 0, rows) // BQ
        high = (jnp.clip(end[BK - 1 :: BK] - base, 0, rows) + BQ - 1) // BQ
        other_bounds.append(jnp.stack([low, high]))
    backward_bounds = jnp.stack(backward_bounds)
    other_bounds = jnp.stack([other_bounds[0], other_bounds[2]])

    tokens_mine = mine(tokens)
    behind_tokens = gather_tensor(shift(tokens_mine, "dp", 1))
    ahead_tokens = gather_tensor(shift(tokens_mine, "dp", -1))

    cond_full = condition.astype(F32)
    silu_cond = jax.nn.silu(cond_full).astype(BF16)
    mod_local = (
        jnp.dot(silu_cond, mod_weight, preferred_element_type=F32) + mod_bias.astype(F32)
    ).astype(BF16)
    modulation = gather_tensor(mod_local[None])
    modulation = modulation.transpose(1, 0, 2).reshape(latents, 6 * width)

    def spread(chosen, first, count):
        return jnp.dot(
            chosen,
            modulation[:, first * width : (first + count) * width],
            preferred_element_type=BF16,
        )

    others = spread(select_mine, 2, 4).astype(F32)
    gate_a, shift_m, scale_m, gate_m = (others[:, i * width : (i + 1) * width] for i in range(4))
    gate_m_all = spread(select, 5, 1).astype(F32)

    bias_full = in_bias.astype(F32)
    proj_bias = jnp.stack([bias_full[0], jnp.zeros_like(bias_full[0]), bias_full[1]])

    def entry_of(rows_of, chosen):
        shift_scale = spread(chosen, 0, 2)
        scale = shift_scale[:, width:].astype(F32)
        value = rows_of.astype(F32)
        center = value - jnp.mean(value, axis=-1, keepdims=True)
        inverse = lax.rsqrt(jnp.mean(center * center, axis=-1, keepdims=True) + 1e-06)
        normed = center * inverse
        entry = (normed * (1.0 + scale) + shift_scale[:, :width].astype(F32)).astype(BF16)
        return entry, normed, inverse

    def project(entry):
        found = jnp.einsum("dcf,td->cft", in_weight, entry, preferred_element_type=F32)
        found = (found + proj_bias[:, :, None]).astype(BF16)
        return found.reshape(3, heads, HD, rows)

    entry, normed, inverse = entry_of(tokens, select)
    normed_turned, inverse = normed.T, inverse.T
    own = project(entry)
    sides = [
        project(entry_of(behind_tokens, selects[0])[0]),
        project(entry_of(ahead_tokens, selects[2])[0]),
    ]
    query = own[0]
    line = jnp.zeros((heads, 1, rows), F32)
    carried = attend(
        jnp.stack([forward_bounds[1]]),
        span,
        query,
        (jnp.zeros((heads, HD, rows), F32), line + NEG, line),
        [own[1]],
        [own[2]],
        (0,),
        False,
    )
    attended, logsum, _ = attend(
        jnp.stack([forward_bounds[0], forward_bounds[2]]),
        span,
        query,
        carried,
        [side[1] for side in sides],
        [side[2] for side in sides],
        (-rows, rows),
        True,
    )
    attended_flat = attended.reshape(local_width, rows)
    attn_part = lax.dot_general(
        attended_flat, out_weight, (((0,), (1,)), ((), ())), preferred_element_type=F32
    )
    attn_steps = scatter_tensor(attn_part)
    next(attn_steps)
    branch = finish(attn_steps) + out_bias.astype(F32)

    middle = tokens_mine.astype(F32) + gate_a * branch
    normed_m, norm_back_m = jax.vjp(layer_norm, middle)
    entry_m = gather_tensor((normed_m * (1.0 + scale_m) + shift_m).astype(BF16))
    hidden_pre = jnp.dot(entry_m, up_weight, preferred_element_type=F32) + up_bias.astype(F32)
    hidden_full, gelu_back = jax.vjp(gelu_tanh, hidden_pre)
    hidden = hidden_full.astype(BF16)
    grad_out = out_grad.astype(F32)
    grad_branch_m = (gate_m_all * grad_out).astype(BF16)
    grad_hidden = jnp.einsum("td,df->tf", grad_branch_m, down_weight, preferred_element_type=F32)
    grad_pre = gelu_back(grad_hidden)[0].astype(BF16)
    grad_down_w = jnp.einsum("td,tf->df", grad_branch_m, hidden, preferred_element_type=F32)
    entry_part = jnp.einsum("tf,df->td", grad_pre, up_weight, preferred_element_type=F32)
    entry_steps = scatter_tensor(entry_part)
    grad_pre = after(next(entry_steps), grad_pre)
    grad_out_mine = mine(out_grad).astype(F32)
    grad_up_w = jnp.einsum("td,tf->df", entry_m, grad_pre, preferred_element_type=F32)
    sum_down_w, sum_up_w = scatter_data([grad_down_w, grad_up_w])
    grad_entry_m = finish(entry_steps)
    grad_down_b = jnp.sum(grad_branch_m.astype(F32), axis=0)
    grad_up_b = jnp.sum(grad_pre.astype(F32), axis=0)
    grad_middle = grad_out_mine + norm_back_m(grad_entry_m * (1.0 + scale_m))[0]
    grad_gate_a = grad_middle * branch
    grad_branch_mine = (gate_a * grad_middle).astype(BF16)
    grad_out_b = jnp.sum(grad_branch_mine.astype(F32), axis=0)
    grad_branch = gather_tensor(grad_branch_mine)
    grad_attended = lax.dot_general(
        out_weight, grad_branch, (((0,), (1,)), ((), ())), preferred_element_type=F32
    ).astype(BF16)

    mlp_part = jnp.einsum(
        "tf,df->td",
        after(grad_branch_mine, hidden),
        down_weight,
        preferred_element_type=F32,
    )
    mlp_steps = scatter_tensor(mlp_part)
    next(mlp_steps)

    grad_heads = grad_attended.reshape(heads, HD, rows)
    delta = jnp.sum(grad_heads.astype(F32) * attended.astype(F32), axis=1, keepdims=True)
    stats = jnp.stack([logsum, delta])
    side_grads = [shift(grad_heads, "dp", 1), shift(grad_heads, "dp", -1)]
    side_stats = [shift(stats, "dp", 1), shift(stats, "dp", -1)]
    grad_query, part_keys, part_values = attend_back(
        backward_bounds,
        span,
        query,
        grad_heads,
        logsum,
        delta,
        [sides[0][1], own[1], sides[1][1]],
        [sides[0][2], own[2], sides[1][2]],
        bases,
    )
    mlp_steps.send(grad_heads)
    branch_m = finish(mlp_steps, grad_query) + down_bias.astype(F32)
    output = (middle + gate_m * branch_m).astype(BF16)
    grad_gate_m = grad_out_mine * branch_m
    grad_out_w = lax.dot_general(
        grad_branch, attended_flat, (((0,), (1,)), ((), ())), preferred_element_type=F32
    )
    grad_keys, grad_values = others_back(
        other_bounds,
        own[1],
        own[2],
        part_keys,
        part_values,
        [spans[0], spans[2]],
        [side[0] for side in sides],
        side_grads,
        [side[0] for side in side_stats],
        [side[1] for side in side_stats],
    )
    grad_proj = [x.reshape(local_width, rows) for x in (grad_query, grad_keys, grad_values)]
    grad_q_w, grad_k_w, grad_v_w = (
        lax.dot_general(entry, x, (((0,), (1,)), ((), ())), preferred_element_type=F32)
        for x in grad_proj
    )
    sum_out_w, sum_q_w = scatter_data([grad_out_w, grad_q_w])
    sum_k_w, sum_v_w = scatter_data([grad_k_w, grad_v_w])
    grad_proj = after((grad_k_w, grad_v_w), *grad_proj)
    grad_in_b = jnp.stack([jnp.sum(grad_proj[c].astype(F32), axis=1) for c in (0, 2)])
    grad_entry = lax.dot_general(
        in_weight.reshape(width, 3 * local_width),
        jnp.concatenate(grad_proj, axis=0),
        (((1,), (0,)), ((), ())),
        preferred_element_type=F32,
    )

    scale_turned = lax.dot_general(
        modulation[:, width : 2 * width],
        select,
        (((0,), (1,)), ((), ())),
        preferred_element_type=BF16,
    ).astype(F32)
    scaled = grad_entry * (1.0 + scale_turned)
    input_part = (
        scaled
        - jnp.mean(scaled, axis=0, keepdims=True)
        - normed_turned * jnp.mean(scaled * normed_turned, axis=0, keepdims=True)
    ) * inverse

    split_terms = jnp.concatenate([grad_entry, grad_entry * normed_turned], axis=0)
    kept_terms = jnp.concatenate(
        [grad_gate_a, grad_entry_m, grad_entry_m * normed_m, grad_gate_m], axis=1
    )
    per_latent = jnp.concatenate(
        [onehot_sum(select, split_terms, "tl,mt->lm"), onehot_sum(select_mine, kept_terms, "tl,tm->lm")],
        axis=1,
    )
    columns_here = mod_weight.shape[1]
    arranged = per_latent.reshape(latents, 4, columns_here).transpose(1, 0, 2)

    out_b_row = jnp.pad(grad_out_b, (0, columns_here - width))[None]

    def for_device(flip):
        chosen = lax.dynamic_index_in_dim(arranged, tensor_index ^ flip, 0, keepdims=False)
        return jnp.concatenate([chosen, out_b_row])

    given = [for_device(flip) for flip in range(4)]
    come = [swap(given[flip], "tensor", flip) for flip in (1, 2, 3)]
    placed = lax.dynamic_update_slice_in_dim(
        jnp.zeros((width, rows), F32), grad_middle.T, row_start, 1
    )
    tokens_steps = scatter_tensor(input_part + placed)
    tokens_sent = next(tokens_steps)
    come = after(tokens_sent, *come)
    small = (given[0] + come[0]) + (come[1] + come[2])
    small = jnp.concatenate(
        [small]
        + [
            jnp.pad(value, (0, columns_here - value.shape[0]))[None]
            for value in (grad_in_b.reshape(-1), grad_up_b, grad_down_b)
        ]
    )
    tokens_sent = tokens_steps.send(small)
    for place, bit in enumerate(bits_of("dp")):
        come = swap(small, "dp", bit)
        if place == 0:
            come = after(tokens_sent, come)
        small = small + come
    grad_mod = small[:latents].astype(BF16)
    sum_out_b = small[latents, :width]
    sum_in_b = small[latents + 1, : 2 * local_width]
    sum_up_b = small[latents + 2, : grad_up_b.shape[0]]
    sum_down_b = small[latents + 3, :width]
    own_width = width // data_size
    own_silu = lax.dynamic_slice_in_dim(silu_cond, data_index * own_width, own_width, 1)
    grad_mod_w = jnp.einsum("ld,lm->dm", own_silu, grad_mod, preferred_element_type=F32)
    grad_mod_b = jnp.sum(grad_mod.astype(F32), axis=0)
    own_count = latents // data_size
    own_grad_mod = lax.dynamic_slice_in_dim(grad_mod, data_index * own_count, own_count, 0)
    own_cond = lax.dynamic_slice_in_dim(cond_full, data_index * own_count, own_count, 0)
    silu_grad = jnp.einsum("lm,dm->ld", own_grad_mod, mod_weight, preferred_element_type=F32)
    cond_part = jax.vjp(jax.nn.silu, own_cond)[1](silu_grad)[0]
    cond_parts = cond_part.reshape(own_count, 4, width // 4).transpose(1, 0, 2)
    grad_cond = lax.dynamic_index_in_dim(cond_parts, tensor_index, 0, keepdims=False)
    for bit in (1, 2, 3):
        grad_cond = grad_cond + swap(
            lax.dynamic_index_in_dim(cond_parts, tensor_index ^ bit, 0, keepdims=False),
            "tensor",
            bit,
        )

    grad_tokens = finish(tokens_steps, grad_mod_w).T
    sum_in_w = jnp.stack([sum_q_w, sum_k_w, sum_v_w], axis=1)
    return (
        output,
        grad_tokens,
        grad_cond,
        sum_in_w,
        sum_in_b.reshape(2, local_width),
        sum_out_w,
        sum_out_b,
        sum_up_w,
        sum_up_b,
        sum_down_w,
        sum_down_b,
        grad_mod_w,
        grad_mod_b,
    )


def solution(mesh):
    placed = (
        P("dp", None),
        P(),
        P(),
        P(None, None, "tensor"),
        P(None, "tensor"),
        P(None, "tensor"),
        P(),
        P(None, "tensor"),
        P("tensor"),
        P(None, "tensor"),
        P(),
        P(None, "tensor"),
        P("tensor"),
        P("dp", None),
    )
    return jax.shard_map(
        on_device,
        mesh=mesh,
        in_specs=placed,
        out_specs=(
            P(("dp", "tensor"), None),
            P("dp", "tensor"),
            P("dp", "tensor"),
            P("dp", None, "tensor"),
            P(None, "tensor"),
            P("dp", "tensor"),
            P(),
            P("dp", "tensor"),
            P("tensor"),
            P("dp", "tensor"),
            P(),
            P("dp", "tensor"),
            P("tensor"),
        ),
        check_vma=False,
    )
```

```python
import functools
import math

import jax
import jax.numpy as jnp
from jax import lax
from jax.experimental import pallas as pl
from jax.experimental.pallas import tpu as pltpu
from jax.sharding import PartitionSpec as P

HD = 72
FACTOR = HD ** (-0.5)
LOG2E = math.log2(math.e)
NEG = -1e30
BQ = 256
BK = 256
COST = pl.CostEstimate(flops=18 << 30, bytes_accessed=24 << 20, transcendentals=1 << 22)
F32 = jnp.float32
BF16 = jnp.bfloat16


def contract(a, b, dims):
    return lax.dot_general(a, b, (dims, ((), ())), preferred_element_type=F32)


def forward_kernel(bases, heads, last, bounds, span, query, mixed_in, top_in, total_in, *refs):
    segments = len(bases)
    keys = refs[:segments]
    values = refs[segments : 2 * segments]
    mixed_out, top_out, total_out, mixed = refs[2 * segments :]
    rows = query.shape[2]
    scale = FACTOR * LOG2E

    def query_block(i, _):
        own = pl.ds(pl.multiple_of(i * BQ, BQ), BQ)
        begin = span[0:1, own]
        end = span[1:2, own]
        for h in range(heads):
            mixed[h] = mixed_in[h, :, own]
        state = tuple(top_in[h, :, own] for h in range(heads)) + tuple(
            total_in[h, :, own] for h in range(heads)
        )
        for s, base in enumerate(bases):

            def key_block(j, state, s=s, base=base):
                k_at = pl.multiple_of(j * BK, BK)
                block = pl.ds(k_at, BK)
                place = lax.broadcasted_iota(jnp.int32, (BK, BQ), 0) + (k_at + base)
                allowed = (place >= begin) & (place < end)
                raws = [
                    contract(keys[s][h, :, block], query[h, :, own], ((0,), (0,)))
                    for h in range(heads)
                ]
                tops, totals, shrinks, lows = [], [], [], []
                for h in range(heads):
                    raw = jnp.where(allowed, raws[h] * scale, NEG)
                    top = jnp.maximum(state[h], jnp.max(raw, axis=0, keepdims=True))
                    probs = jnp.exp2(raw - top)
                    shrink = jnp.exp2(state[h] - top)
                    tops.append(top)
                    totals.append(state[heads + h] * shrink + jnp.sum(probs, axis=0, keepdims=True))
                    shrinks.append(shrink)
                    lows.append(probs.astype(BF16))
                for h in range(heads):
                    mixed[h] = mixed[h] * shrinks[h] + contract(
                        values[s][h, :, block], lows[h], ((1,), (0,))
                    )
                return tuple(tops) + tuple(totals)

            state = lax.fori_loop(bounds[s, 0, i], bounds[s, 1, i], key_block, state)
        for h in range(heads):
            top, total = state[h], state[heads + h]
            if last:
                mixed_out[h, :, own] = (mixed[h] / total).astype(BF16)
                top_out[h, :, own] = top + jnp.log2(total)
            else:
                mixed_out[h, :, own] = mixed[h]
                top_out[h, :, own] = top
            total_out[h, :, own] = total
        return 0

    lax.fori_loop(0, rows // BQ, query_block, 0)


def attend(bounds, span, query, carried, keys, values, bases, last):
    heads, hd, rows = query.shape
    vmem = pl.BlockSpec(memory_space=pltpu.VMEM)
    line = jax.ShapeDtypeStruct((heads, 1, rows), F32)
    return pl.pallas_call(
        functools.partial(forward_kernel, bases, heads, last),
        out_shape=(
            jax.ShapeDtypeStruct((heads, hd, rows), BF16 if last else F32),
            line,
            line,
        ),
        in_specs=[pl.BlockSpec(memory_space=pltpu.SMEM)] + [vmem] * (5 + 2 * len(bases)),
        out_specs=(vmem,) * 3,
        scratch_shapes=[pltpu.VMEM((heads, hd, BQ), F32)],
        compiler_params=pltpu.CompilerParams(vmem_limit_bytes=40 << 20),
        cost_estimate=COST,
    )(bounds, span, query, *carried, *keys, *values)


def tile_back(heads, allowed, keys, values, query, grad, logsum, delta):
    scale = FACTOR * LOG2E
    raws = [contract(keys[h], query[h], ((0,), (0,))) for h in range(heads)]
    grads = [contract(values[h], grad[h], ((0,), (0,))) for h in range(heads)]
    found = []
    for h in range(heads):
        raw = jnp.where(allowed, raws[h] * scale - logsum[h], NEG)
        probs = jnp.exp2(raw)
        found.append((probs.astype(BF16), (probs * (grads[h] - delta[h])).astype(BF16)))
    return found


def backward_kernel(bases, heads, bounds, span, query, grad, logsum, delta, *refs):
    segments = len(bases)
    keys = refs[:segments]
    values = refs[segments : 2 * segments]
    grad_query, grad_keys, grad_values, sum_query, sum_keys, sum_values = refs[2 * segments :]
    sum_query[...] = jnp.zeros_like(sum_query)
    for s, base in enumerate(bases):

        def key_block(j, _, s=s, base=base):
            k_at = pl.multiple_of(j * BK, BK)
            block = pl.ds(k_at, BK)
            place = lax.broadcasted_iota(jnp.int32, (BK, BQ), 0) + (k_at + base)
            if base == 0:
                sum_keys[...] = jnp.zeros_like(sum_keys)
                sum_values[...] = jnp.zeros_like(sum_values)

            def query_block(i, _):
                own = pl.ds(pl.multiple_of(i * BQ, BQ), BQ)
                allowed = (place >= span[0:1, own]) & (place < span[1:2, own])
                q = [query[h, :, own] for h in range(heads)]
                g = [grad[h, :, own] for h in range(heads)]
                k = [keys[s][h, :, block] for h in range(heads)]
                found = tile_back(
                    heads,
                    allowed,
                    k,
                    [values[s][h, :, block] for h in range(heads)],
                    q,
                    g,
                    [logsum[h, :, own] for h in range(heads)],
                    [delta[h, :, own] for h in range(heads)],
                )
                for h in range(heads):
                    probs, grad_raw = found[h]
                    if base == 0:
                        sum_values[h] += contract(g[h], probs, ((1,), (1,)))
                        sum_keys[h] += contract(q[h], grad_raw, ((1,), (1,)))
                    sum_query[h, :, own] += contract(k[h], grad_raw, ((1,), (0,)))
                return 0

            lax.fori_loop(bounds[s, 0, j], bounds[s, 1, j], query_block, 0)
            if base == 0:
                for h in range(heads):
                    grad_keys[h, :, block] = sum_keys[h]
                    grad_values[h, :, block] = sum_values[h]
            return 0

        lax.fori_loop(0, keys[s].shape[2] // BK, key_block, 0)
    grad_query[...] = (sum_query[...] * FACTOR).astype(BF16)


def attend_back(bounds, span, query, grad, logsum, delta, keys, values, bases):
    heads, hd, rows = query.shape
    vmem = pl.BlockSpec(memory_space=pltpu.VMEM)
    full = jax.ShapeDtypeStruct((heads, hd, rows), F32)
    return pl.pallas_call(
        functools.partial(backward_kernel, bases, heads),
        out_shape=(jax.ShapeDtypeStruct((heads, hd, rows), BF16), full, full),
        in_specs=[pl.BlockSpec(memory_space=pltpu.SMEM)] + [vmem] * (5 + 2 * len(bases)),
        out_specs=(vmem,) * 3,
        scratch_shapes=[
            pltpu.VMEM((heads, hd, rows), F32),
            pltpu.VMEM((heads, hd, BK), F32),
            pltpu.VMEM((heads, hd, BK), F32),
        ],
        compiler_params=pltpu.CompilerParams(vmem_limit_bytes=44 << 20),
        cost_estimate=COST,
    )(bounds, span, query, grad, logsum, delta, *keys, *values)


def others_kernel(segments, heads, bounds, keys, values, keys_in, values_in, *refs):
    spans, query, grad, logsum, delta = (refs[n * segments : (n + 1) * segments] for n in range(5))
    grad_keys, grad_values, sum_keys, sum_values = refs[5 * segments :]

    def key_block(j, _):
        k_at = pl.multiple_of(j * BK, BK)
        block = pl.ds(k_at, BK)
        place = lax.broadcasted_iota(jnp.int32, (BK, BQ), 0) + k_at
        for h in range(heads):
            sum_keys[h] = keys_in[h, :, block]
            sum_values[h] = values_in[h, :, block]
        for s in range(segments):

            def query_block(i, _, s=s):
                own = pl.ds(pl.multiple_of(i * BQ, BQ), BQ)
                allowed = (place >= spans[s][0:1, own]) & (place < spans[s][1:2, own])
                q = [query[s][h, :, own] for h in range(heads)]
                g = [grad[s][h, :, own] for h in range(heads)]
                found = tile_back(
                    heads,
                    allowed,
                    [keys[h, :, block] for h in range(heads)],
                    [values[h, :, block] for h in range(heads)],
                    q,
                    g,
                    [logsum[s][h, :, own] for h in range(heads)],
                    [delta[s][h, :, own] for h in range(heads)],
                )
                for h in range(heads):
                    probs, grad_raw = found[h]
                    sum_values[h] += contract(g[h], probs, ((1,), (1,)))
                    sum_keys[h] += contract(q[h], grad_raw, ((1,), (1,)))
                return 0

            lax.fori_loop(bounds[s, 0, j], bounds[s, 1, j], query_block, 0)
        for h in range(heads):
            grad_keys[h, :, block] = (sum_keys[h] * FACTOR).astype(BF16)
            grad_values[h, :, block] = sum_values[h].astype(BF16)
        return 0

    lax.fori_loop(0, keys.shape[2] // BK, key_block, 0)


def others_back(bounds, keys, values, keys_in, values_in, spans, query, grad, logsum, delta):
    heads, hd, rows = keys.shape
    segments = len(query)
    vmem = pl.BlockSpec(memory_space=pltpu.VMEM)
    shape = jax.ShapeDtypeStruct((heads, hd, rows), BF16)
    return pl.pallas_call(
        functools.partial(others_kernel, segments, heads),
        out_shape=(shape, shape),
        in_specs=[pl.BlockSpec(memory_space=pltpu.SMEM)] + [vmem] * (4 + 5 * segments),
        out_specs=(vmem, vmem),
        scratch_shapes=[pltpu.VMEM((heads, hd, BK), F32), pltpu.VMEM((heads, hd, BK), F32)],
        compiler_params=pltpu.CompilerParams(vmem_limit_bytes=40 << 20),
        cost_estimate=COST,
    )(bounds, keys, values, keys_in, values_in, *spans, *query, *grad, *logsum, *delta)


def swap(value, axis, bit):
    return lax.ppermute(value, axis, [(i, i ^ bit) for i in range(lax.axis_size(axis))])


def shift(value, axis, distance):
    devices = range(lax.axis_size(axis))
    return lax.ppermute(value, axis, [(i, i + distance) for i in devices if i + distance in devices])


def bits_of(axis):
    size = lax.axis_size(axis)
    return [1 << b for b in range(size.bit_length() - 1)]


def bit_set(axis, bit):
    return (lax.axis_index(axis) & bit) != 0


def sum_all(value, axis):
    for bit in bits_of(axis):
        value = value + swap(value, axis, bit)
    return value


def after(anchor, *values):
    held = values if anchor is None else lax.optimization_barrier((anchor, *values))[1:]
    return held[0] if len(values) == 1 else held


def in_order(mine, other, upper, dim=0):
    return jnp.where(
        upper, jnp.stack([other, mine], axis=dim), jnp.stack([mine, other], axis=dim)
    )


def gather_tensor(value):
    pair = in_order(value, swap(value, "tensor", 2), bit_set("tensor", 2))
    quad = in_order(pair, swap(pair, "tensor", 1), bit_set("tensor", 1), dim=1)
    return lax.optimization_barrier(quad.reshape((4 * value.shape[0],) + value.shape[1:]))


def scatter_tensor(partial):
    n = partial.shape[0] // 4
    core = lax.axis_index("tensor") % 2
    across = lax.axis_index("tensor") // 2
    parts = partial.astype(BF16).reshape((2, 2, n) + partial.shape[1:])
    kept = lax.dynamic_index_in_dim(parts, core, 1, keepdims=False)
    sent = lax.dynamic_index_in_dim(parts, 1 - core, 1, keepdims=False)
    come = swap(sent, "tensor", 1)
    come = after((yield sent), come)
    half = kept.astype(F32) + come.astype(F32)
    half_low = half.astype(BF16)
    stay = lax.dynamic_index_in_dim(half, across, 0, keepdims=False)
    leave = lax.dynamic_index_in_dim(half_low, 1 - across, 0, keepdims=False)
    come = swap(leave, "tensor", 2)
    come = after((yield leave), come)
    return stay + come.astype(F32)


def scatter_data_steps(partial):
    size = lax.axis_size("dp")
    index = lax.axis_index("dp")
    bits = bits_of("dp")
    count = len(bits)
    rest = (partial.shape[0] // size,) + partial.shape[1:]
    held = partial.astype(BF16).reshape((2,) * count + rest)
    left = list(reversed(bits))
    for bit in [1] + bits[:0:-1]:
        axis = left.index(bit)
        mine = (index // bit) % 2
        kept = lax.dynamic_index_in_dim(held, mine, axis, keepdims=False)
        sent = lax.dynamic_index_in_dim(held, 1 - mine, axis, keepdims=False).astype(BF16)
        come = swap(sent, "dp", bit)
        come = after((yield sent), come)
        held = kept.astype(F32) + come.astype(F32)
        left.remove(bit)
    return held


def scatter_data(partials):
    joined = jnp.concatenate([partial.astype(BF16) for partial in partials], axis=1)
    found = lax.psum_scatter(joined, "dp", scatter_dimension=0, tiled=True)
    cuts, at = [], 0
    for partial in partials[:-1]:
        at += partial.shape[1]
        cuts.append(at)
    return joined, lambda anchor: jnp.split(after(anchor, found).astype(F32), cuts, axis=1)


def finish(steps, anchor=None):
    try:
        while True:
            steps.send(anchor)
    except StopIteration as end:
        return end.value


def layer_norm(value):
    center = value - jnp.mean(value, axis=-1, keepdims=True)
    spread = jnp.mean(center * center, axis=-1, keepdims=True)
    return center * lax.rsqrt(spread + 1e-06)


def gelu_tanh(value):
    return jax.nn.gelu(value, approximate=True)


def onehot_sum(select, values, form):
    upper = values.astype(BF16)
    lower = (values - upper.astype(F32)).astype(BF16)
    first = jnp.einsum(form, select, upper, preferred_element_type=F32)
    return first + jnp.einsum(form, select, lower, preferred_element_type=F32)


def on_device(
    tokens,
    condition,
    latent_lengths,
    in_weight,
    in_bias,
    out_weight,
    out_bias,
    up_weight,
    up_bias,
    down_weight,
    down_bias,
    mod_weight,
    mod_bias,
    out_grad,
):
    rows, width = tokens.shape
    latents = condition.shape[0]
    local_width = in_weight.shape[2]
    heads = local_width // HD
    data_size = lax.axis_size("dp")
    data_index = lax.axis_index("dp")
    tensor_index = lax.axis_index("tensor")
    quarter = rows // 4
    row_start = tensor_index * quarter

    def mine(value):
        return lax.dynamic_slice_in_dim(value, row_start, quarter, 0)

    places = jnp.arange(latents, dtype=jnp.int32)
    earlier = places[None, :] < places[:, None]
    starts = jnp.sum(jnp.where(earlier, latent_lengths[None, :], 0), axis=1)
    ends = starts + latent_lengths
    first_row = data_index * rows
    own_places = first_row + jnp.arange(rows, dtype=jnp.int32)

    def span_of(at):
        inside = (at[:, None] >= starts[None, :]) & (at[:, None] < ends[None, :])
        begin = jnp.sum(jnp.where(inside, starts[None, :] - first_row, 0), axis=1)
        end = jnp.sum(jnp.where(inside, ends[None, :] - first_row, 0), axis=1)
        return begin, end, inside

    bases = (-rows, 0, rows)
    windows = [span_of(own_places + base) for base in bases]
    spans = [jnp.stack(window[:2]) for window in windows]
    selects = [window[2].astype(BF16) for window in windows]
    begin, end = windows[1][:2]
    span, select = spans[1], selects[1]
    select_mine = mine(select)
    forward_bounds, backward_bounds, other_bounds = [], [], []
    for base in bases:
        low = jnp.clip(begin[::BQ] - base, 0, rows) // BK
        high = (jnp.clip(end[BQ - 1 :: BQ] - base, 0, rows) + BK - 1) // BK
        forward_bounds.append(jnp.stack([low, high]))
        key_at = first_row + base + jnp.arange(rows // BK, dtype=jnp.int32) * BK
        low = jnp.clip(span_of(key_at)[0], 0, rows) // BQ
        high = (jnp.clip(span_of(key_at + BK - 1)[1], 0, rows) + BQ - 1) // BQ
        valid = (key_at >= 0) & (key_at < rows * data_size)
        backward_bounds.append(jnp.where(valid[None, :], jnp.stack([low, high]), 0))
        low = jnp.clip(begin[::BK] - base, 0, rows) // BQ
        high = (jnp.clip(end[BK - 1 :: BK] - base, 0, rows) + BQ - 1) // BQ
        other_bounds.append(jnp.stack([low, high]))
    backward_bounds = jnp.stack(backward_bounds)
    other_bounds = jnp.stack([other_bounds[0], other_bounds[2]])

    tokens_mine = mine(tokens)
    behind_tokens = gather_tensor(shift(tokens_mine, "dp", 1))
    ahead_tokens = gather_tensor(shift(tokens_mine, "dp", -1))

    cond_full = condition.astype(F32)
    silu_cond = jax.nn.silu(cond_full).astype(BF16)
    mod_local = (
        jnp.dot(silu_cond, mod_weight, preferred_element_type=F32) + mod_bias.astype(F32)
    ).astype(BF16)
    modulation = gather_tensor(mod_local[None])
    modulation = modulation.transpose(1, 0, 2).reshape(latents, 6 * width)

    def spread(chosen, first, count):
        return jnp.dot(
            chosen,
            modulation[:, first * width : (first + count) * width],
            preferred_element_type=BF16,
        )

    others = spread(select_mine, 2, 4).astype(F32)
    gate_a, shift_m, scale_m, gate_m = (others[:, i * width : (i + 1) * width] for i in range(4))
    gate_m_all = spread(select, 5, 1).astype(F32)

    bias_full = in_bias.astype(F32)
    proj_bias = jnp.stack([bias_full[0], jnp.zeros_like(bias_full[0]), bias_full[1]])

    def entry_of(rows_of, chosen):
        shift_scale = spread(chosen, 0, 2)
        scale = shift_scale[:, width:].astype(F32)
        value = rows_of.astype(F32)
        center = value - jnp.mean(value, axis=-1, keepdims=True)
        inverse = lax.rsqrt(jnp.mean(center * center, axis=-1, keepdims=True) + 1e-06)
        normed = center * inverse
        entry = (normed * (1.0 + scale) + shift_scale[:, :width].astype(F32)).astype(BF16)
        return entry, normed, inverse

    def project(entry):
        found = jnp.einsum("dcf,td->cft", in_weight, entry, preferred_element_type=F32)
        found = (found + proj_bias[:, :, None]).astype(BF16)
        return found.reshape(3, heads, HD, rows)

    entry, normed, inverse = entry_of(tokens, select)
    normed_turned, inverse = normed.T, inverse.T
    own = project(entry)
    sides = [
        project(entry_of(behind_tokens, selects[0])[0]),
        project(entry_of(ahead_tokens, selects[2])[0]),
    ]
    query = own[0]
    line = jnp.zeros((heads, 1, rows), F32)
    carried = attend(
        jnp.stack([forward_bounds[1]]),
        span,
        query,
        (jnp.zeros((heads, HD, rows), F32), line + NEG, line),
        [own[1]],
        [own[2]],
        (0,),
        False,
    )
    attended, logsum, _ = attend(
        jnp.stack([forward_bounds[0], forward_bounds[2]]),
        span,
        query,
        carried,
        [side[1] for side in sides],
        [side[2] for side in sides],
        (-rows, rows),
        True,
    )
    attended_flat = attended.reshape(local_width, rows)
    attn_part = lax.dot_general(
        attended_flat, out_weight, (((0,), (1,)), ((), ())), preferred_element_type=F32
    )
    attn_steps = scatter_tensor(attn_part)
    next(attn_steps)
    branch = finish(attn_steps) + out_bias.astype(F32)

    middle = tokens_mine.astype(F32) + gate_a * branch
    normed_m, norm_back_m = jax.vjp(layer_norm, middle)
    entry_m = gather_tensor((normed_m * (1.0 + scale_m) + shift_m).astype(BF16))
    hidden_pre = jnp.dot(entry_m, up_weight, preferred_element_type=F32) + up_bias.astype(F32)
    hidden_full, gelu_back = jax.vjp(gelu_tanh, hidden_pre)
    hidden = hidden_full.astype(BF16)
    grad_out = out_grad.astype(F32)
    grad_branch_m = (gate_m_all * grad_out).astype(BF16)
    grad_hidden = jnp.einsum("td,df->tf", grad_branch_m, down_weight, preferred_element_type=F32)
    grad_pre = gelu_back(grad_hidden)[0].astype(BF16)
    grad_down_w = jnp.einsum("td,tf->df", grad_branch_m, hidden, preferred_element_type=F32)
    entry_part = jnp.einsum("tf,df->td", grad_pre, up_weight, preferred_element_type=F32)
    entry_steps = scatter_tensor(entry_part)
    grad_pre = after(next(entry_steps), grad_pre)
    grad_out_mine = mine(out_grad).astype(F32)
    grad_up_w = jnp.einsum("td,tf->df", entry_m, grad_pre, preferred_element_type=F32)
    wide_sent, wide_sums = scatter_data([grad_down_w, grad_up_w])
    grad_entry_m = finish(entry_steps, wide_sent)
    grad_down_b = jnp.sum(grad_branch_m.astype(F32), axis=0)
    grad_up_b = jnp.sum(grad_pre.astype(F32), axis=0)
    grad_middle = grad_out_mine + norm_back_m(grad_entry_m * (1.0 + scale_m))[0]
    grad_gate_a = grad_middle * branch
    grad_branch_mine = (gate_a * grad_middle).astype(BF16)
    grad_out_b = jnp.sum(grad_branch_mine.astype(F32), axis=0)
    grad_branch = gather_tensor(grad_branch_mine)
    grad_attended = lax.dot_general(
        out_weight, grad_branch, (((0,), (1,)), ((), ())), preferred_element_type=F32
    ).astype(BF16)

    mlp_part = jnp.einsum(
        "tf,df->td",
        after(grad_branch_mine, hidden),
        down_weight,
        preferred_element_type=F32,
    )
    mlp_steps = scatter_tensor(mlp_part)
    next(mlp_steps)

    grad_heads = grad_attended.reshape(heads, HD, rows)
    delta = jnp.sum(grad_heads.astype(F32) * attended.astype(F32), axis=1, keepdims=True)
    stats = jnp.stack([logsum, delta])
    side_grads = [shift(grad_heads, "dp", 1), shift(grad_heads, "dp", -1)]
    side_stats = [shift(stats, "dp", 1), shift(stats, "dp", -1)]
    grad_query, part_keys, part_values = attend_back(
        backward_bounds,
        span,
        query,
        grad_heads,
        logsum,
        delta,
        [sides[0][1], own[1], sides[1][1]],
        [sides[0][2], own[2], sides[1][2]],
        bases,
    )
    mlp_steps.send(grad_heads)
    branch_m = finish(mlp_steps, grad_query) + down_bias.astype(F32)
    output = (middle + gate_m * branch_m).astype(BF16)
    grad_gate_m = grad_out_mine * branch_m
    grad_out_w = lax.dot_general(
        grad_branch, attended_flat, (((0,), (1,)), ((), ())), preferred_element_type=F32
    )
    grad_keys, grad_values = others_back(
        other_bounds,
        own[1],
        own[2],
        part_keys,
        part_values,
        [spans[0], spans[2]],
        [side[0] for side in sides],
        side_grads,
        [side[0] for side in side_stats],
        [side[1] for side in side_stats],
    )
    grad_proj = [x.reshape(local_width, rows) for x in (grad_query, grad_keys, grad_values)]
    grad_q_w, grad_k_w, grad_v_w = (
        lax.dot_general(entry, x, (((0,), (1,)), ((), ())), preferred_element_type=F32)
        for x in grad_proj
    )
    early_steps = scatter_data_steps(jnp.concatenate([grad_out_w, grad_q_w], axis=1))
    next(early_steps)
    early_sent = early_steps.send(grad_keys)
    late_steps = scatter_data_steps(jnp.concatenate([grad_k_w, grad_v_w], axis=1))
    late_sent = next(late_steps)
    grad_proj = after((late_sent, early_sent), *grad_proj)
    grad_in_b = jnp.stack([jnp.sum(grad_proj[c].astype(F32), axis=1) for c in (0, 2)])
    grad_entry = lax.dot_general(
        in_weight.reshape(width, 3 * local_width),
        jnp.concatenate(grad_proj, axis=0),
        (((1,), (0,)), ((), ())),
        preferred_element_type=F32,
    )

    scale_turned = lax.dot_general(
        modulation[:, width : 2 * width],
        select,
        (((0,), (1,)), ((), ())),
        preferred_element_type=BF16,
    ).astype(F32)
    scaled = grad_entry * (1.0 + scale_turned)
    input_part = (
        scaled
        - jnp.mean(scaled, axis=0, keepdims=True)
        - normed_turned * jnp.mean(scaled * normed_turned, axis=0, keepdims=True)
    ) * inverse

    split_terms = jnp.concatenate([grad_entry, grad_entry * normed_turned], axis=0)
    kept_terms = jnp.concatenate(
        [grad_gate_a, grad_entry_m, grad_entry_m * normed_m, grad_gate_m], axis=1
    )
    per_latent = jnp.concatenate(
        [onehot_sum(select, split_terms, "tl,mt->lm"), onehot_sum(select_mine, kept_terms, "tl,tm->lm")],
        axis=1,
    )
    columns_here = mod_weight.shape[1]
    arranged = per_latent.reshape(latents, 4, columns_here).transpose(1, 0, 2)

    out_b_row = jnp.pad(grad_out_b, (0, columns_here - width))[None]

    def for_device(flip):
        chosen = lax.dynamic_index_in_dim(arranged, tensor_index ^ flip, 0, keepdims=False)
        return jnp.concatenate([chosen, out_b_row])

    given = [for_device(flip) for flip in range(4)]
    come = [swap(given[flip], "tensor", flip) for flip in (1, 2, 3)]
    placed = lax.dynamic_update_slice_in_dim(
        jnp.zeros((width, rows), F32), grad_middle.T, row_start, 1
    )
    tokens_steps = scatter_tensor(input_part + placed)
    tokens_sent = next(tokens_steps)
    come = after(tokens_sent, *come)
    small = (given[0] + come[0]) + (come[1] + come[2])
    small = jnp.concatenate(
        [small]
        + [
            jnp.pad(value, (0, columns_here - value.shape[0]))[None]
            for value in (grad_in_b.reshape(-1), grad_up_b, grad_down_b)
        ]
    )
    late_sent = late_steps.send(tokens_sent)
    tokens_sent = tokens_steps.send(late_sent)
    for place, bit in enumerate(bits_of("dp")):
        come = swap(small, "dp", bit)
        if place == 0:
            come = after(tokens_sent, come)
        small = small + come
    grad_mod = small[:latents].astype(BF16)
    sum_out_b = small[latents, :width]
    sum_in_b = small[latents + 1, : 2 * local_width]
    sum_up_b = small[latents + 2, : grad_up_b.shape[0]]
    sum_down_b = small[latents + 3, :width]
    own_width = width // data_size
    own_silu = lax.dynamic_slice_in_dim(silu_cond, data_index * own_width, own_width, 1)
    grad_mod_w = jnp.einsum("ld,lm->dm", own_silu, grad_mod, preferred_element_type=F32)
    grad_mod_b = jnp.sum(grad_mod.astype(F32), axis=0)
    own_count = latents // data_size
    own_grad_mod = lax.dynamic_slice_in_dim(grad_mod, data_index * own_count, own_count, 0)
    own_cond = lax.dynamic_slice_in_dim(cond_full, data_index * own_count, own_count, 0)
    silu_grad = jnp.einsum("lm,dm->ld", own_grad_mod, mod_weight, preferred_element_type=F32)
    cond_part = jax.vjp(jax.nn.silu, own_cond)[1](silu_grad)[0]
    cond_parts = cond_part.reshape(own_count, 4, width // 4).transpose(1, 0, 2)
    grad_cond = lax.dynamic_index_in_dim(cond_parts, tensor_index, 0, keepdims=False)
    for bit in (1, 2, 3):
        grad_cond = grad_cond + swap(
            lax.dynamic_index_in_dim(cond_parts, tensor_index ^ bit, 0, keepdims=False),
            "tensor",
            bit,
        )

    grad_tokens = finish(tokens_steps, grad_mod_w).T
    sum_down_w, sum_up_w = wide_sums(grad_mod_w)
    early = finish(early_steps, tokens_sent)
    late = finish(late_steps, small)
    sum_out_w = early[:, :local_width]
    sum_in_w = jnp.stack(
        [early[:, local_width:], late[:, :local_width], late[:, local_width:]], axis=1
    )
    return (
        output,
        grad_tokens,
        grad_cond,
        sum_in_w,
        sum_in_b.reshape(2, local_width),
        sum_out_w,
        sum_out_b,
        sum_up_w,
        sum_up_b,
        sum_down_w,
        sum_down_b,
        grad_mod_w,
        grad_mod_b,
    )


def solution(mesh):
    placed = (
        P("dp", None),
        P(),
        P(),
        P(None, None, "tensor"),
        P(None, "tensor"),
        P(None, "tensor"),
        P(),
        P(None, "tensor"),
        P("tensor"),
        P(None, "tensor"),
        P(),
        P(None, "tensor"),
        P("tensor"),
        P("dp", None),
    )
    return jax.shard_map(
        on_device,
        mesh=mesh,
        in_specs=placed,
        out_specs=(
            P(("dp", "tensor"), None),
            P("dp", "tensor"),
            P("dp", "tensor"),
            P("dp", None, "tensor"),
            P(None, "tensor"),
            P("dp", "tensor"),
            P(),
            P("dp", "tensor"),
            P("tensor"),
            P("dp", "tensor"),
            P(),
            P("dp", "tensor"),
            P("tensor"),
        ),
        check_vma=False,
    )
```

```python
import functools
import math

import jax
import jax.numpy as jnp
from jax import lax
from jax.experimental import pallas as pl
from jax.experimental.pallas import tpu as pltpu
from jax.sharding import PartitionSpec as P

HD = 72
FACTOR = HD ** (-0.5)
LOG2E = math.log2(math.e)
NEG = -1e30
BQ = 256
BK = 256
COST = pl.CostEstimate(flops=18 << 30, bytes_accessed=24 << 20, transcendentals=1 << 22)
F32 = jnp.float32
BF16 = jnp.bfloat16


def contract(a, b, dims):
    return lax.dot_general(a, b, (dims, ((), ())), preferred_element_type=F32)


def forward_kernel(bases, heads, last, bounds, span, query, mixed_in, top_in, total_in, *refs):
    segments = len(bases)
    keys = refs[:segments]
    values = refs[segments : 2 * segments]
    mixed_out, top_out, total_out, mixed = refs[2 * segments :]
    rows = query.shape[2]
    scale = FACTOR * LOG2E

    def query_block(i, _):
        own = pl.ds(pl.multiple_of(i * BQ, BQ), BQ)
        begin = span[0:1, own]
        end = span[1:2, own]
        for h in range(heads):
            mixed[h] = mixed_in[h, :, own]
        state = tuple(top_in[h, :, own] for h in range(heads)) + tuple(
            total_in[h, :, own] for h in range(heads)
        )
        for s, base in enumerate(bases):

            def key_block(j, state, s=s, base=base):
                k_at = pl.multiple_of(j * BK, BK)
                block = pl.ds(k_at, BK)
                place = lax.broadcasted_iota(jnp.int32, (BK, BQ), 0) + (k_at + base)
                allowed = (place >= begin) & (place < end)
                raws = [
                    contract(keys[s][h, :, block], query[h, :, own], ((0,), (0,)))
                    for h in range(heads)
                ]
                tops, totals, shrinks, lows = [], [], [], []
                for h in range(heads):
                    raw = jnp.where(allowed, raws[h] * scale, NEG)
                    top = jnp.maximum(state[h], jnp.max(raw, axis=0, keepdims=True))
                    probs = jnp.exp2(raw - top)
                    shrink = jnp.exp2(state[h] - top)
                    tops.append(top)
                    totals.append(state[heads + h] * shrink + jnp.sum(probs, axis=0, keepdims=True))
                    shrinks.append(shrink)
                    lows.append(probs.astype(BF16))
                for h in range(heads):
                    mixed[h] = mixed[h] * shrinks[h] + contract(
                        values[s][h, :, block], lows[h], ((1,), (0,))
                    )
                return tuple(tops) + tuple(totals)

            state = lax.fori_loop(bounds[s, 0, i], bounds[s, 1, i], key_block, state)
        for h in range(heads):
            top, total = state[h], state[heads + h]
            if last:
                mixed_out[h, :, own] = (mixed[h] / total).astype(BF16)
                top_out[h, :, own] = top + jnp.log2(total)
            else:
                mixed_out[h, :, own] = mixed[h]
                top_out[h, :, own] = top
            total_out[h, :, own] = total
        return 0

    lax.fori_loop(0, rows // BQ, query_block, 0)


def attend(bounds, span, query, carried, keys, values, bases, last):
    heads, hd, rows = query.shape
    vmem = pl.BlockSpec(memory_space=pltpu.VMEM)
    line = jax.ShapeDtypeStruct((heads, 1, rows), F32)
    return pl.pallas_call(
        functools.partial(forward_kernel, bases, heads, last),
        out_shape=(
            jax.ShapeDtypeStruct((heads, hd, rows), BF16 if last else F32),
            line,
            line,
        ),
        in_specs=[pl.BlockSpec(memory_space=pltpu.SMEM)] + [vmem] * (5 + 2 * len(bases)),
        out_specs=(vmem,) * 3,
        scratch_shapes=[pltpu.VMEM((heads, hd, BQ), F32)],
        compiler_params=pltpu.CompilerParams(vmem_limit_bytes=40 << 20),
        cost_estimate=COST,
    )(bounds, span, query, *carried, *keys, *values)


def tile_back(heads, allowed, keys, values, query, grad, logsum, delta):
    scale = FACTOR * LOG2E
    raws = [contract(keys[h], query[h], ((0,), (0,))) for h in range(heads)]
    grads = [contract(values[h], grad[h], ((0,), (0,))) for h in range(heads)]
    found = []
    for h in range(heads):
        raw = jnp.where(allowed, raws[h] * scale - logsum[h], NEG)
        probs = jnp.exp2(raw)
        found.append((probs.astype(BF16), (probs * (grads[h] - delta[h])).astype(BF16)))
    return found


def backward_kernel(bases, heads, bounds, span, query, grad, logsum, delta, *refs):
    segments = len(bases)
    keys = refs[:segments]
    values = refs[segments : 2 * segments]
    grad_query, grad_keys, grad_values, sum_query, sum_keys, sum_values = refs[2 * segments :]
    sum_query[...] = jnp.zeros_like(sum_query)
    for s, base in enumerate(bases):

        def key_block(j, _, s=s, base=base):
            k_at = pl.multiple_of(j * BK, BK)
            block = pl.ds(k_at, BK)
            place = lax.broadcasted_iota(jnp.int32, (BK, BQ), 0) + (k_at + base)
            if base == 0:
                sum_keys[...] = jnp.zeros_like(sum_keys)
                sum_values[...] = jnp.zeros_like(sum_values)

            def query_block(i, _):
                own = pl.ds(pl.multiple_of(i * BQ, BQ), BQ)
                allowed = (place >= span[0:1, own]) & (place < span[1:2, own])
                q = [query[h, :, own] for h in range(heads)]
                g = [grad[h, :, own] for h in range(heads)]
                k = [keys[s][h, :, block] for h in range(heads)]
                found = tile_back(
                    heads,
                    allowed,
                    k,
                    [values[s][h, :, block] for h in range(heads)],
                    q,
                    g,
                    [logsum[h, :, own] for h in range(heads)],
                    [delta[h, :, own] for h in range(heads)],
                )
                for h in range(heads):
                    probs, grad_raw = found[h]
                    if base == 0:
                        sum_values[h] += contract(g[h], probs, ((1,), (1,)))
                        sum_keys[h] += contract(q[h], grad_raw, ((1,), (1,)))
                    sum_query[h, :, own] += contract(k[h], grad_raw, ((1,), (0,)))
                return 0

            lax.fori_loop(bounds[s, 0, j], bounds[s, 1, j], query_block, 0)
            if base == 0:
                for h in range(heads):
                    grad_keys[h, :, block] = sum_keys[h]
                    grad_values[h, :, block] = sum_values[h]
            return 0

        lax.fori_loop(0, keys[s].shape[2] // BK, key_block, 0)
    grad_query[...] = (sum_query[...] * FACTOR).astype(BF16)


def attend_back(bounds, span, query, grad, logsum, delta, keys, values, bases):
    heads, hd, rows = query.shape
    vmem = pl.BlockSpec(memory_space=pltpu.VMEM)
    full = jax.ShapeDtypeStruct((heads, hd, rows), F32)
    return pl.pallas_call(
        functools.partial(backward_kernel, bases, heads),
        out_shape=(jax.ShapeDtypeStruct((heads, hd, rows), BF16), full, full),
        in_specs=[pl.BlockSpec(memory_space=pltpu.SMEM)] + [vmem] * (5 + 2 * len(bases)),
        out_specs=(vmem,) * 3,
        scratch_shapes=[
            pltpu.VMEM((heads, hd, rows), F32),
            pltpu.VMEM((heads, hd, BK), F32),
            pltpu.VMEM((heads, hd, BK), F32),
        ],
        compiler_params=pltpu.CompilerParams(vmem_limit_bytes=44 << 20),
        cost_estimate=COST,
    )(bounds, span, query, grad, logsum, delta, *keys, *values)


def others_kernel(segments, heads, bounds, keys, values, keys_in, values_in, *refs):
    spans, query, grad, logsum, delta = (refs[n * segments : (n + 1) * segments] for n in range(5))
    grad_keys, grad_values, sum_keys, sum_values = refs[5 * segments :]

    def key_block(j, _):
        k_at = pl.multiple_of(j * BK, BK)
        block = pl.ds(k_at, BK)
        place = lax.broadcasted_iota(jnp.int32, (BK, BQ), 0) + k_at
        for h in range(heads):
            sum_keys[h] = keys_in[h, :, block]
            sum_values[h] = values_in[h, :, block]
        for s in range(segments):

            def query_block(i, _, s=s):
                own = pl.ds(pl.multiple_of(i * BQ, BQ), BQ)
                allowed = (place >= spans[s][0:1, own]) & (place < spans[s][1:2, own])
                q = [query[s][h, :, own] for h in range(heads)]
                g = [grad[s][h, :, own] for h in range(heads)]
                found = tile_back(
                    heads,
                    allowed,
                    [keys[h, :, block] for h in range(heads)],
                    [values[h, :, block] for h in range(heads)],
                    q,
                    g,
                    [logsum[s][h, :, own] for h in range(heads)],
                    [delta[s][h, :, own] for h in range(heads)],
                )
                for h in range(heads):
                    probs, grad_raw = found[h]
                    sum_values[h] += contract(g[h], probs, ((1,), (1,)))
                    sum_keys[h] += contract(q[h], grad_raw, ((1,), (1,)))
                return 0

            lax.fori_loop(bounds[s, 0, j], bounds[s, 1, j], query_block, 0)
        for h in range(heads):
            grad_keys[h, :, block] = (sum_keys[h] * FACTOR).astype(BF16)
            grad_values[h, :, block] = sum_values[h].astype(BF16)
        return 0

    lax.fori_loop(0, keys.shape[2] // BK, key_block, 0)


def others_back(bounds, keys, values, keys_in, values_in, spans, query, grad, logsum, delta):
    heads, hd, rows = keys.shape
    segments = len(query)
    vmem = pl.BlockSpec(memory_space=pltpu.VMEM)
    shape = jax.ShapeDtypeStruct((heads, hd, rows), BF16)
    return pl.pallas_call(
        functools.partial(others_kernel, segments, heads),
        out_shape=(shape, shape),
        in_specs=[pl.BlockSpec(memory_space=pltpu.SMEM)] + [vmem] * (4 + 5 * segments),
        out_specs=(vmem, vmem),
        scratch_shapes=[pltpu.VMEM((heads, hd, BK), F32), pltpu.VMEM((heads, hd, BK), F32)],
        compiler_params=pltpu.CompilerParams(vmem_limit_bytes=40 << 20),
        cost_estimate=COST,
    )(bounds, keys, values, keys_in, values_in, *spans, *query, *grad, *logsum, *delta)


def swap(value, axis, bit):
    return lax.ppermute(value, axis, [(i, i ^ bit) for i in range(lax.axis_size(axis))])


def shift(value, axis, distance):
    devices = range(lax.axis_size(axis))
    return lax.ppermute(value, axis, [(i, i + distance) for i in devices if i + distance in devices])


def bits_of(axis):
    size = lax.axis_size(axis)
    return [1 << b for b in range(size.bit_length() - 1)]


def bit_set(axis, bit):
    return (lax.axis_index(axis) & bit) != 0


def sum_all(value, axis):
    for bit in bits_of(axis):
        value = value + swap(value, axis, bit)
    return value


def after(anchor, *values):
    held = values if anchor is None else lax.optimization_barrier((anchor, *values))[1:]
    return held[0] if len(values) == 1 else held


def in_order(mine, other, upper, dim=0):
    return jnp.where(
        upper, jnp.stack([other, mine], axis=dim), jnp.stack([mine, other], axis=dim)
    )


def gather_tensor(value):
    pair = in_order(value, swap(value, "tensor", 2), bit_set("tensor", 2))
    quad = in_order(pair, swap(pair, "tensor", 1), bit_set("tensor", 1), dim=1)
    return lax.optimization_barrier(quad.reshape((4 * value.shape[0],) + value.shape[1:]))


def scatter_tensor(partial):
    n = partial.shape[0] // 4
    core = lax.axis_index("tensor") % 2
    across = lax.axis_index("tensor") // 2
    parts = partial.astype(BF16).reshape((2, 2, n) + partial.shape[1:])
    kept = lax.dynamic_index_in_dim(parts, core, 1, keepdims=False)
    sent = lax.dynamic_index_in_dim(parts, 1 - core, 1, keepdims=False)
    come = swap(sent, "tensor", 1)
    come = after((yield sent), come)
    half = kept.astype(F32) + come.astype(F32)
    half_low = half.astype(BF16)
    stay = lax.dynamic_index_in_dim(half, across, 0, keepdims=False)
    leave = lax.dynamic_index_in_dim(half_low, 1 - across, 0, keepdims=False)
    come = swap(leave, "tensor", 2)
    come = after((yield leave), come)
    return stay + come.astype(F32)


def scatter_data(partial):
    size = lax.axis_size("dp")
    index = lax.axis_index("dp")
    bits = bits_of("dp")
    count = len(bits)
    rest = (partial.shape[0] // size,) + partial.shape[1:]
    held = partial.astype(BF16).reshape((2,) * count + rest)
    left = list(reversed(bits))
    for bit in [1] + bits[:0:-1]:
        axis = left.index(bit)
        mine = (index // bit) % 2
        kept = lax.dynamic_index_in_dim(held, mine, axis, keepdims=False)
        sent = lax.dynamic_index_in_dim(held, 1 - mine, axis, keepdims=False).astype(BF16)
        come = swap(sent, "dp", bit)
        come = after((yield sent), come)
        held = kept.astype(F32) + come.astype(F32)
        left.remove(bit)
        if left:
            held = held.astype(BF16)
    return held


def finish(steps, anchor=None):
    try:
        while True:
            steps.send(anchor)
    except StopIteration as end:
        return end.value


def layer_norm(value):
    center = value - jnp.mean(value, axis=-1, keepdims=True)
    spread = jnp.mean(center * center, axis=-1, keepdims=True)
    return center * lax.rsqrt(spread + 1e-06)


def gelu_tanh(value):
    return jax.nn.gelu(value, approximate=True)


def onehot_sum(select, values, form):
    upper = values.astype(BF16)
    lower = (values - upper.astype(F32)).astype(BF16)
    first = jnp.einsum(form, select, upper, preferred_element_type=F32)
    return first + jnp.einsum(form, select, lower, preferred_element_type=F32)


def on_device(
    tokens,
    condition,
    latent_lengths,
    in_weight,
    in_bias,
    out_weight,
    out_bias,
    up_weight,
    up_bias,
    down_weight,
    down_bias,
    mod_weight,
    mod_bias,
    out_grad,
):
    rows, width = tokens.shape
    latents = condition.shape[0]
    local_width = in_weight.shape[2]
    heads = local_width // HD
    data_size = lax.axis_size("dp")
    data_index = lax.axis_index("dp")
    tensor_index = lax.axis_index("tensor")
    quarter = rows // 4
    row_start = tensor_index * quarter

    def mine(value):
        return lax.dynamic_slice_in_dim(value, row_start, quarter, 0)

    places = jnp.arange(latents, dtype=jnp.int32)
    earlier = places[None, :] < places[:, None]
    starts = jnp.sum(jnp.where(earlier, latent_lengths[None, :], 0), axis=1)
    ends = starts + latent_lengths
    first_row = data_index * rows
    own_places = first_row + jnp.arange(rows, dtype=jnp.int32)

    def span_of(at):
        inside = (at[:, None] >= starts[None, :]) & (at[:, None] < ends[None, :])
        begin = jnp.sum(jnp.where(inside, starts[None, :] - first_row, 0), axis=1)
        end = jnp.sum(jnp.where(inside, ends[None, :] - first_row, 0), axis=1)
        return begin, end, inside

    bases = (-rows, 0, rows)
    windows = [span_of(own_places + base) for base in bases]
    spans = [jnp.stack(window[:2]) for window in windows]
    selects = [window[2].astype(BF16) for window in windows]
    begin, end = windows[1][:2]
    span, select = spans[1], selects[1]
    select_mine = mine(select)
    forward_bounds, backward_bounds, other_bounds = [], [], []
    for base in bases:
        low = jnp.clip(begin[::BQ] - base, 0, rows) // BK
        high = (jnp.clip(end[BQ - 1 :: BQ] - base, 0, rows) + BK - 1) // BK
        forward_bounds.append(jnp.stack([low, high]))
        key_at = first_row + base + jnp.arange(rows // BK, dtype=jnp.int32) * BK
        low = jnp.clip(span_of(key_at)[0], 0, rows) // BQ
        high = (jnp.clip(span_of(key_at + BK - 1)[1], 0, rows) + BQ - 1) // BQ
        valid = (key_at >= 0) & (key_at < rows * data_size)
        backward_bounds.append(jnp.where(valid[None, :], jnp.stack([low, high]), 0))
        low = jnp.clip(begin[::BK] - base, 0, rows) // BQ
        high = (jnp.clip(end[BK - 1 :: BK] - base, 0, rows) + BQ - 1) // BQ
        other_bounds.append(jnp.stack([low, high]))
    backward_bounds = jnp.stack(backward_bounds)
    other_bounds = jnp.stack([other_bounds[0], other_bounds[2]])

    tokens_mine = mine(tokens)
    behind_tokens = gather_tensor(shift(tokens_mine, "dp", 1))
    ahead_tokens = gather_tensor(shift(tokens_mine, "dp", -1))

    cond_full = condition.astype(F32)
    silu_cond = jax.nn.silu(cond_full).astype(BF16)
    mod_local = (
        jnp.dot(silu_cond, mod_weight, preferred_element_type=F32) + mod_bias.astype(F32)
    ).astype(BF16)
    modulation = gather_tensor(mod_local[None])
    modulation = modulation.transpose(1, 0, 2).reshape(latents, 6 * width)

    def spread(chosen, first, count):
        return jnp.dot(
            chosen,
            modulation[:, first * width : (first + count) * width],
            preferred_element_type=BF16,
        )

    others = spread(select_mine, 2, 4).astype(F32)
    gate_a, shift_m, scale_m, gate_m = (others[:, i * width : (i + 1) * width] for i in range(4))
    gate_m_all = spread(select, 5, 1).astype(F32)

    bias_full = in_bias.astype(F32)
    proj_bias = jnp.stack([bias_full[0], jnp.zeros_like(bias_full[0]), bias_full[1]])

    def entry_of(rows_of, chosen):
        shift_scale = spread(chosen, 0, 2)
        scale = shift_scale[:, width:].astype(F32)
        value = rows_of.astype(F32)
        center = value - jnp.mean(value, axis=-1, keepdims=True)
        inverse = lax.rsqrt(jnp.mean(center * center, axis=-1, keepdims=True) + 1e-06)
        normed = center * inverse
        entry = (normed * (1.0 + scale) + shift_scale[:, :width].astype(F32)).astype(BF16)
        return entry, normed, inverse

    def project(entry):
        found = jnp.einsum("dcf,td->cft", in_weight, entry, preferred_element_type=F32)
        found = (found + proj_bias[:, :, None]).astype(BF16)
        return found.reshape(3, heads, HD, rows)

    entry, normed, inverse = entry_of(tokens, select)
    normed_turned, inverse = normed.T, inverse.T
    own = project(entry)
    sides = [
        project(entry_of(behind_tokens, selects[0])[0]),
        project(entry_of(ahead_tokens, selects[2])[0]),
    ]
    query = own[0]
    line = jnp.zeros((heads, 1, rows), F32)
    carried = attend(
        jnp.stack([forward_bounds[1]]),
        span,
        query,
        (jnp.zeros((heads, HD, rows), F32), line + NEG, line),
        [own[1]],
        [own[2]],
        (0,),
        False,
    )
    attended, logsum, _ = attend(
        jnp.stack([forward_bounds[0], forward_bounds[2]]),
        span,
        query,
        carried,
        [side[1] for side in sides],
        [side[2] for side in sides],
        (-rows, rows),
        True,
    )
    attended_flat = attended.reshape(local_width, rows)
    attn_part = lax.dot_general(
        attended_flat, out_weight, (((0,), (1,)), ((), ())), preferred_element_type=F32
    )
    attn_steps = scatter_tensor(attn_part)
    next(attn_steps)
    branch = finish(attn_steps) + out_bias.astype(F32)

    middle = tokens_mine.astype(F32) + gate_a * branch
    normed_m, norm_back_m = jax.vjp(layer_norm, middle)
    entry_m = gather_tensor((normed_m * (1.0 + scale_m) + shift_m).astype(BF16))
    hidden_pre = jnp.dot(entry_m, up_weight, preferred_element_type=F32) + up_bias.astype(F32)
    hidden_full, gelu_back = jax.vjp(gelu_tanh, hidden_pre)
    hidden = hidden_full.astype(BF16)
    grad_out = out_grad.astype(F32)
    grad_branch_m = (gate_m_all * grad_out).astype(BF16)
    grad_hidden = jnp.einsum("td,df->tf", grad_branch_m, down_weight, preferred_element_type=F32)
    grad_pre = gelu_back(grad_hidden)[0].astype(BF16)
    grad_down_w = jnp.einsum("td,tf->df", grad_branch_m, hidden, preferred_element_type=F32)
    entry_part = jnp.einsum("tf,df->td", grad_pre, up_weight, preferred_element_type=F32)
    entry_steps = scatter_tensor(entry_part)
    grad_pre = after(next(entry_steps), grad_pre)
    grad_out_mine = mine(out_grad).astype(F32)
    grad_up_w = jnp.einsum("td,tf->df", entry_m, grad_pre, preferred_element_type=F32)
    down_steps, up_steps = scatter_data(grad_down_w), scatter_data(grad_up_w)
    wide_sent = next(down_steps), next(up_steps)
    grad_entry_m = finish(entry_steps, wide_sent)
    grad_down_b = jnp.sum(grad_branch_m.astype(F32), axis=0)
    grad_up_b = jnp.sum(grad_pre.astype(F32), axis=0)
    grad_middle = grad_out_mine + norm_back_m(grad_entry_m * (1.0 + scale_m))[0]
    grad_gate_a = grad_middle * branch
    grad_branch_mine = (gate_a * grad_middle).astype(BF16)
    grad_out_b = jnp.sum(grad_branch_mine.astype(F32), axis=0)
    grad_branch = gather_tensor(grad_branch_mine)
    grad_attended = lax.dot_general(
        out_weight, grad_branch, (((0,), (1,)), ((), ())), preferred_element_type=F32
    ).astype(BF16)

    mlp_part = jnp.einsum(
        "tf,df->td",
        after(grad_branch_mine, hidden),
        down_weight,
        preferred_element_type=F32,
    )
    mlp_steps = scatter_tensor(mlp_part)
    next(mlp_steps)

    grad_heads = grad_attended.reshape(heads, HD, rows)
    delta = jnp.sum(grad_heads.astype(F32) * attended.astype(F32), axis=1, keepdims=True)
    stats = jnp.stack([logsum, delta])
    side_grads = [shift(grad_heads, "dp", 1), shift(grad_heads, "dp", -1)]
    side_stats = [shift(stats, "dp", 1), shift(stats, "dp", -1)]
    grad_query, part_keys, part_values = attend_back(
        backward_bounds,
        span,
        query,
        grad_heads,
        logsum,
        delta,
        [sides[0][1], own[1], sides[1][1]],
        [sides[0][2], own[2], sides[1][2]],
        bases,
    )
    mlp_steps.send(grad_heads)
    grad_out_w = lax.dot_general(
        grad_branch, attended_flat, (((0,), (1,)), ((), ())), preferred_element_type=F32
    )
    grad_keys, grad_values = others_back(
        other_bounds,
        own[1],
        own[2],
        part_keys,
        part_values,
        [spans[0], spans[2]],
        [side[0] for side in sides],
        side_grads,
        [side[0] for side in side_stats],
        [side[1] for side in side_stats],
    )
    branch_m = finish(mlp_steps, grad_keys) + down_bias.astype(F32)
    output = (middle + gate_m * branch_m).astype(BF16)
    grad_gate_m = grad_out_mine * branch_m
    down_steps.send(grad_keys)
    grad_proj = [x.reshape(local_width, rows) for x in (grad_query, grad_keys, grad_values)]
    grad_q_w, grad_k_w, grad_v_w = (
        lax.dot_general(entry, x, (((0,), (1,)), ((), ())), preferred_element_type=F32)
        for x in grad_proj
    )
    early_steps = scatter_data(jnp.concatenate([grad_out_w, grad_q_w], axis=1))
    next(early_steps)
    up_steps.send(grad_keys)
    late_steps = scatter_data(jnp.concatenate([grad_k_w, grad_v_w], axis=1))
    late_sent = next(late_steps)
    grad_proj = after(late_sent, *grad_proj)
    grad_in_b = jnp.stack([jnp.sum(grad_proj[c].astype(F32), axis=1) for c in (0, 2)])
    grad_entry = lax.dot_general(
        in_weight.reshape(width, 3 * local_width),
        jnp.concatenate(grad_proj, axis=0),
        (((1,), (0,)), ((), ())),
        preferred_element_type=F32,
    )

    scale_turned = lax.dot_general(
        modulation[:, width : 2 * width],
        select,
        (((0,), (1,)), ((), ())),
        preferred_element_type=BF16,
    ).astype(F32)
    scaled = grad_entry * (1.0 + scale_turned)
    input_part = (
        scaled
        - jnp.mean(scaled, axis=0, keepdims=True)
        - normed_turned * jnp.mean(scaled * normed_turned, axis=0, keepdims=True)
    ) * inverse

    split_terms = jnp.concatenate([grad_entry, grad_entry * normed_turned], axis=0)
    kept_terms = jnp.concatenate(
        [grad_gate_a, grad_entry_m, grad_entry_m * normed_m, grad_gate_m], axis=1
    )
    per_latent = jnp.concatenate(
        [onehot_sum(select, split_terms, "tl,mt->lm"), onehot_sum(select_mine, kept_terms, "tl,tm->lm")],
        axis=1,
    )
    columns_here = mod_weight.shape[1]
    arranged = per_latent.reshape(latents, 4, columns_here).transpose(1, 0, 2)

    out_b_row = jnp.pad(grad_out_b, (0, columns_here - width))[None]

    def for_device(flip):
        chosen = lax.dynamic_index_in_dim(arranged, tensor_index ^ flip, 0, keepdims=False)
        return jnp.concatenate([chosen, out_b_row])

    given = [for_device(flip) for flip in range(4)]
    come = [swap(given[flip], "tensor", flip) for flip in (1, 2, 3)]
    placed = lax.dynamic_update_slice_in_dim(
        jnp.zeros((width, rows), F32), grad_middle.T, row_start, 1
    )
    tokens_steps = scatter_tensor(input_part + placed)
    tokens_sent = next(tokens_steps)
    come = after(tokens_sent, *come)
    small = (given[0] + come[0]) + (come[1] + come[2])
    small = jnp.concatenate(
        [small]
        + [
            jnp.pad(value, (0, columns_here - value.shape[0]))[None]
            for value in (grad_in_b.reshape(-1), grad_up_b, grad_down_b)
        ]
    )
    early_steps.send(tokens_sent)
    late_sent = late_steps.send(input_part)
    tokens_sent = tokens_steps.send(late_sent)
    for place, bit in enumerate(bits_of("dp")):
        come = swap(small, "dp", bit)
        if place == 0:
            come = after(tokens_sent, come)
        small = small + come
        if place == 0:
            tokens_come = finish(tokens_steps, small)
    small = after(tokens_come, small)
    grad_mod = small[:latents].astype(BF16)
    sum_out_b = small[latents, :width]
    sum_in_b = small[latents + 1, : 2 * local_width]
    sum_up_b = small[latents + 2, : grad_up_b.shape[0]]
    sum_down_b = small[latents + 3, :width]
    own_width = width // data_size
    own_silu = lax.dynamic_slice_in_dim(silu_cond, data_index * own_width, own_width, 1)
    grad_mod_w = jnp.einsum("ld,lm->dm", own_silu, grad_mod, preferred_element_type=F32)
    grad_mod_b = jnp.sum(grad_mod.astype(F32), axis=0)
    own_count = latents // data_size
    own_grad_mod = lax.dynamic_slice_in_dim(grad_mod, data_index * own_count, own_count, 0)
    own_cond = lax.dynamic_slice_in_dim(cond_full, data_index * own_count, own_count, 0)
    silu_grad = jnp.einsum("lm,dm->ld", own_grad_mod, mod_weight, preferred_element_type=F32)
    cond_part = jax.vjp(jax.nn.silu, own_cond)[1](silu_grad)[0]
    cond_parts = cond_part.reshape(own_count, 4, width // 4).transpose(1, 0, 2)
    grad_cond = lax.dynamic_index_in_dim(cond_parts, tensor_index, 0, keepdims=False)
    for bit in (1, 2, 3):
        grad_cond = grad_cond + swap(
            lax.dynamic_index_in_dim(cond_parts, tensor_index ^ bit, 0, keepdims=False),
            "tensor",
            bit,
        )

    grad_tokens = tokens_come.T
    sum_down_w = finish(down_steps, tokens_come)
    sum_up_w = finish(up_steps, small)
    early = finish(early_steps, small)
    late = finish(late_steps, small)
    sum_out_w = early[:, :local_width]
    sum_in_w = jnp.stack(
        [early[:, local_width:], late[:, :local_width], late[:, local_width:]], axis=1
    )
    return (
        output,
        grad_tokens,
        grad_cond,
        sum_in_w,
        sum_in_b.reshape(2, local_width),
        sum_out_w,
        sum_out_b,
        sum_up_w,
        sum_up_b,
        sum_down_w,
        sum_down_b,
        grad_mod_w,
        grad_mod_b,
    )


def solution(mesh):
    placed = (
        P("dp", None),
        P(),
        P(),
        P(None, None, "tensor"),
        P(None, "tensor"),
        P(None, "tensor"),
        P(),
        P(None, "tensor"),
        P("tensor"),
        P(None, "tensor"),
        P(),
        P(None, "tensor"),
        P("tensor"),
        P("dp", None),
    )
    return jax.shard_map(
        on_device,
        mesh=mesh,
        in_specs=placed,
        out_specs=(
            P(("dp", "tensor"), None),
            P("dp", "tensor"),
            P("dp", "tensor"),
            P("dp", None, "tensor"),
            P(None, "tensor"),
            P("dp", "tensor"),
            P(),
            P("dp", "tensor"),
            P("tensor"),
            P("dp", "tensor"),
            P(),
            P("dp", "tensor"),
            P("tensor"),
        ),
        check_vma=False,
    )
```

```python
import functools
import math

import jax
import jax.numpy as jnp
from jax import lax
from jax.experimental import pallas as pl
from jax.experimental.pallas import tpu as pltpu
from jax.sharding import PartitionSpec as P

HD = 72
FACTOR = HD ** (-0.5)
LOG2E = math.log2(math.e)
NEG = -1e30
BQ = 256
BK = 256
COST = pl.CostEstimate(flops=18 << 30, bytes_accessed=24 << 20, transcendentals=1 << 22)
F32 = jnp.float32
BF16 = jnp.bfloat16


def contract(a, b, dims):
    return lax.dot_general(a, b, (dims, ((), ())), preferred_element_type=F32)


def forward_kernel(bases, heads, last, bounds, span, query, mixed_in, top_in, total_in, *refs):
    segments = len(bases)
    keys = refs[:segments]
    values = refs[segments : 2 * segments]
    mixed_out, top_out, total_out, mixed = refs[2 * segments :]
    rows = query.shape[2]
    scale = FACTOR * LOG2E

    def query_block(i, _):
        own = pl.ds(pl.multiple_of(i * BQ, BQ), BQ)
        begin = span[0:1, own]
        end = span[1:2, own]
        for h in range(heads):
            mixed[h] = mixed_in[h, :, own]
        state = tuple(top_in[h, :, own] for h in range(heads)) + tuple(
            total_in[h, :, own] for h in range(heads)
        )
        for s, base in enumerate(bases):

            def key_block(j, state, s=s, base=base):
                k_at = pl.multiple_of(j * BK, BK)
                block = pl.ds(k_at, BK)
                place = lax.broadcasted_iota(jnp.int32, (BK, BQ), 0) + (k_at + base)
                allowed = (place >= begin) & (place < end)
                raws = [
                    contract(keys[s][h, :, block], query[h, :, own], ((0,), (0,)))
                    for h in range(heads)
                ]
                tops, totals, shrinks, lows = [], [], [], []
                for h in range(heads):
                    raw = jnp.where(allowed, raws[h] * scale, NEG)
                    top = jnp.maximum(state[h], jnp.max(raw, axis=0, keepdims=True))
                    probs = jnp.exp2(raw - top)
                    shrink = jnp.exp2(state[h] - top)
                    tops.append(top)
                    totals.append(state[heads + h] * shrink + jnp.sum(probs, axis=0, keepdims=True))
                    shrinks.append(shrink)
                    lows.append(probs.astype(BF16))
                for h in range(heads):
                    mixed[h] = mixed[h] * shrinks[h] + contract(
                        values[s][h, :, block], lows[h], ((1,), (0,))
                    )
                return tuple(tops) + tuple(totals)

            state = lax.fori_loop(bounds[s, 0, i], bounds[s, 1, i], key_block, state)
        for h in range(heads):
            top, total = state[h], state[heads + h]
            if last:
                mixed_out[h, :, own] = (mixed[h] / total).astype(BF16)
                top_out[h, :, own] = top + jnp.log2(total)
            else:
                mixed_out[h, :, own] = mixed[h]
                top_out[h, :, own] = top
            total_out[h, :, own] = total
        return 0

    lax.fori_loop(0, rows // BQ, query_block, 0)


def attend(bounds, span, query, carried, keys, values, bases, last):
    heads, hd, rows = query.shape
    vmem = pl.BlockSpec(memory_space=pltpu.VMEM)
    line = jax.ShapeDtypeStruct((heads, 1, rows), F32)
    return pl.pallas_call(
        functools.partial(forward_kernel, bases, heads, last),
        out_shape=(
            jax.ShapeDtypeStruct((heads, hd, rows), BF16 if last else F32),
            line,
            line,
        ),
        in_specs=[pl.BlockSpec(memory_space=pltpu.SMEM)] + [vmem] * (5 + 2 * len(bases)),
        out_specs=(vmem,) * 3,
        scratch_shapes=[pltpu.VMEM((heads, hd, BQ), F32)],
        compiler_params=pltpu.CompilerParams(vmem_limit_bytes=40 << 20),
        cost_estimate=COST,
    )(bounds, span, query, *carried, *keys, *values)


def tile_back(heads, allowed, keys, values, query, grad, logsum, delta):
    scale = FACTOR * LOG2E
    raws = [contract(keys[h], query[h], ((0,), (0,))) for h in range(heads)]
    grads = [contract(values[h], grad[h], ((0,), (0,))) for h in range(heads)]
    found = []
    for h in range(heads):
        raw = jnp.where(allowed, raws[h] * scale - logsum[h], NEG)
        probs = jnp.exp2(raw)
        found.append((probs.astype(BF16), (probs * (grads[h] - delta[h])).astype(BF16)))
    return found


def backward_kernel(bases, heads, bounds, span, query, grad, logsum, delta, *refs):
    segments = len(bases)
    keys = refs[:segments]
    values = refs[segments : 2 * segments]
    grad_query, grad_keys, grad_values, sum_query, sum_keys, sum_values = refs[2 * segments :]
    sum_query[...] = jnp.zeros_like(sum_query)
    for s, base in enumerate(bases):

        def key_block(j, _, s=s, base=base):
            k_at = pl.multiple_of(j * BK, BK)
            block = pl.ds(k_at, BK)
            place = lax.broadcasted_iota(jnp.int32, (BK, BQ), 0) + (k_at + base)
            if base == 0:
                sum_keys[...] = jnp.zeros_like(sum_keys)
                sum_values[...] = jnp.zeros_like(sum_values)

            def query_block(i, _):
                own = pl.ds(pl.multiple_of(i * BQ, BQ), BQ)
                allowed = (place >= span[0:1, own]) & (place < span[1:2, own])
                q = [query[h, :, own] for h in range(heads)]
                g = [grad[h, :, own] for h in range(heads)]
                k = [keys[s][h, :, block] for h in range(heads)]
                found = tile_back(
                    heads,
                    allowed,
                    k,
                    [values[s][h, :, block] for h in range(heads)],
                    q,
                    g,
                    [logsum[h, :, own] for h in range(heads)],
                    [delta[h, :, own] for h in range(heads)],
                )
                for h in range(heads):
                    probs, grad_raw = found[h]
                    if base == 0:
                        sum_values[h] += contract(g[h], probs, ((1,), (1,)))
                        sum_keys[h] += contract(q[h], grad_raw, ((1,), (1,)))
                    sum_query[h, :, own] += contract(k[h], grad_raw, ((1,), (0,)))
                return 0

            lax.fori_loop(bounds[s, 0, j], bounds[s, 1, j], query_block, 0)
            if base == 0:
                for h in range(heads):
                    grad_keys[h, :, block] = sum_keys[h]
                    grad_values[h, :, block] = sum_values[h]
            return 0

        lax.fori_loop(0, keys[s].shape[2] // BK, key_block, 0)
    grad_query[...] = (sum_query[...] * FACTOR).astype(BF16)


def attend_back(bounds, span, query, grad, logsum, delta, keys, values, bases):
    heads, hd, rows = query.shape
    vmem = pl.BlockSpec(memory_space=pltpu.VMEM)
    full = jax.ShapeDtypeStruct((heads, hd, rows), F32)
    return pl.pallas_call(
        functools.partial(backward_kernel, bases, heads),
        out_shape=(jax.ShapeDtypeStruct((heads, hd, rows), BF16), full, full),
        in_specs=[pl.BlockSpec(memory_space=pltpu.SMEM)] + [vmem] * (5 + 2 * len(bases)),
        out_specs=(vmem,) * 3,
        scratch_shapes=[
            pltpu.VMEM((heads, hd, rows), F32),
            pltpu.VMEM((heads, hd, BK), F32),
            pltpu.VMEM((heads, hd, BK), F32),
        ],
        compiler_params=pltpu.CompilerParams(vmem_limit_bytes=44 << 20),
        cost_estimate=COST,
    )(bounds, span, query, grad, logsum, delta, *keys, *values)


def others_kernel(segments, heads, bounds, keys, values, keys_in, values_in, *refs):
    spans, query, grad, logsum, delta = (refs[n * segments : (n + 1) * segments] for n in range(5))
    grad_keys, grad_values, sum_keys, sum_values = refs[5 * segments :]

    def key_block(j, _):
        k_at = pl.multiple_of(j * BK, BK)
        block = pl.ds(k_at, BK)
        place = lax.broadcasted_iota(jnp.int32, (BK, BQ), 0) + k_at
        for h in range(heads):
            sum_keys[h] = keys_in[h, :, block]
            sum_values[h] = values_in[h, :, block]
        for s in range(segments):

            def query_block(i, _, s=s):
                own = pl.ds(pl.multiple_of(i * BQ, BQ), BQ)
                allowed = (place >= spans[s][0:1, own]) & (place < spans[s][1:2, own])
                q = [query[s][h, :, own] for h in range(heads)]
                g = [grad[s][h, :, own] for h in range(heads)]
                found = tile_back(
                    heads,
                    allowed,
                    [keys[h, :, block] for h in range(heads)],
                    [values[h, :, block] for h in range(heads)],
                    q,
                    g,
                    [logsum[s][h, :, own] for h in range(heads)],
                    [delta[s][h, :, own] for h in range(heads)],
                )
                for h in range(heads):
                    probs, grad_raw = found[h]
                    sum_values[h] += contract(g[h], probs, ((1,), (1,)))
                    sum_keys[h] += contract(q[h], grad_raw, ((1,), (1,)))
                return 0

            lax.fori_loop(bounds[s, 0, j], bounds[s, 1, j], query_block, 0)
        for h in range(heads):
            grad_keys[h, :, block] = (sum_keys[h] * FACTOR).astype(BF16)
            grad_values[h, :, block] = sum_values[h].astype(BF16)
        return 0

    lax.fori_loop(0, keys.shape[2] // BK, key_block, 0)


def others_back(bounds, keys, values, keys_in, values_in, spans, query, grad, logsum, delta):
    heads, hd, rows = keys.shape
    segments = len(query)
    vmem = pl.BlockSpec(memory_space=pltpu.VMEM)
    shape = jax.ShapeDtypeStruct((heads, hd, rows), BF16)
    return pl.pallas_call(
        functools.partial(others_kernel, segments, heads),
        out_shape=(shape, shape),
        in_specs=[pl.BlockSpec(memory_space=pltpu.SMEM)] + [vmem] * (4 + 5 * segments),
        out_specs=(vmem, vmem),
        scratch_shapes=[pltpu.VMEM((heads, hd, BK), F32), pltpu.VMEM((heads, hd, BK), F32)],
        compiler_params=pltpu.CompilerParams(vmem_limit_bytes=40 << 20),
        cost_estimate=COST,
    )(bounds, keys, values, keys_in, values_in, *spans, *query, *grad, *logsum, *delta)


def swap(value, axis, bit):
    return lax.ppermute(value, axis, [(i, i ^ bit) for i in range(lax.axis_size(axis))])


def shift(value, axis, distance):
    devices = range(lax.axis_size(axis))
    return lax.ppermute(value, axis, [(i, i + distance) for i in devices if i + distance in devices])


def bits_of(axis):
    size = lax.axis_size(axis)
    return [1 << b for b in range(size.bit_length() - 1)]


def bit_set(axis, bit):
    return (lax.axis_index(axis) & bit) != 0


def sum_all(value, axis):
    for bit in bits_of(axis):
        value = value + swap(value, axis, bit)
    return value


def after(anchor, *values):
    held = values if anchor is None else lax.optimization_barrier((anchor, *values))[1:]
    return held[0] if len(values) == 1 else held


def in_order(mine, other, upper, dim=0):
    return jnp.where(
        upper, jnp.stack([other, mine], axis=dim), jnp.stack([mine, other], axis=dim)
    )


def gather_tensor(value):
    pair = in_order(value, swap(value, "tensor", 2), bit_set("tensor", 2))
    quad = in_order(pair, swap(pair, "tensor", 1), bit_set("tensor", 1), dim=1)
    return lax.optimization_barrier(quad.reshape((4 * value.shape[0],) + value.shape[1:]))


def scatter_tensor(partial):
    n = partial.shape[0] // 4
    core = lax.axis_index("tensor") % 2
    across = lax.axis_index("tensor") // 2
    parts = partial.astype(BF16).reshape((2, 2, n) + partial.shape[1:])
    kept = lax.dynamic_index_in_dim(parts, core, 1, keepdims=False)
    sent = lax.dynamic_index_in_dim(parts, 1 - core, 1, keepdims=False)
    come = swap(sent, "tensor", 1)
    come = after((yield sent), come)
    half = kept.astype(F32) + come.astype(F32)
    half_low = half.astype(BF16)
    stay = lax.dynamic_index_in_dim(half, across, 0, keepdims=False)
    leave = lax.dynamic_index_in_dim(half_low, 1 - across, 0, keepdims=False)
    come = swap(leave, "tensor", 2)
    come = after((yield leave), come)
    return stay + come.astype(F32)


def scatter_data_steps(partial):
    size = lax.axis_size("dp")
    index = lax.axis_index("dp")
    bits = bits_of("dp")
    count = len(bits)
    rest = (partial.shape[0] // size,) + partial.shape[1:]
    held = partial.astype(BF16).reshape((2,) * count + rest)
    left = list(reversed(bits))
    for bit in [1] + bits[:0:-1]:
        axis = left.index(bit)
        mine = (index // bit) % 2
        kept = lax.dynamic_index_in_dim(held, mine, axis, keepdims=False)
        sent = lax.dynamic_index_in_dim(held, 1 - mine, axis, keepdims=False).astype(BF16)
        come = swap(sent, "dp", bit)
        come = after((yield sent), come)
        held = kept.astype(F32) + come.astype(F32)
        left.remove(bit)
        if left:
            held = held.astype(BF16)
    return held


def scatter_whole(partial):
    low = partial.astype(BF16)
    found = lax.psum_scatter(low, "dp", scatter_dimension=0, tiled=True)
    return low, lambda anchor: after(anchor, found).astype(F32)


def finish(steps, anchor=None):
    try:
        while True:
            steps.send(anchor)
    except StopIteration as end:
        return end.value


def layer_norm(value):
    center = value - jnp.mean(value, axis=-1, keepdims=True)
    spread = jnp.mean(center * center, axis=-1, keepdims=True)
    return center * lax.rsqrt(spread + 1e-06)


def gelu_tanh(value):
    return jax.nn.gelu(value, approximate=True)


def onehot_sum(select, values, form):
    upper = values.astype(BF16)
    lower = (values - upper.astype(F32)).astype(BF16)
    first = jnp.einsum(form, select, upper, preferred_element_type=F32)
    return first + jnp.einsum(form, select, lower, preferred_element_type=F32)


def on_device(
    tokens,
    condition,
    latent_lengths,
    in_weight,
    in_bias,
    out_weight,
    out_bias,
    up_weight,
    up_bias,
    down_weight,
    down_bias,
    mod_weight,
    mod_bias,
    out_grad,
):
    rows, width = tokens.shape
    latents = condition.shape[0]
    local_width = in_weight.shape[2]
    heads = local_width // HD
    data_size = lax.axis_size("dp")
    data_index = lax.axis_index("dp")
    tensor_index = lax.axis_index("tensor")
    quarter = rows // 4
    row_start = tensor_index * quarter

    def mine(value):
        return lax.dynamic_slice_in_dim(value, row_start, quarter, 0)

    places = jnp.arange(latents, dtype=jnp.int32)
    earlier = places[None, :] < places[:, None]
    starts = jnp.sum(jnp.where(earlier, latent_lengths[None, :], 0), axis=1)
    ends = starts + latent_lengths
    first_row = data_index * rows
    own_places = first_row + jnp.arange(rows, dtype=jnp.int32)

    def span_of(at):
        inside = (at[:, None] >= starts[None, :]) & (at[:, None] < ends[None, :])
        begin = jnp.sum(jnp.where(inside, starts[None, :] - first_row, 0), axis=1)
        end = jnp.sum(jnp.where(inside, ends[None, :] - first_row, 0), axis=1)
        return begin, end, inside

    bases = (-rows, 0, rows)
    windows = [span_of(own_places + base) for base in bases]
    spans = [jnp.stack(window[:2]) for window in windows]
    selects = [window[2].astype(BF16) for window in windows]
    begin, end = windows[1][:2]
    span, select = spans[1], selects[1]
    select_mine = mine(select)
    forward_bounds, backward_bounds, other_bounds = [], [], []
    for base in bases:
        low = jnp.clip(begin[::BQ] - base, 0, rows) // BK
        high = (jnp.clip(end[BQ - 1 :: BQ] - base, 0, rows) + BK - 1) // BK
        forward_bounds.append(jnp.stack([low, high]))
        key_at = first_row + base + jnp.arange(rows // BK, dtype=jnp.int32) * BK
        low = jnp.clip(span_of(key_at)[0], 0, rows) // BQ
        high = (jnp.clip(span_of(key_at + BK - 1)[1], 0, rows) + BQ - 1) // BQ
        valid = (key_at >= 0) & (key_at < rows * data_size)
        backward_bounds.append(jnp.where(valid[None, :], jnp.stack([low, high]), 0))
        low = jnp.clip(begin[::BK] - base, 0, rows) // BQ
        high = (jnp.clip(end[BK - 1 :: BK] - base, 0, rows) + BQ - 1) // BQ
        other_bounds.append(jnp.stack([low, high]))
    backward_bounds = jnp.stack(backward_bounds)
    other_bounds = jnp.stack([other_bounds[0], other_bounds[2]])

    tokens_mine = mine(tokens)
    behind_tokens = gather_tensor(shift(tokens_mine, "dp", 1))
    ahead_tokens = gather_tensor(shift(tokens_mine, "dp", -1))

    cond_full = condition.astype(F32)
    silu_cond = jax.nn.silu(cond_full).astype(BF16)
    mod_local = (
        jnp.dot(silu_cond, mod_weight, preferred_element_type=F32) + mod_bias.astype(F32)
    ).astype(BF16)
    modulation = gather_tensor(mod_local[None])
    modulation = modulation.transpose(1, 0, 2).reshape(latents, 6 * width)

    def spread(chosen, first, count):
        return jnp.dot(
            chosen,
            modulation[:, first * width : (first + count) * width],
            preferred_element_type=BF16,
        )

    others = spread(select_mine, 2, 4).astype(F32)
    gate_a, shift_m, scale_m, gate_m = (others[:, i * width : (i + 1) * width] for i in range(4))
    gate_m_all = spread(select, 5, 1).astype(F32)

    bias_full = in_bias.astype(F32)
    proj_bias = jnp.stack([bias_full[0], jnp.zeros_like(bias_full[0]), bias_full[1]])

    def entry_of(rows_of, chosen):
        shift_scale = spread(chosen, 0, 2)
        scale = shift_scale[:, width:].astype(F32)
        value = rows_of.astype(F32)
        center = value - jnp.mean(value, axis=-1, keepdims=True)
        inverse = lax.rsqrt(jnp.mean(center * center, axis=-1, keepdims=True) + 1e-06)
        normed = center * inverse
        entry = (normed * (1.0 + scale) + shift_scale[:, :width].astype(F32)).astype(BF16)
        return entry, normed, inverse

    def project(entry):
        found = jnp.einsum("dcf,td->cft", in_weight, entry, preferred_element_type=F32)
        found = (found + proj_bias[:, :, None]).astype(BF16)
        return found.reshape(3, heads, HD, rows)

    entry, normed, inverse = entry_of(tokens, select)
    normed_turned, inverse = normed.T, inverse.T
    own = project(entry)
    sides = [
        project(entry_of(behind_tokens, selects[0])[0]),
        project(entry_of(ahead_tokens, selects[2])[0]),
    ]
    query = own[0]
    line = jnp.zeros((heads, 1, rows), F32)
    carried = attend(
        jnp.stack([forward_bounds[1]]),
        span,
        query,
        (jnp.zeros((heads, HD, rows), F32), line + NEG, line),
        [own[1]],
        [own[2]],
        (0,),
        False,
    )
    attended, logsum, _ = attend(
        jnp.stack([forward_bounds[0], forward_bounds[2]]),
        span,
        query,
        carried,
        [side[1] for side in sides],
        [side[2] for side in sides],
        (-rows, rows),
        True,
    )
    attended_flat = attended.reshape(local_width, rows)
    attn_part = lax.dot_general(
        attended_flat, out_weight, (((0,), (1,)), ((), ())), preferred_element_type=F32
    )
    attn_steps = scatter_tensor(attn_part)
    next(attn_steps)
    branch = finish(attn_steps) + out_bias.astype(F32)

    middle = tokens_mine.astype(F32) + gate_a * branch
    normed_m, norm_back_m = jax.vjp(layer_norm, middle)
    entry_m = gather_tensor((normed_m * (1.0 + scale_m) + shift_m).astype(BF16))
    hidden_pre = jnp.dot(entry_m, up_weight, preferred_element_type=F32) + up_bias.astype(F32)
    hidden_full, gelu_back = jax.vjp(gelu_tanh, hidden_pre)
    hidden = hidden_full.astype(BF16)
    grad_out = out_grad.astype(F32)
    grad_branch_m = (gate_m_all * grad_out).astype(BF16)
    grad_hidden = jnp.einsum("td,df->tf", grad_branch_m, down_weight, preferred_element_type=F32)
    grad_pre = gelu_back(grad_hidden)[0].astype(BF16)
    grad_down_w = jnp.einsum("td,tf->df", grad_branch_m, hidden, preferred_element_type=F32)
    entry_part = jnp.einsum("tf,df->td", grad_pre, up_weight, preferred_element_type=F32)
    entry_steps = scatter_tensor(entry_part)
    grad_pre = after(next(entry_steps), grad_pre)
    grad_out_mine = mine(out_grad).astype(F32)
    grad_up_w = jnp.einsum("td,tf->df", entry_m, grad_pre, preferred_element_type=F32)
    down_sent, down_sum = scatter_whole(grad_down_w)
    up_sent, up_sum = scatter_whole(grad_up_w)
    grad_entry_m = finish(entry_steps, (down_sent, up_sent))
    grad_down_b = jnp.sum(grad_branch_m.astype(F32), axis=0)
    grad_up_b = jnp.sum(grad_pre.astype(F32), axis=0)
    grad_middle = grad_out_mine + norm_back_m(grad_entry_m * (1.0 + scale_m))[0]
    grad_gate_a = grad_middle * branch
    grad_branch_mine = (gate_a * grad_middle).astype(BF16)
    grad_out_b = jnp.sum(grad_branch_mine.astype(F32), axis=0)
    grad_branch = gather_tensor(grad_branch_mine)
    grad_attended = lax.dot_general(
        out_weight, grad_branch, (((0,), (1,)), ((), ())), preferred_element_type=F32
    ).astype(BF16)

    mlp_part = jnp.einsum(
        "tf,df->td",
        after(grad_branch_mine, hidden),
        down_weight,
        preferred_element_type=F32,
    )
    mlp_steps = scatter_tensor(mlp_part)
    next(mlp_steps)

    grad_heads = grad_attended.reshape(heads, HD, rows)
    delta = jnp.sum(grad_heads.astype(F32) * attended.astype(F32), axis=1, keepdims=True)
    stats = jnp.stack([logsum, delta])
    side_grads = [shift(grad_heads, "dp", 1), shift(grad_heads, "dp", -1)]
    side_stats = [shift(stats, "dp", 1), shift(stats, "dp", -1)]
    grad_query, part_keys, part_values = attend_back(
        backward_bounds,
        span,
        query,
        grad_heads,
        logsum,
        delta,
        [sides[0][1], own[1], sides[1][1]],
        [sides[0][2], own[2], sides[1][2]],
        bases,
    )
    mlp_steps.send(grad_heads)
    branch_m = finish(mlp_steps, grad_query) + down_bias.astype(F32)
    output = (middle + gate_m * branch_m).astype(BF16)
    grad_gate_m = grad_out_mine * branch_m
    grad_out_w = lax.dot_general(
        grad_branch, attended_flat, (((0,), (1,)), ((), ())), preferred_element_type=F32
    )
    grad_keys, grad_values = others_back(
        other_bounds,
        own[1],
        own[2],
        part_keys,
        part_values,
        [spans[0], spans[2]],
        [side[0] for side in sides],
        side_grads,
        [side[0] for side in side_stats],
        [side[1] for side in side_stats],
    )
    grad_proj = [x.reshape(local_width, rows) for x in (grad_query, grad_keys, grad_values)]
    grad_q_w, grad_k_w, grad_v_w = (
        lax.dot_general(entry, x, (((0,), (1,)), ((), ())), preferred_element_type=F32)
        for x in grad_proj
    )
    early_steps = scatter_data_steps(jnp.concatenate([grad_out_w, grad_q_w], axis=1))
    next(early_steps)
    late_steps = scatter_data_steps(jnp.concatenate([grad_k_w, grad_v_w], axis=1))
    late_sent = next(late_steps)
    grad_proj = after(late_sent, *grad_proj)
    grad_in_b = jnp.stack([jnp.sum(grad_proj[c].astype(F32), axis=1) for c in (0, 2)])
    grad_entry = lax.dot_general(
        in_weight.reshape(width, 3 * local_width),
        jnp.concatenate(grad_proj, axis=0),
        (((1,), (0,)), ((), ())),
        preferred_element_type=F32,
    )

    scale_turned = lax.dot_general(
        modulation[:, width : 2 * width],
        select,
        (((0,), (1,)), ((), ())),
        preferred_element_type=BF16,
    ).astype(F32)
    scaled = grad_entry * (1.0 + scale_turned)
    input_part = (
        scaled
        - jnp.mean(scaled, axis=0, keepdims=True)
        - normed_turned * jnp.mean(scaled * normed_turned, axis=0, keepdims=True)
    ) * inverse

    split_terms = jnp.concatenate([grad_entry, grad_entry * normed_turned], axis=0)
    kept_terms = jnp.concatenate(
        [grad_gate_a, grad_entry_m, grad_entry_m * normed_m, grad_gate_m], axis=1
    )
    per_latent = jnp.concatenate(
        [onehot_sum(select, split_terms, "tl,mt->lm"), onehot_sum(select_mine, kept_terms, "tl,tm->lm")],
        axis=1,
    )
    columns_here = mod_weight.shape[1]
    arranged = per_latent.reshape(latents, 4, columns_here).transpose(1, 0, 2)

    out_b_row = jnp.pad(grad_out_b, (0, columns_here - width))[None]

    def for_device(flip):
        chosen = lax.dynamic_index_in_dim(arranged, tensor_index ^ flip, 0, keepdims=False)
        return jnp.concatenate([chosen, out_b_row])

    given = [for_device(flip) for flip in range(4)]
    come = [swap(given[flip], "tensor", flip) for flip in (1, 2, 3)]
    placed = lax.dynamic_update_slice_in_dim(
        jnp.zeros((width, rows), F32), grad_middle.T, row_start, 1
    )
    tokens_steps = scatter_tensor(input_part + placed)
    tokens_sent = next(tokens_steps)
    come = after(tokens_sent, *come)
    small = (given[0] + come[0]) + (come[1] + come[2])
    small = jnp.concatenate(
        [small]
        + [
            jnp.pad(value, (0, columns_here - value.shape[0]))[None]
            for value in (grad_in_b.reshape(-1), grad_up_b, grad_down_b)
        ]
    )
    early_sent = early_steps.send(input_part)
    late_sent = late_steps.send(input_part)
    tokens_sent = tokens_steps.send((early_sent, late_sent))
    for place, bit in enumerate(bits_of("dp")):
        come = swap(small, "dp", bit)
        if place == 0:
            come = after(tokens_sent, come)
        small = small + come
    grad_mod = small[:latents].astype(BF16)
    sum_out_b = small[latents, :width]
    sum_in_b = small[latents + 1, : 2 * local_width]
    sum_up_b = small[latents + 2, : grad_up_b.shape[0]]
    sum_down_b = small[latents + 3, :width]
    own_width = width // data_size
    own_silu = lax.dynamic_slice_in_dim(silu_cond, data_index * own_width, own_width, 1)
    grad_mod_w = jnp.einsum("ld,lm->dm", own_silu, grad_mod, preferred_element_type=F32)
    grad_mod_b = jnp.sum(grad_mod.astype(F32), axis=0)
    own_count = latents // data_size
    own_grad_mod = lax.dynamic_slice_in_dim(grad_mod, data_index * own_count, own_count, 0)
    own_cond = lax.dynamic_slice_in_dim(cond_full, data_index * own_count, own_count, 0)
    silu_grad = jnp.einsum("lm,dm->ld", own_grad_mod, mod_weight, preferred_element_type=F32)
    cond_part = jax.vjp(jax.nn.silu, own_cond)[1](silu_grad)[0]
    cond_parts = cond_part.reshape(own_count, 4, width // 4).transpose(1, 0, 2)
    grad_cond = lax.dynamic_index_in_dim(cond_parts, tensor_index, 0, keepdims=False)
    for bit in (1, 2, 3):
        grad_cond = grad_cond + swap(
            lax.dynamic_index_in_dim(cond_parts, tensor_index ^ bit, 0, keepdims=False),
            "tensor",
            bit,
        )

    grad_tokens = finish(tokens_steps, grad_mod_w).T
    sum_down_w, sum_up_w = down_sum(grad_mod_w), up_sum(grad_mod_w)
    early = finish(early_steps, small)
    late = finish(late_steps, small)
    sum_out_w = early[:, :local_width]
    sum_in_w = jnp.stack(
        [early[:, local_width:], late[:, :local_width], late[:, local_width:]], axis=1
    )
    return (
        output,
        grad_tokens,
        grad_cond,
        sum_in_w,
        sum_in_b.reshape(2, local_width),
        sum_out_w,
        sum_out_b,
        sum_up_w,
        sum_up_b,
        sum_down_w,
        sum_down_b,
        grad_mod_w,
        grad_mod_b,
    )


def solution(mesh):
    placed = (
        P("dp", None),
        P(),
        P(),
        P(None, None, "tensor"),
        P(None, "tensor"),
        P(None, "tensor"),
        P(),
        P(None, "tensor"),
        P("tensor"),
        P(None, "tensor"),
        P(),
        P(None, "tensor"),
        P("tensor"),
        P("dp", None),
    )
    return jax.shard_map(
        on_device,
        mesh=mesh,
        in_specs=placed,
        out_specs=(
            P(("dp", "tensor"), None),
            P("dp", "tensor"),
            P("dp", "tensor"),
            P("dp", None, "tensor"),
            P(None, "tensor"),
            P("dp", "tensor"),
            P(),
            P("dp", "tensor"),
            P("tensor"),
            P("dp", "tensor"),
            P(),
            P("dp", "tensor"),
            P("tensor"),
        ),
        check_vma=False,
    )
```
